256 devices in a mesh: dp: 8 (over y, core), expert: 32 (over x, z).
Axes of the slice: x: 4, y: 4, z: 8, core: 2. Of those that a mesh axis runs over, the one named last changes fastest.
Arguments:
- tokens: bfloat16 [16384, 2048], P(('dp', 'expert')), may hold values from -6 to 6
- cotangent: bfloat16 [16384, 2048], P(('dp', 'expert')), may hold values from -1.5 to 1.5
- routes: int32 [16384, 8], P(('dp', 'expert')), may hold values from 0 to 31, as said below
- slot_index: int32 [16384, 8], P(('dp', 'expert')), may hold values from 0 to 17, as said below
- gate_probs: float32 [16384, 8], P(('dp', 'expert')), may hold values from 0.05 to 0.25
- lengths: int32 [256, 4], P(('dp', 'expert')), may hold values from 1 to 32, 64 in all within a row
- w_gate_up: bfloat16 [32, 2048, 1536], P('expert'), may hold values from -0.125 to 0.125
- w_down: bfloat16 [32, 768, 2048], P('expert'), may hold values from -0.21875 to 0.21875
Outputs:
- token_grad: bfloat16 [16384, 2048], P(('dp', 'expert'))
- grad_gate_up: bfloat16 [32, 2048, 1536], P('expert', 'dp')
- grad_down: bfloat16 [32, 768, 2048], P('expert', None, 'dp')
The draws below stay inside these ranges and needn't reach their ends.
Inputs may be any that keep to these rules, and one draw needn't show every extreme that they name: `routes`: each row names 8 different experts. Among one device's pairs no expert is named more than 18 times, and for every index of dp one expert is named exactly 18 times on each device of that index. `slot_index`: on each device the pairs that name one expert hold the slots 0 to their count minus 1, each once. `lengths`: each row sums to 64.
All inputs are finite; a program needn't handle non-finite values.
Results may differ from the reference program's by a relative error of at most 0.017.
Values may be sent and summed in bfloat16 or wider, within the bound.
No kernel may reach another device: no remote copies, remote signals or barrier semaphores. Data moves between devices by JAX's collectives and lax.ppermute only.
A program may use at most 128 MiB of HBM per device.

```python
import math
import jax
import jax.numpy as jnp
import numpy as np
from jax import lax

D = 2048
FF = 768
TOP = 8
SEGS = 4
TOK_DEV = 64
EXPERTS = 32
TOKENS = 16384
CAP = 18
N_DP = 8
N_EXPERT = 32


def distinct_order(key, layout, extent):
    scores = jax.random.randint(key, layout, 0, 1 << 20) * extent + jnp.arange(extent, dtype=jnp.int32)
    return jnp.argsort(scores, axis=-1)


def routing_plan(key):
    blocks = TOKENS // TOK_DEV
    entries = TOK_DEV * TOP
    remaining = entries - CAP
    groups = blocks // EXPERTS
    key_busiest, key_weights, key_fill, key_rows, key_cols = jax.random.split(key, 5)
    busiest = jnp.repeat(jax.random.randint(key_busiest, (groups,), 0, EXPERTS), EXPERTS)
    expert_ids = jnp.arange(EXPERTS, dtype=jnp.int32)
    is_busiest = expert_ids[None, :] == busiest[:, None]
    weights = jnp.where(is_busiest, 0, jax.random.randint(key_weights, (blocks, EXPERTS), 1, 5))
    weight_sum = jnp.sum(weights, axis=1, keepdims=True)
    counts = jnp.minimum(weights * remaining // weight_sum, CAP)
    counts = jnp.where(is_busiest, CAP, counts)
    deficit = entries - jnp.sum(counts, axis=1, keepdims=True)
    headroom = CAP - counts
    fill_order = distinct_order(key_fill, (blocks, EXPERTS), EXPERTS)
    sorted_room = jnp.take_along_axis(headroom, fill_order, axis=1)
    before = jnp.cumsum(sorted_room, axis=1) - sorted_room
    extra_rows = jnp.clip(deficit - before, 0, sorted_room)
    row_index = jnp.arange(blocks)[:, None]
    counts = counts + jnp.zeros_like(counts).at[row_index, fill_order].set(extra_rows)
    run_ends = jnp.cumsum(counts, axis=1)
    run_starts = run_ends - counts
    entry_ids = jnp.arange(entries, dtype=jnp.int32)
    owners = jnp.sum((run_ends[:, None, :] <= entry_ids[None, :, None]).astype(jnp.int32), axis=2)
    run_rank = entry_ids[None, :] - jnp.take_along_axis(run_starts, owners, axis=1)
    owners = owners.reshape(blocks, TOP, TOK_DEV).transpose(0, 2, 1)
    run_rank = run_rank.reshape(blocks, TOP, TOK_DEV).transpose(0, 2, 1)
    row_order = distinct_order(key_rows, (blocks, TOK_DEV), TOK_DEV)
    owners = jnp.take_along_axis(owners, row_order[:, :, None], axis=1)
    run_rank = jnp.take_along_axis(run_rank, row_order[:, :, None], axis=1)
    col_order = distinct_order(key_cols, (blocks, TOK_DEV, TOP), TOP)
    owners = jnp.take_along_axis(owners, col_order, axis=2)
    run_rank = jnp.take_along_axis(run_rank, col_order, axis=2)
    return (owners.reshape(TOKENS, TOP).astype(jnp.int32), run_rank.reshape(TOKENS, TOP).astype(jnp.int32))


def draw_routes(key, part):
    owners, run_rank = routing_plan(key)
    return owners


def draw_slot_index(key, part):
    owners, run_rank = routing_plan(key)
    return run_rank


def levels(own_key, dims, shards, low, largest):
    factor_of, own = 1.0, jax.random.fold_in(own_key, 6)
    for dim, parts in shards:
        draws = jnp.exp(jax.random.uniform(jax.random.fold_in(own, dim), (parts,), jnp.float32, low / len(shards), largest / len(shards)))
        factor_of = factor_of * jnp.repeat(draws, dims[dim] // parts).reshape([-1 if axis == dim else 1 for axis in range(len(dims))])
    return factor_of


def split_up(number_of, total, most, slope):
    loads = [(1 << 20) // math.isqrt(standing ** slope) + 1 for standing in range(2, number_of + 1)]
    spare, given = total - most - (number_of - 1), [1] * (number_of - 1)
    while spare > 0:
        free = [i for i in range(number_of - 1) if given[i] < most]
        pool, left = sum([loads[i] for i in free]), spare
        for i in free:
            addition = min(most - given[i], max(1, left * loads[i] // pool), spare)
            given[i] = given[i] + addition
            spare = spare - addition
    return np.array([most] + given)


def uneven_parts(key, amount, total, most, lean):
    if amount == 2:
        one = jax.random.randint(key, (), max(1, total - most), min(most, total - 1) + 1)
        return jnp.stack([one, total - one])
    tallies = jnp.asarray(split_up(amount, total, most, lean), jnp.int32)
    pairs = (amount - 1) // 2
    source_of, sink = tallies[1:1 + 2 * pairs:2], tallies[2:2 + 2 * pairs:2]
    margin = jnp.minimum(source_of - 1, most - sink)
    shifted = jax.random.randint(jax.random.fold_in(key, 1), (pairs,), 0, 1 << 20) % (margin + 1)
    tallies = tallies.at[1:1 + 2 * pairs:2].set(source_of - shifted).at[2:2 + 2 * pairs:2].set(sink + shifted)
    return tallies[jax.random.permutation(jax.random.fold_in(key, 2), amount)]


def scatter_about(rng, dims, width, reach, pieces=(), kind=jnp.bfloat16):
    level = levels(rng, dims, pieces, -0.22, 0.18) if pieces else 1.0
    values = jax.random.normal(rng, dims, jnp.float32) * width * level
    return jnp.minimum(jnp.maximum(values, -reach), reach).astype(kind)


def setup_inputs(seed: int = 0) -> dict:
    seeds = jax.random.split(jax.random.key(seed), 9)
    return {
        "tokens": scatter_about(seeds[0], (TOKENS, D), 1.0, 6.0, ((0, 256),)),
        "cotangent": scatter_about(seeds[1], (TOKENS, D), 0.25, 1.5, ((0, 256),)),
        "routes": draw_routes(jax.random.fold_in(seeds[8], 71), 0),
        "slot_index": draw_slot_index(jax.random.fold_in(seeds[8], 71), 0),
        "gate_probs": jnp.clip(0.05 + 0.2 * jax.random.uniform(seeds[4], (TOKENS, TOP), jnp.float32) ** levels(seeds[4], (TOKENS, TOP), ((0, 256),), -0.2, 0.2), 0.05, 0.25),
        "lengths": jax.vmap(lambda own: uneven_parts(own, SEGS, TOK_DEV, TOK_DEV // 2, 2))(jax.random.split(seeds[5], (N_DP * N_EXPERT))).reshape((N_DP * N_EXPERT, SEGS)).astype(jnp.int32),
        "w_gate_up": scatter_about(seeds[6], (EXPERTS, D, 2 * FF), D ** -0.5, 0.125, ((0, 32),)),
        "w_down": scatter_about(seeds[7], (EXPERTS, FF, D), FF ** -0.5, 0.21875, ((0, 32),)),
    }


def row_weights(lengths):
    segment_ends = jnp.cumsum(lengths, axis=1)
    position = jnp.arange(TOK_DEV, dtype=jnp.int32)
    segment_of = jnp.sum((segment_ends[:, None, :] <= position[None, :, None]).astype(jnp.int32), axis=2)
    choose = segment_of[:, :, None] == jnp.arange(SEGS, dtype=jnp.int32)[None, None, :]
    picked = jnp.sum(jnp.where(choose, lengths[:, None, :], 0), axis=2)
    return (TOK_DEV / SEGS) / picked.astype(jnp.float32)


def silu_grads(gate_pre, up_pre, back_grad, scales):
    sigmoid_gate = jax.nn.sigmoid(gate_pre)
    activation = gate_pre * sigmoid_gate * up_pre
    scaled_back = back_grad * scales[:, None]
    gate_grad = scaled_back * up_pre * sigmoid_gate * (1.0 + gate_pre * (1.0 - sigmoid_gate))
    up_grad = scaled_back * gate_pre * sigmoid_gate
    preact_grad = jnp.concatenate([gate_grad, up_grad], axis=1).astype(jnp.bfloat16)
    scaled_act = (activation * scales[:, None]).astype(jnp.bfloat16)
    return preact_grad, scaled_act


def expert_rows(rows_in, rows_grad, scales, gate_up, down_proj):
    hidden = down_proj.shape[0]
    preact = jnp.dot(rows_in, gate_up, preferred_element_type=jnp.float32)
    back_grad = lax.dot_general(rows_grad, down_proj, (((1,), (1,)), ((), ())), preferred_element_type=jnp.float32)
    preact_grad, scaled_act = silu_grads(preact[:, :hidden], preact[:, hidden:], back_grad, scales.astype(jnp.float32))
    row_grads = lax.dot_general(preact_grad, gate_up, (((1,), (1,)), ((), ())), preferred_element_type=jnp.float32).astype(jnp.bfloat16)
    return row_grads, preact_grad, scaled_act


def reference(tokens, cotangent, routes, slot_index, gate_probs, lengths, w_gate_up, w_down):
    blocks = TOKENS // TOK_DEV
    entries = TOKENS * TOP
    scales = (row_weights(lengths).reshape(TOKENS, 1) * gate_probs).astype(jnp.bfloat16).reshape(entries)
    token_ids = jnp.arange(TOKENS, dtype=jnp.int32)
    source = token_ids // TOK_DEV
    target = (routes * (blocks * CAP) + source[:, None] * CAP + slot_index).reshape(entries).astype(jnp.int32)
    inverse = jnp.full((EXPERTS * blocks * CAP,), entries, jnp.int32)
    inverse = inverse.at[target].set(jnp.arange(entries, dtype=jnp.int32)).reshape(EXPERTS, blocks * CAP)
    shard_rows = (blocks * CAP) // N_DP

    def per_expert(accumulated, operands):
        inverse_row, gate_up, down_proj = operands
        filled = inverse_row < entries
        safe_entry = jnp.where(filled, inverse_row, 0).astype(jnp.int32)
        token_of = safe_entry // TOP
        rows_in = jnp.where(filled[:, None], tokens[token_of], jnp.zeros((), tokens.dtype))
        rows_grad = jnp.where(filled[:, None], cotangent[token_of], jnp.zeros((), cotangent.dtype))
        scale_rows = jnp.where(filled, scales[safe_entry], jnp.zeros((), scales.dtype))
        row_grads, preact_grad, scaled_act = expert_rows(rows_in, rows_grad, scale_rows, gate_up, down_proj)
        added = jnp.where(filled[:, None], row_grads.astype(jnp.float32), jnp.zeros((), jnp.float32))
        accumulated = accumulated.at[token_of].add(added)
        gate_up_parts = jnp.einsum(
            "srd,srf->sdf",
            rows_in.reshape(N_DP, shard_rows, D).astype(jnp.float32),
            preact_grad.reshape(N_DP, shard_rows, 2 * FF).astype(jnp.float32),
        )
        down_parts = jnp.einsum(
            "srf,srd->sfd",
            scaled_act.reshape(N_DP, shard_rows, FF).astype(jnp.float32),
            rows_grad.reshape(N_DP, shard_rows, D).astype(jnp.float32),
        )
        gate_up_sum = jnp.sum(lax.optimization_barrier(gate_up_parts.astype(jnp.bfloat16)).astype(jnp.float32), axis=0)
        down_sum = jnp.sum(lax.optimization_barrier(down_parts.astype(jnp.bfloat16)).astype(jnp.float32), axis=0)
        return accumulated, (gate_up_sum.astype(jnp.bfloat16), down_sum.astype(jnp.bfloat16))

    accumulated, stacked = lax.scan(per_expert, jnp.zeros((TOKENS, D), jnp.float32), (inverse, w_gate_up, w_down))
    return accumulated.astype(jnp.bfloat16), stacked[0], stacked[1]
```

```python
import functools

import jax
import jax.numpy as jnp
from jax import lax
from jax.experimental import pallas as pl
from jax.experimental.pallas import tpu as pltpu
from jax.sharding import Mesh
from jax.sharding import PartitionSpec as P

TOP = 8
SEGS = 4
TOK = 64
CAP = 18
D = 2048
FF = 768
GU = 2 * FF
META = 128
NX = 4
NZ = 8
NY = 4
BLK_D = 256
BF = jnp.bfloat16
F32 = jnp.float32
VMEM = pl.BlockSpec(memory_space=pltpu.VMEM)
SMEM = pl.BlockSpec(memory_space=pltpu.SMEM)


def params():
    return pltpu.CompilerParams(vmem_limit_bytes=48 * 1024 * 1024)


def pad8(n):
    return (n + 7) // 8 * 8


def send_rows(blocks):
    return pad8(2 * CAP * blocks)


def slot_rows(blocks):
    return pad8(CAP * blocks)


def cost(flops, nbytes):
    return pl.CostEstimate(flops=int(flops), bytes_accessed=int(nbytes), transcendentals=0)


def pack_kernel(len_ref, tok_ref, cot_ref, routes_ref, slots_ref, gate_ref, out_ref):
    position = lax.broadcasted_iota(jnp.int32, (TOK, 1), 0)
    end = jnp.int32(0)
    picked = jnp.zeros((TOK, 1), F32)
    for seg in range(SEGS):
        length = len_ref[0, seg]
        inside = (position >= end) & (position < end + length)
        picked = jnp.where(inside, length.astype(F32), picked)
        end = end + length
    weight = (TOK / SEGS) / picked
    scale = (weight * gate_ref[...]).astype(BF).astype(F32)
    routes = routes_ref[...].astype(F32)
    slots = slots_ref[...].astype(F32)
    ones = jnp.ones((TOK, TOP), F32)
    fill = jnp.zeros((TOK, META - 3 * TOP), F32)
    out_ref[0:TOK, 0:D] = tok_ref[...]
    out_ref[TOK : 2 * TOK, 0:D] = cot_ref[...]
    out_ref[0:TOK, D : D + META] = jnp.concatenate([routes, slots, ones, fill], axis=1).astype(BF)
    out_ref[TOK : 2 * TOK, D : D + META] = jnp.concatenate([routes, slots, scale, fill], axis=1).astype(BF)


def pack(tokens, cotangent, routes, slots, gates, lengths):
    return pl.pallas_call(
        pack_kernel,
        out_shape=jax.ShapeDtypeStruct((2 * TOK, D + META), BF),
        in_specs=[SMEM] + [VMEM] * 5,
        out_specs=VMEM,
        compiler_params=params(),
        cost_estimate=cost(1e6, 2 << 20),
        name="pack",
    )(lengths, tokens, cotangent, routes, slots, gates)


def select_kernel(blocks, split, pos_ref, *refs):
    if split:
        tok_ref, cot_ref = refs[0], refs[1]
        data = jnp.concatenate([tok_ref[:, 0:D], cot_ref[:, 0:D]], axis=0)
        metas = [jnp.concatenate([tok_ref[:, D:], cot_ref[:, D:]], axis=0)]
        outs = refs[2:]
    else:
        data = jnp.concatenate([r[:, 0:D] for r in refs[:blocks]], axis=0)
        metas = [r[:, D:] for r in refs[:blocks]]
        outs = refs[blocks:]
    meta = jnp.concatenate([m.astype(F32).T for m in metas], axis=1)
    width = 2 * TOK * blocks
    lane = lax.broadcasted_iota(jnp.int32, (1, width), 1)
    second = (lane >= 2 * TOK).astype(jnp.int32)
    within = lane - second * (2 * TOK)
    is_cot = (within >= TOK).astype(jnp.int32)
    code = meta[0:TOP] * CAP + meta[TOP : 2 * TOP] + (1024 * is_cot + 2048 * second).astype(F32)
    value = meta[2 * TOP : 3 * TOP]
    rows = send_rows(blocks)
    row = lax.broadcasted_iota(jnp.int32, (rows, 1), 0)
    row_cot = (row >= CAP * blocks).astype(jnp.int32)
    rest = row - row_cot * (CAP * blocks)
    row_second = (rest >= CAP).astype(jnp.int32)
    slot = rest - row_second * CAP
    used = row < 2 * CAP * blocks
    for step in range(NX):
        expert = ((pos_ref[0] + step) & (NX - 1)) * NZ + pos_ref[1]
        row_code = expert * CAP + slot + 1024 * row_cot + 2048 * row_second
        row_code = jnp.where(used, row_code, -1).astype(F32)
        chosen = jnp.zeros((rows, width), F32)
        for k in range(TOP):
            chosen = chosen + jnp.where(code[k : k + 1] == row_code, value[k : k + 1], 0.0)
        outs[step][...] = jnp.dot(chosen.astype(BF), data, preferred_element_type=F32).astype(BF)


def select(position, inputs, blocks, split=False):
    rows = send_rows(blocks)
    return pl.pallas_call(
        functools.partial(select_kernel, blocks, split),
        out_shape=[jax.ShapeDtypeStruct((rows, D), BF)] * NX,
        in_specs=[SMEM] + [VMEM] * len(inputs),
        out_specs=[VMEM] * NX,
        compiler_params=params(),
        cost_estimate=cost(2 * NX * rows * 128 * blocks * D, 2 << 20),
        name="select",
    )(position, *inputs)


def expert_kernel(blocks, a0, a1, a2, a3, gate_up, down, tok_ref, cot_ref, grad_ref, act_ref, *back_refs):
    rows, slots = send_rows(blocks), slot_rows(blocks)
    out_row = lax.broadcasted_iota(jnp.int32, (2 * slots, rows), 0)
    in_row = lax.broadcasted_iota(jnp.int32, (2 * slots, rows), 1)
    half = (out_row >= slots).astype(jnp.int32)
    inner = out_row - half * slots
    regroup = ((inner < CAP * blocks) & (in_row == inner + half * (CAP * blocks))).astype(F32).astype(BF)
    parts = [jnp.dot(regroup, a[...], preferred_element_type=F32) for a in (a0, a1, a2, a3)]
    tok = jnp.concatenate([p[0:slots] for p in parts], axis=0).astype(BF)
    cot = jnp.concatenate([p[slots:] for p in parts], axis=0).astype(BF)
    tok_ref[...] = tok
    cot_ref[...] = cot
    preact = jnp.dot(tok, gate_up[...], preferred_element_type=F32)
    back = lax.dot_general(cot, down[...], (((1,), (1,)), ((), ())), preferred_element_type=F32)
    gate_pre, up_pre = preact[:, 0:FF], preact[:, FF:]
    sigmoid = jax.nn.sigmoid(gate_pre)
    silu = gate_pre * sigmoid
    act_ref[...] = (silu * up_pre).astype(BF)
    gate_grad = back * up_pre * sigmoid * (1.0 + gate_pre * (1.0 - sigmoid))
    grad_ref[:, 0:FF] = gate_grad.astype(BF)
    grad_ref[:, FF:] = (back * silu).astype(BF)
    row_grad = lax.dot_general(grad_ref[...], gate_up[...], (((1,), (1,)), ((), ())), preferred_element_type=F32)
    for step in range(NX):
        back_refs[step][...] = row_grad[step * slots : (step + 1) * slots].astype(BF)


def expert(arrays, gate_up, down, blocks):
    slots = slot_rows(blocks)
    total = NX * slots
    shapes = [(total, D), (total, D), (total, GU), (total, FF)] + [(slots, D)] * NX
    outs = pl.pallas_call(
        functools.partial(expert_kernel, blocks),
        out_shape=[jax.ShapeDtypeStruct(s, BF) for s in shapes],
        in_specs=[VMEM] * 6,
        out_specs=[VMEM] * len(shapes),
        compiler_params=params(),
        cost_estimate=cost(2 * 256 * D * GU * 2.5, 14 << 20),
        name="expert",
    )(*arrays, gate_up, down)
    return outs[:4], outs[4:]


def combine_kernel(blocks, pos_ref, *refs):
    metas, rows_refs, outs = refs[:blocks], refs[blocks : blocks + NX], refs[blocks + NX :]
    slots = slot_rows(blocks)
    data = jnp.concatenate([r[...].astype(F32) for r in rows_refs], axis=0).astype(BF)
    col = lax.broadcasted_iota(jnp.int32, (1, NX * slots), 1)
    step = jnp.zeros((1, NX * slots), jnp.int32)
    for i in range(1, NX):
        step = step + (col >= i * slots).astype(jnp.int32)
    inner = col - step * slots
    second = (inner >= CAP).astype(jnp.int32)
    slot = inner - second * CAP
    expert_id = ((pos_ref[0] + step) & (NX - 1)) * NZ + pos_ref[1]
    used = inner < CAP * blocks
    for b in range(blocks):
        meta = metas[b][0:TOK, :].astype(F32)
        col_code = jnp.where(used & (second == b), expert_id * CAP + slot, -1).astype(F32)
        chosen = jnp.zeros((TOK, NX * slots), F32)
        for k in range(TOP):
            code = meta[:, k : k + 1] * CAP + meta[:, TOP + k : TOP + k + 1]
            chosen = chosen + jnp.where(code == col_code, 1.0, 0.0)
        outs[b][...] = jnp.dot(chosen.astype(BF), data, preferred_element_type=F32).astype(BF)


def combine(position, metas, rows, blocks):
    return pl.pallas_call(
        functools.partial(combine_kernel, blocks),
        out_shape=[jax.ShapeDtypeStruct((TOK, D), BF)] * blocks,
        in_specs=[SMEM] + [VMEM] * (blocks + NX),
        out_specs=[VMEM] * blocks,
        compiler_params=params(),
        cost_estimate=cost(2 * TOK * blocks * 256 * D, 2 << 20),
        name="combine",
    )(position, *metas, *rows)


def add_kernel(*refs):
    total = refs[0][...].astype(F32)
    for r in refs[1:-1]:
        total = total + r[...].astype(F32)
    refs[-1][...] = total.astype(BF)


def add_all(parts):
    return pl.pallas_call(
        add_kernel,
        out_shape=jax.ShapeDtypeStruct(parts[0].shape, BF),
        in_specs=[VMEM] * len(parts),
        out_specs=VMEM,
        compiler_params=params(),
        cost_estimate=cost(1e6, 2 << 20),
        name="add_all",
    )(*parts)


def weight_kernel(chunks, which_ref, *refs):
    toks, cots = refs[0:chunks], refs[chunks : 2 * chunks]
    grads, acts = refs[2 * chunks : 3 * chunks], refs[3 * chunks : 4 * chunks]
    rest = refs[4 * chunks :]
    out = rest[-1]
    first = (((0,), (0,)), ((), ()))

    def total(lefts, rights):
        acc = lax.dot_general(lefts[0][...], rights[0][...], first, preferred_element_type=F32)
        for left, right in zip(lefts[1:], rights[1:], strict=True):
            acc = acc + lax.dot_general(left[...], right[...], first, preferred_element_type=F32)
        return acc

    gate_up = total(toks, grads)
    down = total(cots, acts)
    for r in rest[:-1]:
        gate_up = gate_up + r[:, 0:GU].astype(F32)
        down = down + r[:, GU:].astype(F32)
    out[:, 0:GU] = gate_up.astype(BF)
    out[:, GU:] = down.astype(BF)


def weight_block(which, groups, extra=()):
    toks, cots, grads, acts = zip(*groups, strict=True)
    chunks = len(groups)

    def cut(a):
        return pl.BlockSpec((a.shape[0], BLK_D), lambda i, w: (0, w[0]))

    def whole(a):
        return pl.BlockSpec(a.shape, lambda i, w: (0, 0))

    specs = [cut(a) for a in toks + cots] + [whole(a) for a in grads + acts] + [whole(a) for a in extra]
    return pl.pallas_call(
        functools.partial(weight_kernel, chunks),
        out_shape=jax.ShapeDtypeStruct((BLK_D, GU + FF), BF),
        grid_spec=pltpu.PrefetchScalarGridSpec(
            num_scalar_prefetch=1,
            grid=(1,),
            in_specs=specs,
            out_specs=pl.BlockSpec((BLK_D, GU + FF), lambda i, w: (0, 0)),
        ),
        compiler_params=params(),
        cost_estimate=cost(2 * 640 * BLK_D * (GU + FF), 5 << 20),
        name="weight_block",
    )(which, *toks, *cots, *grads, *acts, *extra)


def finish_kernel(own, plus, minus, gate_up, down):
    gate_up[...] = (
        own[:, 0:GU].astype(F32) + plus[:, 0:GU].astype(F32) + minus[:, 0:GU].astype(F32)
    ).astype(BF)
    total = own[:, GU:].astype(F32) + plus[:, GU:].astype(F32) + minus[:, GU:].astype(F32)
    down[...] = total.T.astype(BF)


def finish(own, plus, minus):
    return pl.pallas_call(
        finish_kernel,
        out_shape=[jax.ShapeDtypeStruct((BLK_D, GU), BF), jax.ShapeDtypeStruct((FF, BLK_D), BF)],
        in_specs=[VMEM] * 3,
        out_specs=[VMEM] * 2,
        compiler_params=params(),
        cost_estimate=cost(1e6, 4 << 20),
        name="finish",
    )(own, plus, minus)


def shift(array, axis, size, by):
    return lax.ppermute(array, axis, [(i, (i + by) % size) for i in range(size)])


def per_device(tokens, cotangent, routes, slot_index, gate_probs, lengths, w_gate_up, w_down):
    x, z = lax.axis_index("x"), lax.axis_index("z")
    y, core = lax.axis_index("y"), lax.axis_index("core")
    position = jnp.stack([x, z]).astype(jnp.int32)
    gate_up, down = w_gate_up[0], w_down[0]

    own = pack(tokens, cotangent, routes, slot_index, gate_probs, lengths)
    up, dn = {0: own}, {0: own}
    for d in range(1, NZ // 2):
        up[d] = shift(up[d - 1], "z", NZ, 1)
        dn[d] = shift(dn[d - 1], "z", NZ, -1)
    half = NZ // 2
    far_tok = shift(up[half - 1][0:TOK], "z", NZ, 1)
    far_cot = shift(dn[half - 1][TOK:], "z", NZ, -1)

    chunks = [((own,), 1, False)]
    chunks += [((up[d], dn[d]), 2, False) for d in range(1, half)]
    chunks += [((far_tok, far_cot), 1, True)]

    groups, sums = [], []
    for index, (inputs, blocks, split) in enumerate(chunks):
        sent = select(position, inputs, blocks, split)
        arrays = [sent[0]] + [shift(sent[s], "x", NX, s) for s in range(1, NX)]
        group, back = expert(arrays, gate_up, down, blocks)
        groups.append(group)
        back = [back[0]] + [shift(back[s], "x", NX, -s) for s in range(1, NX)]
        metas = [b[0:TOK, D:] for b in (inputs[:1] if split else inputs)]
        parts = combine(position, metas, back, blocks)
        if index == 0:
            sums.append(parts[0])
        elif split:
            sums.append(shift(parts[0], "z", NZ, half))
        else:
            sums.append(shift(parts[0], "z", NZ, -index))
            sums.append(shift(parts[1], "z", NZ, index))
    token_grad = add_all(sums)

    def block_of(step, of_core):
        return (2 * ((y + step) % NY) + of_core).astype(jnp.int32).reshape(1)

    received = {}
    for step in (2, 1, 3, 0):
        other = weight_block(block_of(step, 1 - core), groups)
        received[step] = shift(other, "core", 2, 1)
    opposite = weight_block(block_of(2, core), groups, (received[2],))
    hop = BLK_D // 2
    zeros = jnp.zeros((hop, GU + FF), BF)
    top = shift(opposite[:hop], "y", NY, 1)
    bottom = shift(opposite[hop:], "y", NY, -1)
    plus = weight_block(block_of(1, core), groups, (received[1], jnp.concatenate([top, zeros])))
    minus = weight_block(block_of(3, core), groups, (received[3], jnp.concatenate([zeros, bottom])))
    plus = shift(plus, "y", NY, 1)
    minus = shift(minus, "y", NY, -1)
    mine = weight_block(block_of(0, core), groups, (received[0],))
    grad_gate_up, grad_down = finish(mine, plus, minus)
    return token_grad, grad_gate_up[None], grad_down[None]


def solution(mesh):
    torus = Mesh(mesh.devices.reshape(NY, 2, NX, NZ), ("y", "core", "x", "z"))
    dp, ep = ("y", "core"), ("x", "z")
    return jax.shard_map(
        per_device,
        mesh=torus,
        in_specs=(P(dp + ep, None),) * 6 + (P(ep, None, None),) * 2,
        out_specs=(P(dp + ep, None), P(ep, dp, None), P(ep, None, dp)),
        check_vma=False,
    )
```

```python
import functools

import jax
import jax.numpy as jnp
from jax import lax
from jax.experimental import pallas as pl
from jax.experimental.pallas import tpu as pltpu
from jax.sharding import Mesh
from jax.sharding import PartitionSpec as P

TOP = 8
SEGS = 4
TOK = 64
CAP = 18
D = 2048
FF = 768
GU = 2 * FF
META = 128
NX = 4
NZ = 8
NY = 4
BLK_D = 256
BF = jnp.bfloat16
F32 = jnp.float32
VMEM = pl.BlockSpec(memory_space=pltpu.VMEM)
SMEM = pl.BlockSpec(memory_space=pltpu.SMEM)

FULL = {1: 16, 2: 32}
HEAD = 16


def params(mib):
    return pltpu.CompilerParams(vmem_limit_bytes=mib * 1024 * 1024)


def send_rows(blocks):
    return 2 * FULL[blocks] + 8


def slot_rows(blocks):
    return FULL[blocks] + 8


def cost(flops, nbytes):
    return pl.CostEstimate(flops=int(flops), bytes_accessed=int(nbytes), transcendentals=0)


def pack_kernel(len_ref, tok_ref, cot_ref, routes_ref, slots_ref, gate_ref, out_ref):
    position = lax.broadcasted_iota(jnp.int32, (1, TOK), 1)
    end = jnp.int32(0)
    picked = jnp.zeros((1, TOK), F32)
    for seg in range(SEGS):
        length = len_ref[0, seg]
        inside = (position >= end) & (position < end + length)
        picked = jnp.where(inside, length.astype(F32), picked)
        end = end + length
    weight = (TOK / SEGS) / picked
    scale = (weight * gate_ref[...]).astype(BF).astype(F32)
    routes = routes_ref[...].astype(F32)
    slots = slots_ref[...].astype(F32)
    ones = jnp.ones((TOP, TOK), F32)
    fill = jnp.zeros((META - 3 * TOP, TOK), F32)
    out_ref[0:TOK, 0:D] = tok_ref[...]
    out_ref[TOK : 2 * TOK, 0:D] = cot_ref[...]
    out_ref[0:TOK, D : D + META] = jnp.concatenate([routes, slots, ones, fill], axis=0).T.astype(BF)
    out_ref[TOK : 2 * TOK, D : D + META] = jnp.concatenate([routes, slots, scale, fill], axis=0).T.astype(BF)


def pack(tokens, cotangent, routes, slots, gates, lengths):
    return pl.pallas_call(
        pack_kernel,
        out_shape=jax.ShapeDtypeStruct((2 * TOK, D + META), BF),
        in_specs=[SMEM] + [VMEM] * 5,
        out_specs=VMEM,
        compiler_params=params(8),
        cost_estimate=cost(1e6, 2 << 20),
        name="pack",
    )(lengths, tokens, cotangent, routes, slots, gates)


def select_kernel(blocks, split, pos_ref, *refs):
    if split:
        tok_ref, cot_ref = refs[0], refs[1]
        data = jnp.concatenate([tok_ref[:, 0:D], cot_ref[:, 0:D]], axis=0)
        metas = [jnp.concatenate([tok_ref[:, D:], cot_ref[:, D:]], axis=0)]
        outs = refs[2:]
    else:
        data = jnp.concatenate([r[:, 0:D] for r in refs[:blocks]], axis=0)
        metas = [r[:, D:] for r in refs[:blocks]]
        outs = refs[blocks:]
    meta = jnp.concatenate([m.astype(F32).T for m in metas], axis=1)
    width = 2 * TOK * blocks
    lane = lax.broadcasted_iota(jnp.int32, (1, width), 1)
    second = (lane >= 2 * TOK).astype(jnp.int32)
    within = lane - second * (2 * TOK)
    is_cot = (within >= TOK).astype(jnp.int32)
    code = meta[0:TOP] * CAP + meta[TOP : 2 * TOP] + (1024 * is_cot + 2048 * second).astype(F32)
    value = meta[2 * TOP : 3 * TOP]
    rows, full, count = send_rows(blocks), FULL[blocks], CAP * blocks
    rem = count - full
    row = lax.broadcasted_iota(jnp.int32, (rows, 1), 0)
    row_cot = (row >= full + rem).astype(jnp.int32)
    item = jnp.where(row >= full + 8, row - full - 8, row - rem * row_cot)
    used = (row < full + 2 * rem) | (row >= full + 8)
    row_second = (item >= CAP).astype(jnp.int32)
    slot = item - row_second * CAP
    for step in range(NX):
        expert_id = ((pos_ref[0] + step) & (NX - 1)) * NZ + pos_ref[1]
        row_code = expert_id * CAP + slot + 1024 * row_cot + 2048 * row_second
        row_code = jnp.where(used, row_code, -1).astype(F32)
        chosen = jnp.zeros((rows, width), F32)
        for k in range(TOP):
            chosen = chosen + jnp.where(code[k : k + 1] == row_code, value[k : k + 1], 0.0)
        outs[step][...] = jnp.dot(chosen.astype(BF), data, preferred_element_type=F32).astype(BF)


def select(position, inputs, blocks, split=False):
    rows = send_rows(blocks)
    return pl.pallas_call(
        functools.partial(select_kernel, blocks, split),
        out_shape=[jax.ShapeDtypeStruct((rows, D), BF)] * NX,
        in_specs=[SMEM] + [VMEM] * len(inputs),
        out_specs=[VMEM] * NX,
        compiler_params=params(12),
        cost_estimate=cost(2 * NX * rows * 128 * blocks * D, 2 << 20),
        name="select",
    )(position, *inputs)


def chunk_bases(blocks_of):
    bases, base = [], 0
    for blocks in blocks_of:
        bases.append(base)
        base += NX * slot_rows(blocks)
    return bases, base


def expert_kernel(blocks_of, *refs):
    arrays = refs[: NX * len(blocks_of)]
    gate_up, down, tok_ref, cot_ref, grad_ref, act_ref = refs[NX * len(blocks_of) :]
    bases, _ = chunk_bases(blocks_of)
    for index, blocks in enumerate(blocks_of):
        full, rem = FULL[blocks], CAP * blocks - FULL[blocks]
        sub = lax.broadcasted_iota(jnp.int32, (8, 1), 0)
        tok_parts, cot_parts = [], []
        for a in arrays[NX * index : NX * (index + 1)]:
            rows = a[...].astype(F32)
            mixed = rows[full : full + 8]
            tok_parts += [rows[0:full], jnp.where(sub < rem, mixed, 0.0)]
            cot_parts += [rows[full + 8 :], jnp.where(sub < rem, pltpu.roll(mixed, 8 - rem, 0), 0.0)]
        at = pl.ds(bases[index], NX * slot_rows(blocks))
        tok_ref[at, :] = jnp.concatenate(tok_parts, axis=0).astype(BF)
        cot_ref[at, :] = jnp.concatenate(cot_parts, axis=0).astype(BF)
    tile = 256
    for f in range(0, FF, tile):
        gate_pre = jnp.dot(tok_ref[...], gate_up[:, f : f + tile], preferred_element_type=F32)
        up_pre = jnp.dot(tok_ref[...], gate_up[:, FF + f : FF + f + tile], preferred_element_type=F32)
        back = lax.dot_general(
            cot_ref[...], down[f : f + tile, :], (((1,), (1,)), ((), ())), preferred_element_type=F32
        )
        sigmoid = jax.nn.sigmoid(gate_pre)
        silu = gate_pre * sigmoid
        act_ref[:, f : f + tile] = (silu * up_pre).astype(BF)
        gate_grad = back * up_pre * sigmoid * (1.0 + gate_pre * (1.0 - sigmoid))
        grad_ref[:, f : f + tile] = gate_grad.astype(BF)
        grad_ref[:, FF + f : FF + f + tile] = (back * silu).astype(BF)


def expert(arrays, gate_up, down, blocks_of):
    _, total = chunk_bases(blocks_of)
    shapes = [(total, D), (total, D), (total, GU), (total, FF)]
    return pl.pallas_call(
        functools.partial(expert_kernel, blocks_of),
        out_shape=[jax.ShapeDtypeStruct(s, BF) for s in shapes],
        in_specs=[VMEM] * (len(arrays) + 2),
        out_specs=[VMEM] * len(shapes),
        compiler_params=params(24),
        cost_estimate=cost(2 * total * D * GU * 1.5, 20 << 20),
        name="expert",
    )(*arrays, gate_up, down)


def row_grad_kernel(blocks_of, pos_ref, grad_ref, gate_up, out_ref):
    bases, total = chunk_bases(blocks_of)
    main, devices = NX * NZ * HEAD, NX * NZ
    extra = CAP - HEAD
    row = lax.broadcasted_iota(jnp.int32, (main + devices * extra, 1), 0)
    late = (row >= main).astype(jnp.int32)
    rest = row - main
    device = jnp.where(late == 1, rest >> 1, row >> 4)
    slot = jnp.where(late == 1, HEAD + (rest & 1), row & (HEAD - 1))
    step = (pos_ref[0] - (device >> 3)) & (NX - 1)
    away = ((device & (NZ - 1)) - pos_ref[1]) & (NZ - 1)
    place = jnp.zeros_like(row)
    half = NZ // 2
    for index, blocks in enumerate(blocks_of):
        if blocks == 1:
            hit, second = away == (0 if index == 0 else half), 0
        else:
            hit = (away == index) | (away == NZ - index)
            second = (away == index).astype(jnp.int32)
        place = jnp.where(hit, bases[index] + step * slot_rows(blocks) + second * CAP + slot, place)
    col = lax.broadcasted_iota(jnp.int32, (1, total), 1)
    chosen = (col == place).astype(F32).astype(BF)
    ordered = jnp.dot(chosen, grad_ref[...], preferred_element_type=F32).astype(BF)
    tile = 512
    lates = []
    for d in range(0, D, tile):
        part = lax.dot_general(
            ordered, gate_up[d : d + tile, :], (((1,), (1,)), ((), ())), preferred_element_type=F32
        ).astype(BF)
        out_ref[:, d : d + tile] = part[0:main]
        lates.append(part[main:])
    width = D * extra // HEAD
    pieces = [p[:, c : c + width] for p in lates for c in range(0, tile, width)]
    stacked = jnp.concatenate(pieces, axis=0)
    out_row = lax.broadcasted_iota(jnp.int32, (main, 1), 0)
    within = out_row & (HEAD - 1)
    source = (within & 7) * (devices * extra) + (out_row >> 4) * extra + (within >> 3)
    in_row = lax.broadcasted_iota(jnp.int32, (1, len(pieces) * devices * extra), 1)
    fold = (in_row == source).astype(F32).astype(BF)
    out_ref[:, D:] = jnp.dot(fold, stacked, preferred_element_type=F32).astype(BF)


def row_grads(position, grads, gate_up, blocks_of):
    main = NX * NZ * HEAD
    return pl.pallas_call(
        functools.partial(row_grad_kernel, blocks_of),
        out_shape=jax.ShapeDtypeStruct((main, D + D * (CAP - HEAD) // HEAD), BF),
        in_specs=[SMEM, VMEM, VMEM],
        out_specs=VMEM,
        compiler_params=params(24),
        cost_estimate=cost(2 * 640 * D * GU * 1.5, 12 << 20),
        name="row_grads",
    )(position, grads, gate_up)


def combine_kernel(routes_ref, slots_ref, rows_ref, out_ref):
    code = (routes_ref[...].astype(F32) * CAP + slots_ref[...].astype(F32)).T
    main = NX * NZ * HEAD
    col = lax.broadcasted_iota(jnp.int32, (1, main), 1)
    device, within = col >> 4, col & (HEAD - 1)
    head_code = (device * CAP + within).astype(F32)
    late_code = (device * CAP + HEAD + (within >> 3)).astype(F32)
    head = jnp.zeros((TOK, main), F32)
    late = jnp.zeros((TOK, main), F32)
    for k in range(TOP):
        head = head + (code[:, k : k + 1] == head_code).astype(F32)
        late = late + (code[:, k : k + 1] == late_code).astype(F32)
    folds = HEAD // (CAP - HEAD)
    lates = jnp.concatenate([jnp.where((within & 7) == j, late, 0.0) for j in range(folds)], axis=0)
    tail = jnp.dot(lates.astype(BF), rows_ref[:, D:], preferred_element_type=F32)
    total = jnp.dot(head.astype(BF), rows_ref[:, 0:D], preferred_element_type=F32)
    width = D // folds
    for j in range(folds):
        at = slice(j * width, (j + 1) * width)
        out_ref[:, at] = (total[:, at] + tail[j * TOK : (j + 1) * TOK]).astype(BF)


def combine(routes, slots, rows):
    return pl.pallas_call(
        combine_kernel,
        out_shape=jax.ShapeDtypeStruct((TOK, D), BF),
        in_specs=[VMEM] * 3,
        out_specs=VMEM,
        compiler_params=params(12),
        cost_estimate=cost(2 * TOK * 512 * D, 3 << 20),
        name="combine",
    )(routes, slots, rows)


def weight_kernel(hop, which_ref, tok, cot, grad, act, *rest):
    out = rest[-1]
    first = (((0,), (0,)), ((), ()))
    gate_up = lax.dot_general(tok[...], grad[...], first, preferred_element_type=F32)
    down = lax.dot_general(cot[...], act[...], first, preferred_element_type=F32)
    if len(rest) > 1:
        gate_up = gate_up + rest[0][:, 0:GU].astype(F32)
        down = down + rest[0][:, GU:].astype(F32)
    out[:, 0:GU] = gate_up.astype(BF)
    out[:, GU:] = down.astype(BF)
    if hop is not None:
        at = slice(hop * BLK_D // 2, (hop + 1) * BLK_D // 2)
        out[at, 0:GU] = (gate_up[at] + rest[1][:, 0:GU].astype(F32)).astype(BF)
        out[at, GU:] = (down[at] + rest[1][:, GU:].astype(F32)).astype(BF)


def weight_blocks(which, group, received=None, block=0, added=None, hop=None):
    tok, cot, grad, act = group
    count = which.shape[0]

    def cut(a):
        return pl.BlockSpec((a.shape[0], BLK_D), lambda i, w: (0, w[i]))

    def whole(a):
        return pl.BlockSpec(a.shape, lambda i, w: (0, 0))

    specs = [cut(tok), cut(cot), whole(grad), whole(act)]
    extra = []
    if received is not None:
        specs.append(pl.BlockSpec((BLK_D, GU + FF), lambda i, w: (block, 0)))
        extra.append(received)
    if added is not None:
        specs.append(whole(added))
        extra.append(added)
    return pl.pallas_call(
        functools.partial(weight_kernel, hop),
        out_shape=jax.ShapeDtypeStruct((count * BLK_D, GU + FF), BF),
        grid_spec=pltpu.PrefetchScalarGridSpec(
            num_scalar_prefetch=1,
            grid=(count,),
            in_specs=specs,
            out_specs=pl.BlockSpec((BLK_D, GU + FF), lambda i, w: (i, 0)),
        ),
        compiler_params=params(24),
        cost_estimate=cost(2 * 640 * BLK_D * (GU + FF) * count, 5 << 20),
        name="weight_blocks",
    )(which, tok, cot, grad, act, *extra)


def finish_kernel(own, plus, minus, gate_up, down):
    gate_up[...] = (
        own[:, 0:GU].astype(F32) + plus[:, 0:GU].astype(F32) + minus[:, 0:GU].astype(F32)
    ).astype(BF)
    total = own[:, GU:].astype(F32) + plus[:, GU:].astype(F32) + minus[:, GU:].astype(F32)
    down[...] = total.T.astype(BF)


def finish(own, plus, minus):
    return pl.pallas_call(
        finish_kernel,
        out_shape=[jax.ShapeDtypeStruct((BLK_D, GU), BF), jax.ShapeDtypeStruct((FF, BLK_D), BF)],
        in_specs=[VMEM] * 3,
        out_specs=[VMEM] * 2,
        compiler_params=params(16),
        cost_estimate=cost(1e6, 4 << 20),
        name="finish",
    )(own, plus, minus)


def shift(array, axis, size, by):
    return lax.ppermute(array, axis, [(i, (i + by) % size) for i in range(size)])


def per_device(tokens, cotangent, routes, slot_index, gate_probs, lengths, w_gate_up, w_down):
    x, z = lax.axis_index("x"), lax.axis_index("z")
    y, core = lax.axis_index("y"), lax.axis_index("core")
    position = jnp.stack([x, z]).astype(jnp.int32)
    gate_up, down = w_gate_up[0], w_down[0]
    routes, slots, gates = routes.T, slot_index.T, gate_probs.T

    own = pack(tokens, cotangent, routes, slots, gates, lengths)
    up, dn = {0: own}, {0: own}
    for d in range(1, NZ // 2):
        up[d] = shift(up[d - 1], "z", NZ, 1)
        dn[d] = shift(dn[d - 1], "z", NZ, -1)
    half = NZ // 2
    far_tok = shift(up[half - 1][0:TOK], "z", NZ, 1)
    far_cot = shift(dn[half - 1][TOK:], "z", NZ, -1)

    chunks = [((own,), 1, False)]
    chunks += [((up[d], dn[d]), 2, False) for d in range(1, half)]
    chunks += [((far_tok, far_cot), 1, True)]
    blocks_of = tuple(c[1] for c in chunks)

    arrays = []
    for inputs, blocks, split in chunks:
        sent = select(position, inputs, blocks, split)
        arrays += [sent[0]] + [shift(sent[s], "x", NX, s) for s in range(1, NX)]
    group = expert(arrays, gate_up, down, blocks_of)

    sent_back = row_grads(position, group[2], gate_up, blocks_of)
    width = sent_back.shape[1]
    got_back = lax.all_to_all(
        sent_back.reshape(NX * NZ, HEAD, width), ("x", "z"), split_axis=0, concat_axis=0, tiled=True
    )
    token_grad = combine(routes, slots, got_back.reshape(NX * NZ * HEAD, width))

    def blocks_at(steps, of_core):
        return jnp.stack([2 * ((y + s) % NY) + of_core for s in steps]).astype(jnp.int32)

    early = shift(weight_blocks(blocks_at((2, 1), 1 - core), group), "core", 2, 1)
    late = shift(weight_blocks(blocks_at((3, 0), 1 - core), group), "core", 2, 1)
    opposite = weight_blocks(blocks_at((2,), core), group, early, 0)
    hop = BLK_D // 2
    top = shift(opposite[:hop], "y", NY, 1)
    bottom = shift(opposite[hop:], "y", NY, -1)
    plus = shift(weight_blocks(blocks_at((1,), core), group, early, 1, top, 0), "y", NY, 1)
    minus = shift(weight_blocks(blocks_at((3,), core), group, late, 0, bottom, 1), "y", NY, -1)
    mine = weight_blocks(blocks_at((0,), core), group, late, 1)
    grad_gate_up, grad_down = finish(mine, plus, minus)
    return token_grad, grad_gate_up[None], grad_down[None]


def solution(mesh):
    torus = Mesh(mesh.devices.reshape(NY, 2, NX, NZ), ("y", "core", "x", "z"))
    dp, ep = ("y", "core"), ("x", "z")
    return jax.shard_map(
        per_device,
        mesh=torus,
        in_specs=(P(dp + ep, None),) * 6 + (P(ep, None, None),) * 2,
        out_specs=(P(dp + ep, None), P(ep, dp, None), P(ep, None, dp)),
        check_vma=False,
    )
```

```python
import functools

import jax
import jax.numpy as jnp
from jax import lax
from jax.experimental import pallas as pl
from jax.experimental.pallas import tpu as pltpu
from jax.sharding import Mesh
from jax.sharding import PartitionSpec as P

TOP = 8
SEGS = 4
TOK = 64
CAP = 18
D = 2048
FF = 768
GU = 2 * FF
META = 128
NX = 4
NZ = 8
NY = 4
BLK_D = 256
BF = jnp.bfloat16
F32 = jnp.float32
SMEM = pl.BlockSpec(memory_space=pltpu.SMEM)

FULL = {1: 16, 2: 32}
HEAD = 16


def params():
    return pltpu.CompilerParams(vmem_limit_bytes=56 * 1024 * 1024)


def whole(a):
    return pl.BlockSpec(a.shape, lambda i: (0,) * len(a.shape))


def send_rows(blocks):
    return 2 * FULL[blocks] + 8


def slot_rows(blocks):
    return FULL[blocks] + 8


def cost(flops, nbytes):
    return pl.CostEstimate(flops=int(flops), bytes_accessed=int(nbytes), transcendentals=0)


def pack_kernel(len_ref, tok_ref, cot_ref, routes_ref, slots_ref, gate_ref, out_ref):
    position = lax.broadcasted_iota(jnp.int32, (1, TOK), 1)
    end = jnp.int32(0)
    picked = jnp.zeros((1, TOK), F32)
    for seg in range(SEGS):
        length = len_ref[0, seg]
        inside = (position >= end) & (position < end + length)
        picked = jnp.where(inside, length.astype(F32), picked)
        end = end + length
    weight = (TOK / SEGS) / picked
    scale = (weight * gate_ref[...]).astype(BF).astype(F32)
    routes = routes_ref[...].astype(F32)
    slots = slots_ref[...].astype(F32)
    ones = jnp.ones((TOP, TOK), F32)
    fill = jnp.zeros((META - 3 * TOP, TOK), F32)
    out_ref[0:TOK, 0:D] = tok_ref[...]
    out_ref[TOK : 2 * TOK, 0:D] = cot_ref[...]
    out_ref[0:TOK, D : D + META] = jnp.concatenate([routes, slots, ones, fill], axis=0).T.astype(BF)
    out_ref[TOK : 2 * TOK, D : D + META] = jnp.concatenate([routes, slots, scale, fill], axis=0).T.astype(BF)


def pack(tokens, cotangent, routes, slots, gates, lengths):
    return pl.pallas_call(
        pack_kernel,
        out_shape=jax.ShapeDtypeStruct((2 * TOK, D + META), BF),
        grid=(1,),
        in_specs=[SMEM] + [whole(a) for a in (tokens, cotangent, routes, slots, gates)],
        out_specs=pl.BlockSpec((2 * TOK, D + META), lambda i: (0, 0)),
        compiler_params=params(),
        cost_estimate=cost(1e6, 2 << 20),
        name="pack",
    )(lengths, tokens, cotangent, routes, slots, gates)


def select_kernel(blocks, split, pos_ref, *refs):
    if split:
        tok_ref, cot_ref = refs[0], refs[1]
        data = jnp.concatenate([tok_ref[:, 0:D], cot_ref[:, 0:D]], axis=0)
        metas = [jnp.concatenate([tok_ref[:, D:], cot_ref[:, D:]], axis=0)]
        outs = refs[2:]
    else:
        data = jnp.concatenate([r[:, 0:D] for r in refs[:blocks]], axis=0)
        metas = [r[:, D:] for r in refs[:blocks]]
        outs = refs[blocks:]
    meta = jnp.concatenate([m.astype(F32).T for m in metas], axis=1)
    width = 2 * TOK * blocks
    lane = lax.broadcasted_iota(jnp.int32, (1, width), 1)
    second = (lane >= 2 * TOK).astype(jnp.int32)
    within = lane - second * (2 * TOK)
    is_cot = (within >= TOK).astype(jnp.int32)
    code = meta[0:TOP] * CAP + meta[TOP : 2 * TOP] + (1024 * is_cot + 2048 * second).astype(F32)
    value = meta[2 * TOP : 3 * TOP]
    rows, full, count = send_rows(blocks), FULL[blocks], CAP * blocks
    rem = count - full
    row = lax.broadcasted_iota(jnp.int32, (rows, 1), 0)
    row_cot = (row >= full + rem).astype(jnp.int32)
    item = jnp.where(row >= full + 8, row - full - 8, row - rem * row_cot)
    used = (row < full + 2 * rem) | (row >= full + 8)
    row_second = (item >= CAP).astype(jnp.int32)
    slot = item - row_second * CAP
    for step in range(NX):
        expert_id = ((pos_ref[0] + step) & (NX - 1)) * NZ + pos_ref[1]
        row_code = expert_id * CAP + slot + 1024 * row_cot + 2048 * row_second
        row_code = jnp.where(used, row_code, -1).astype(F32)
        chosen = jnp.zeros((rows, width), F32)
        for k in range(TOP):
            chosen = chosen + jnp.where(code[k : k + 1] == row_code, value[k : k + 1], 0.0)
        outs[step][...] = jnp.dot(chosen.astype(BF), data, preferred_element_type=F32).astype(BF)


def select(position, inputs, blocks, split=False):
    rows = send_rows(blocks)
    return pl.pallas_call(
        functools.partial(select_kernel, blocks, split),
        out_shape=[jax.ShapeDtypeStruct((rows, D), BF)] * NX,
        grid=(1,),
        in_specs=[SMEM] + [whole(a) for a in inputs],
        out_specs=[pl.BlockSpec((rows, D), lambda i: (0, 0))] * NX,
        compiler_params=params(),
        cost_estimate=cost(2 * NX * rows * 128 * blocks * D, 2 << 20),
        name="select",
    )(position, *inputs)


def chunk_bases(blocks_of):
    bases, base = [], 0
    for blocks in blocks_of:
        bases.append(base)
        base += NX * slot_rows(blocks)
    return bases, base


TILE = 256


def gather_rows(blocks_of, arrays, tok, cot):
    bases, _ = chunk_bases(blocks_of)
    for index, blocks in enumerate(blocks_of):
        full, rem = FULL[blocks], CAP * blocks - FULL[blocks]
        sub = lax.broadcasted_iota(jnp.int32, (8, 1), 0)
        tok_parts, cot_parts = [], []
        for a in arrays[NX * index : NX * (index + 1)]:
            rows = a[...].astype(F32)
            mixed = rows[full : full + 8]
            tok_parts += [rows[0:full], jnp.where(sub < rem, mixed, 0.0)]
            cot_parts += [rows[full + 8 :], jnp.where(sub < rem, pltpu.roll(mixed, 8 - rem, 0), 0.0)]
        at = pl.ds(bases[index], NX * slot_rows(blocks))
        tok[at, :] = jnp.concatenate(tok_parts, axis=0).astype(BF)
        cot[at, :] = jnp.concatenate(cot_parts, axis=0).astype(BF)


def return_order(blocks_of, pos_ref, total):
    bases, _ = chunk_bases(blocks_of)
    main, devices = NX * NZ * HEAD, NX * NZ
    extra = CAP - HEAD
    row = lax.broadcasted_iota(jnp.int32, (main + devices * extra, 1), 0)
    late = row >= main
    rest = row - main
    device = jnp.where(late, rest >> 1, row >> 4)
    slot = jnp.where(late, HEAD + (rest & 1), row & (HEAD - 1))
    step = (pos_ref[0] - (device >> 3)) & (NX - 1)
    away = ((device & (NZ - 1)) - pos_ref[1]) & (NZ - 1)
    place = jnp.zeros_like(row)
    half = NZ // 2
    for index, blocks in enumerate(blocks_of):
        if blocks == 1:
            hit, second = away == (0 if index == 0 else half), 0
        else:
            hit = (away == index) | (away == NZ - index)
            second = (away == index).astype(jnp.int32)
        place = jnp.where(hit, bases[index] + step * slot_rows(blocks) + second * CAP + slot, place)
    col = lax.broadcasted_iota(jnp.int32, (1, total), 1)
    return (col == place).astype(F32).astype(BF)


def expert_kernel(blocks_of, pos_ref, *refs):
    count = NX * len(blocks_of)
    arrays, (gate_up_hbm, down_hbm) = refs[:count], refs[count : count + 2]
    outs = refs[count + 2 : count + 6]
    back_ref = refs[count + 6]
    gate_up, down, tok, cot, grad, act, in_sems, out_sems = refs[count + 7 :]
    _, total = chunk_bases(blocks_of)
    loads = []
    for index, f in enumerate(range(0, FF, TILE)):
        loads.append([
            pltpu.make_async_copy(
                gate_up_hbm.at[:, pl.ds(f, TILE)], gate_up.at[:, pl.ds(f, TILE)], in_sems.at[3 * index]
            ),
            pltpu.make_async_copy(
                gate_up_hbm.at[:, pl.ds(FF + f, TILE)], gate_up.at[:, pl.ds(FF + f, TILE)], in_sems.at[3 * index + 1]
            ),
            pltpu.make_async_copy(
                down_hbm.at[pl.ds(f, TILE), :], down.at[pl.ds(f, TILE), :], in_sems.at[3 * index + 2]
            ),
        ])
    for group in loads:
        for copy in group:
            copy.start()
    stores = [pltpu.make_async_copy(v, o, out_sems.at[i]) for i, (v, o) in enumerate(zip((tok, cot, grad, act), outs))]
    gather_rows(blocks_of, arrays, tok, cot)
    stores[0].start()
    stores[1].start()
    for index, f in enumerate(range(0, FF, TILE)):
        for copy in loads[index]:
            copy.wait()
        gate_pre = jnp.dot(tok[...], gate_up[:, f : f + TILE], preferred_element_type=F32)
        up_pre = jnp.dot(tok[...], gate_up[:, FF + f : FF + f + TILE], preferred_element_type=F32)
        back = lax.dot_general(
            cot[...], down[f : f + TILE, :], (((1,), (1,)), ((), ())), preferred_element_type=F32
        )
        sigmoid = jax.nn.sigmoid(gate_pre)
        silu = gate_pre * sigmoid
        act[:, f : f + TILE] = (silu * up_pre).astype(BF)
        gate_grad = back * up_pre * sigmoid * (1.0 + gate_pre * (1.0 - sigmoid))
        grad[:, f : f + TILE] = gate_grad.astype(BF)
        grad[:, FF + f : FF + f + TILE] = (back * silu).astype(BF)
    stores[2].start()
    stores[3].start()

    main, lates_count = NX * NZ * HEAD, NX * NZ * (CAP - HEAD)
    ordered = jnp.dot(return_order(blocks_of, pos_ref, total), grad[...], preferred_element_type=F32).astype(BF)
    tile = 512
    lates = []
    for d in range(0, D, tile):
        part = lax.dot_general(
            ordered, gate_up[d : d + tile, :], (((1,), (1,)), ((), ())), preferred_element_type=F32
        ).astype(BF)
        back_ref[:, d : d + tile] = part[0:main]
        lates.append(part[main:])
    width = D * (CAP - HEAD) // HEAD
    pieces = [p[:, c : c + width] for p in lates for c in range(0, tile, width)]
    stacked = jnp.concatenate(pieces, axis=0)
    out_row = lax.broadcasted_iota(jnp.int32, (main, 1), 0)
    within = out_row & (HEAD - 1)
    source = (within & 7) * lates_count + (out_row >> 4) * (CAP - HEAD) + (within >> 3)
    in_row = lax.broadcasted_iota(jnp.int32, (1, len(pieces) * lates_count), 1)
    fold = (in_row == source).astype(F32).astype(BF)
    back_ref[:, D:] = jnp.dot(fold, stacked, preferred_element_type=F32).astype(BF)
    for store in stores:
        store.wait()


def expert(position, arrays, gate_up, down, blocks_of):
    _, total = chunk_bases(blocks_of)
    main = NX * NZ * HEAD
    wide = D + D * (CAP - HEAD) // HEAD
    shapes = [(total, D), (total, D), (total, GU), (total, FF)]
    any_spec = pl.BlockSpec(memory_space=pl.ANY)
    outs = pl.pallas_call(
        functools.partial(expert_kernel, blocks_of),
        out_shape=[jax.ShapeDtypeStruct(s, BF) for s in shapes + [(main, wide)]],
        grid=(1,),
        in_specs=[SMEM] + [whole(a) for a in arrays] + [any_spec] * 2,
        out_specs=[any_spec] * len(shapes) + [pl.BlockSpec((main, wide), lambda i: (0, 0))],
        scratch_shapes=[pltpu.VMEM((D, GU), BF), pltpu.VMEM((FF, D), BF)]
        + [pltpu.VMEM(s, BF) for s in shapes]
        + [pltpu.SemaphoreType.DMA((3 * (FF // TILE),)), pltpu.SemaphoreType.DMA((4,))],
        compiler_params=params(),
        cost_estimate=cost(2 * total * D * GU * 2.5, 30 << 20),
        name="expert",
    )(position, *arrays, gate_up, down)
    return outs[:4], outs[4]


def combine_kernel(routes_ref, slots_ref, rows_ref, out_ref):
    code = (routes_ref[...].astype(F32) * CAP + slots_ref[...].astype(F32)).T
    main = NX * NZ * HEAD
    col = lax.broadcasted_iota(jnp.int32, (1, main), 1)
    device, within = col >> 4, col & (HEAD - 1)
    head_code = (device * CAP + within).astype(F32)
    late_code = (device * CAP + HEAD + (within >> 3)).astype(F32)
    head = jnp.zeros((TOK, main), F32)
    late = jnp.zeros((TOK, main), F32)
    for k in range(TOP):
        head = head + (code[:, k : k + 1] == head_code).astype(F32)
        late = late + (code[:, k : k + 1] == late_code).astype(F32)
    folds = HEAD // (CAP - HEAD)
    lates = jnp.concatenate([jnp.where((within & 7) == j, late, 0.0) for j in range(folds)], axis=0)
    tail = jnp.dot(lates.astype(BF), rows_ref[:, D:], preferred_element_type=F32)
    total = jnp.dot(head.astype(BF), rows_ref[:, 0:D], preferred_element_type=F32)
    width = D // folds
    for j in range(folds):
        at = slice(j * width, (j + 1) * width)
        out_ref[:, at] = (total[:, at] + tail[j * TOK : (j + 1) * TOK]).astype(BF)


def combine(routes, slots, rows):
    return pl.pallas_call(
        combine_kernel,
        out_shape=jax.ShapeDtypeStruct((TOK, D), BF),
        grid=(1,),
        in_specs=[whole(a) for a in (routes, slots, rows)],
        out_specs=pl.BlockSpec((TOK, D), lambda i: (0, 0)),
        compiler_params=params(),
        cost_estimate=cost(2 * TOK * 512 * D, 3 << 20),
        name="combine",
    )(routes, slots, rows)


def weight_kernel(extras, hop, which_ref, tok, cot, grad, act, *rest):
    extra, outs = rest[:extras], rest[extras:]
    first = (((0,), (0,)), ((), ()))
    rows = BLK_D // len(outs)
    for cols, left, right in ((slice(0, GU), tok, grad), (slice(GU, GU + FF), cot, act)):
        total = lax.dot_general(left[...], right[...], first, preferred_element_type=F32)
        if extras:
            total = total + extra[0][:, cols].astype(F32)
        for i, out in enumerate(outs):
            out[:, cols] = total[i * rows : (i + 1) * rows].astype(BF)
        if hop is not None:
            at = slice(hop * BLK_D // 2, (hop + 1) * BLK_D // 2)
            outs[0][at, cols] = (total[at] + extra[1][:, cols].astype(F32)).astype(BF)


def weight_blocks(which, group, received=None, block=0, added=None, hop=None, halves=False):
    tok, cot, grad, act = group
    count = which.shape[0]

    def cut(a):
        return pl.BlockSpec((a.shape[0], BLK_D), lambda i, w: (0, w[i]))

    def full(a):
        return pl.BlockSpec(a.shape, lambda i, w: (0, 0))

    specs = [cut(tok), cut(cot), full(grad), full(act)]
    extra = []
    if received is not None:
        specs.append(pl.BlockSpec((BLK_D, GU + FF), lambda i, w: (block, 0)))
        extra.append(received)
    if added is not None:
        specs.append(full(added))
        extra.append(added)
    rows = BLK_D // 2 if halves else BLK_D
    return pl.pallas_call(
        functools.partial(weight_kernel, len(extra), hop),
        out_shape=[jax.ShapeDtypeStruct((count * rows, GU + FF), BF)] * (2 if halves else 1),
        grid_spec=pltpu.PrefetchScalarGridSpec(
            num_scalar_prefetch=1,
            grid=(count,),
            in_specs=specs,
            out_specs=[pl.BlockSpec((rows, GU + FF), lambda i, w: (i, 0))] * (2 if halves else 1),
        ),
        compiler_params=params(),
        cost_estimate=cost(2 * 640 * BLK_D * (GU + FF) * count, 5 << 20),
        name="weight_blocks",
    )(which, tok, cot, grad, act, *extra)


def finish_kernel(own, plus, minus, gate_up, down):
    gate_up[...] = (
        own[:, 0:GU].astype(F32) + plus[:, 0:GU].astype(F32) + minus[:, 0:GU].astype(F32)
    ).astype(BF)
    total = own[:, GU:].astype(F32) + plus[:, GU:].astype(F32) + minus[:, GU:].astype(F32)
    down[...] = total.T.astype(BF)


def finish(own, plus, minus):
    return pl.pallas_call(
        finish_kernel,
        out_shape=[jax.ShapeDtypeStruct((BLK_D, GU), BF), jax.ShapeDtypeStruct((FF, BLK_D), BF)],
        grid=(1,),
        in_specs=[whole(a) for a in (own, plus, minus)],
        out_specs=[pl.BlockSpec((BLK_D, GU), lambda i: (0, 0)), pl.BlockSpec((FF, BLK_D), lambda i: (0, 0))],
        compiler_params=params(),
        cost_estimate=cost(1e6, 4 << 20),
        name="finish",
    )(own, plus, minus)


def shift(array, axis, size, by):
    return lax.ppermute(array, axis, [(i, (i + by) % size) for i in range(size)])


def per_device(tokens, cotangent, routes, slot_index, gate_probs, lengths, w_gate_up, w_down):
    x, z = lax.axis_index("x"), lax.axis_index("z")
    y, core = lax.axis_index("y"), lax.axis_index("core")
    position = jnp.stack([x, z]).astype(jnp.int32)
    gate_up, down = w_gate_up[0], w_down[0]
    routes, slots, gates = routes.T, slot_index.T, gate_probs.T

    own = pack(tokens, cotangent, routes, slots, gates, lengths)
    up, dn = {0: own}, {0: own}
    for d in range(1, NZ // 2):
        up[d] = shift(up[d - 1], "z", NZ, 1)
        dn[d] = shift(dn[d - 1], "z", NZ, -1)
    half = NZ // 2
    far_tok = shift(up[half - 1][0:TOK], "z", NZ, 1)
    far_cot = shift(dn[half - 1][TOK:], "z", NZ, -1)

    chunks = [((own,), 1, False)]
    chunks += [((up[d], dn[d]), 2, False) for d in range(1, half)]
    chunks += [((far_tok, far_cot), 1, True)]
    blocks_of = tuple(c[1] for c in chunks)

    results = []
    for index, (inputs, blocks, split) in enumerate(chunks):
        before = {1: 0, 3: 1, 4: 2}.get(index)
        if before is not None:
            inputs, results[before] = lax.optimization_barrier((inputs, results[before]))
        sent = select(position, inputs, blocks, split)
        results.append([sent[0]] + [shift(sent[s], "x", NX, s) for s in range(1, NX)])
    arrays = [a for r in results for a in r]
    group, sent_back = expert(position, arrays, gate_up, down, blocks_of)
    width = sent_back.shape[1]
    got_back = lax.all_to_all(
        sent_back.reshape(NX * NZ, HEAD, width), ("x", "z"), split_axis=0, concat_axis=0, tiled=True
    )
    token_grad = combine(routes, slots, got_back.reshape(NX * NZ * HEAD, width))

    def blocks_at(steps, of_core):
        return jnp.stack([2 * ((y + s) % NY) + of_core for s in steps]).astype(jnp.int32)

    early = shift(weight_blocks(blocks_at((2, 1), 1 - core), group)[0], "core", 2, 1)
    late = shift(weight_blocks(blocks_at((3, 0), 1 - core), group)[0], "core", 2, 1)
    top, bottom = weight_blocks(blocks_at((2,), core), group, early, 0, halves=True)
    top = shift(top, "y", NY, 1)
    bottom = shift(bottom, "y", NY, -1)
    plus = shift(weight_blocks(blocks_at((1,), core), group, early, 1, top, 0)[0], "y", NY, 1)
    minus = shift(weight_blocks(blocks_at((3,), core), group, late, 0, bottom, 1)[0], "y", NY, -1)
    (mine,) = weight_blocks(blocks_at((0,), core), group, late, 1)
    grad_gate_up, grad_down = finish(mine, plus, minus)
    return token_grad, grad_gate_up[None], grad_down[None]


def solution(mesh):
    torus = Mesh(mesh.devices.reshape(NY, 2, NX, NZ), ("y", "core", "x", "z"))
    dp, ep = ("y", "core"), ("x", "z")
    return jax.shard_map(
        per_device,
        mesh=torus,
        in_specs=(P(dp + ep, None),) * 6 + (P(ep, None, None),) * 2,
        out_specs=(P(dp + ep, None), P(ep, dp, None), P(ep, None, dp)),
        check_vma=False,
    )
```

```python
import functools

import jax
import jax.numpy as jnp
from jax import lax
from jax.experimental import pallas as pl
from jax.experimental.pallas import tpu as pltpu
from jax.sharding import Mesh
from jax.sharding import PartitionSpec as P

TOP = 8
SEGS = 4
TOK = 64
CAP = 18
D = 2048
FF = 768
GU = 2 * FF
META = 128
NX = 4
NZ = 8
NY = 4
BLK_D = 256
BF = jnp.bfloat16
F32 = jnp.float32
SMEM = pl.BlockSpec(memory_space=pltpu.SMEM)

FULL = {1: 16, 2: 32}
HEAD = 16


def params():
    return pltpu.CompilerParams(vmem_limit_bytes=56 * 1024 * 1024)


def whole(a):
    return pl.BlockSpec(a.shape, lambda i: (0,) * len(a.shape))


def send_rows(blocks):
    return 2 * FULL[blocks] + 8


def slot_rows(blocks):
    return FULL[blocks] + 8


def cost(flops, nbytes):
    return pl.CostEstimate(flops=int(flops), bytes_accessed=int(nbytes), transcendentals=0)


def pick(blocks, pos_ref, data, meta, outs):
    width = 2 * TOK * blocks
    lane = lax.broadcasted_iota(jnp.int32, (1, width), 1)
    second = (lane >= 2 * TOK).astype(jnp.int32)
    within = lane - second * (2 * TOK)
    is_cot = (within >= TOK).astype(jnp.int32)
    code = meta[0:TOP] * CAP + meta[TOP : 2 * TOP] + (1024 * is_cot + 2048 * second).astype(F32)
    value = meta[2 * TOP : 3 * TOP]
    rows, full, count = send_rows(blocks), FULL[blocks], CAP * blocks
    rem = count - full
    row = lax.broadcasted_iota(jnp.int32, (rows, 1), 0)
    row_cot = (row >= full + rem).astype(jnp.int32)
    item = jnp.where(row >= full + 8, row - full - 8, row - rem * row_cot)
    used = (row < full + 2 * rem) | (row >= full + 8)
    row_second = (item >= CAP).astype(jnp.int32)
    slot = item - row_second * CAP
    for step in range(NX):
        expert_id = ((pos_ref[0] + step) & (NX - 1)) * NZ + pos_ref[1]
        row_code = expert_id * CAP + slot + 1024 * row_cot + 2048 * row_second
        row_code = jnp.where(used, row_code, -1).astype(F32)
        chosen = jnp.zeros((rows, width), F32)
        for k in range(TOP):
            chosen = chosen + jnp.where(code[k : k + 1] == row_code, value[k : k + 1], 0.0)
        outs[step][...] = jnp.dot(chosen.astype(BF), data, preferred_element_type=F32).astype(BF)


def pack_kernel(pos_ref, len_ref, tok_ref, cot_ref, routes_ref, slots_ref, gate_ref, out_ref, *outs):
    position = lax.broadcasted_iota(jnp.int32, (1, TOK), 1)
    end = jnp.int32(0)
    picked = jnp.zeros((1, TOK), F32)
    for seg in range(SEGS):
        length = len_ref[0, seg]
        inside = (position >= end) & (position < end + length)
        picked = jnp.where(inside, length.astype(F32), picked)
        end = end + length
    weight = (TOK / SEGS) / picked
    scale = (weight * gate_ref[...]).astype(BF).astype(F32)
    routes = routes_ref[...].astype(F32)
    slots = slots_ref[...].astype(F32)
    ones = jnp.ones((TOP, TOK), F32)
    fill = jnp.zeros((META - 3 * TOP, TOK), F32)
    tok_meta = jnp.concatenate([routes, slots, ones, fill], axis=0).T
    cot_meta = jnp.concatenate([routes, slots, scale, fill], axis=0).T
    out_ref[0:TOK, 0:D] = tok_ref[...]
    out_ref[TOK : 2 * TOK, 0:D] = cot_ref[...]
    out_ref[0:TOK, D : D + META] = tok_meta.astype(BF)
    out_ref[TOK : 2 * TOK, D : D + META] = cot_meta.astype(BF)
    data = jnp.concatenate([tok_ref[...], cot_ref[...]], axis=0)
    pick(1, pos_ref, data, jnp.concatenate([tok_meta, cot_meta], axis=0).T, outs)


def pack(position, tokens, cotangent, routes, slots, gates, lengths):
    rows = send_rows(1)
    outs = pl.pallas_call(
        pack_kernel,
        out_shape=[jax.ShapeDtypeStruct((2 * TOK, D + META), BF)] + [jax.ShapeDtypeStruct((rows, D), BF)] * NX,
        grid=(1,),
        in_specs=[SMEM] * 2 + [whole(a) for a in (tokens, cotangent, routes, slots, gates)],
        out_specs=[pl.BlockSpec((2 * TOK, D + META), lambda i: (0, 0))]
        + [pl.BlockSpec((rows, D), lambda i: (0, 0))] * NX,
        compiler_params=params(),
        cost_estimate=cost(1e6, 2 << 20),
        name="pack",
    )(position, lengths, tokens, cotangent, routes, slots, gates)
    return outs[0], outs[1:]


def select_kernel(blocks, split, pos_ref, *refs):
    if split:
        inputs, outs = refs[:2], refs[2:]
        metas = [jnp.concatenate([r[:, D:] for r in inputs], axis=0)]
    else:
        inputs, outs = refs[:blocks], refs[blocks:]
        metas = [r[:, D:] for r in inputs]
    data = jnp.concatenate([r[:, 0:D] for r in inputs], axis=0)
    pick(blocks, pos_ref, data, jnp.concatenate([m.astype(F32).T for m in metas], axis=1), outs)


def select(position, inputs, blocks, split=False):
    rows = send_rows(blocks)
    return pl.pallas_call(
        functools.partial(select_kernel, blocks, split),
        out_shape=[jax.ShapeDtypeStruct((rows, D), BF)] * NX,
        grid=(1,),
        in_specs=[SMEM] + [whole(a) for a in inputs],
        out_specs=[pl.BlockSpec((rows, D), lambda i: (0, 0))] * NX,
        compiler_params=params(),
        cost_estimate=cost(2 * NX * rows * 128 * blocks * D, 2 << 20),
        name="select",
    )(position, *inputs)


def chunk_bases(blocks_of):
    bases, base = [], 0
    for blocks in blocks_of:
        bases.append(base)
        base += NX * slot_rows(blocks)
    return bases, base


TILE = 256


def gather_rows(blocks_of, arrays, copies, tok, cot):
    bases, _ = chunk_bases(blocks_of)
    for index, blocks in enumerate(blocks_of):
        for copy in copies[NX * index : NX * (index + 1)]:
            copy.wait()
        full, rem = FULL[blocks], CAP * blocks - FULL[blocks]
        sub = lax.broadcasted_iota(jnp.int32, (8, 1), 0)
        tok_parts, cot_parts = [], []
        for a in arrays[NX * index : NX * (index + 1)]:
            rows = a[...].astype(F32)
            mixed = rows[full : full + 8]
            tok_parts += [rows[0:full], jnp.where(sub < rem, mixed, 0.0)]
            cot_parts += [rows[full + 8 :], jnp.where(sub < rem, pltpu.roll(mixed, 8 - rem, 0), 0.0)]
        at = pl.ds(bases[index], NX * slot_rows(blocks))
        tok[at, :] = jnp.concatenate(tok_parts, axis=0).astype(BF)
        cot[at, :] = jnp.concatenate(cot_parts, axis=0).astype(BF)


def return_order(blocks_of, pos_ref, total):
    bases, _ = chunk_bases(blocks_of)
    main, devices = NX * NZ * HEAD, NX * NZ
    extra = CAP - HEAD
    row = lax.broadcasted_iota(jnp.int32, (main + devices * extra, 1), 0)
    late = row >= main
    rest = row - main
    device = jnp.where(late, rest >> 1, row >> 4)
    slot = jnp.where(late, HEAD + (rest & 1), row & (HEAD - 1))
    step = (pos_ref[0] - (device >> 3)) & (NX - 1)
    away = ((device & (NZ - 1)) - pos_ref[1]) & (NZ - 1)
    place = jnp.zeros_like(row)
    half = NZ // 2
    for index, blocks in enumerate(blocks_of):
        if blocks == 1:
            hit, second = away == (0 if index == 0 else half), 0
        else:
            hit = (away == index) | (away == NZ - index)
            second = (away == index).astype(jnp.int32)
        place = jnp.where(hit, bases[index] + step * slot_rows(blocks) + second * CAP + slot, place)
    col = lax.broadcasted_iota(jnp.int32, (1, total), 1)
    return (col == place).astype(F32).astype(BF)


def expert_kernel(blocks_of, pos_ref, *refs):
    count = NX * len(blocks_of)
    arrays, (gate_up_hbm, down_hbm) = refs[:count], refs[count : count + 2]
    outs = refs[count + 2 : count + 7]
    held = refs[count + 7 : 2 * count + 7]
    gate_up, down, tok, cot, grad, act, back_ref, row_sems, in_sems, out_sems = refs[2 * count + 7 :]
    _, total = chunk_bases(blocks_of)
    copies = [pltpu.make_async_copy(a, h, row_sems.at[i]) for i, (a, h) in enumerate(zip(arrays, held))]
    for copy in copies:
        copy.start()
    loads = []
    for index, f in enumerate(range(0, FF, TILE)):
        loads.append([
            pltpu.make_async_copy(
                gate_up_hbm.at[:, pl.ds(f, TILE)], gate_up.at[:, pl.ds(f, TILE)], in_sems.at[3 * index]
            ),
            pltpu.make_async_copy(
                gate_up_hbm.at[:, pl.ds(FF + f, TILE)], gate_up.at[:, pl.ds(FF + f, TILE)], in_sems.at[3 * index + 1]
            ),
            pltpu.make_async_copy(
                down_hbm.at[pl.ds(f, TILE), :], down.at[pl.ds(f, TILE), :], in_sems.at[3 * index + 2]
            ),
        ])
    for group in loads:
        for copy in group:
            copy.start()
    stores = [pltpu.make_async_copy(v, o, out_sems.at[i]) for i, (v, o) in enumerate(zip((tok, cot, grad, act), outs))]
    gather_rows(blocks_of, held, copies, tok, cot)
    stores[0].start()
    stores[1].start()
    for index, f in enumerate(range(0, FF, TILE)):
        for copy in loads[index]:
            copy.wait()
        gate_pre = jnp.dot(tok[...], gate_up[:, f : f + TILE], preferred_element_type=F32)
        up_pre = jnp.dot(tok[...], gate_up[:, FF + f : FF + f + TILE], preferred_element_type=F32)
        back = lax.dot_general(
            cot[...], down[f : f + TILE, :], (((1,), (1,)), ((), ())), preferred_element_type=F32
        )
        sigmoid = jax.nn.sigmoid(gate_pre)
        silu = gate_pre * sigmoid
        act[:, f : f + TILE] = (silu * up_pre).astype(BF)
        gate_grad = back * up_pre * sigmoid * (1.0 + gate_pre * (1.0 - sigmoid))
        grad[:, f : f + TILE] = gate_grad.astype(BF)
        grad[:, FF + f : FF + f + TILE] = (back * silu).astype(BF)
    stores[2].start()
    stores[3].start()

    main, lates_count = NX * NZ * HEAD, NX * NZ * (CAP - HEAD)
    ordered = jnp.dot(return_order(blocks_of, pos_ref, total), grad[...], preferred_element_type=F32).astype(BF)
    tile = 512
    lates, back_stores = [], []

    def back_store(at, size):
        cols = pl.ds(at, size)
        return pltpu.make_async_copy(back_ref.at[:, cols], outs[4].at[:, cols], out_sems.at[4 + at // tile])

    for d in range(0, D, tile):
        part = lax.dot_general(
            ordered, gate_up[d : d + tile, :], (((1,), (1,)), ((), ())), preferred_element_type=F32
        ).astype(BF)
        back_ref[:, d : d + tile] = part[0:main]
        back_stores.append(back_store(d, tile))
        back_stores[-1].start()
        lates.append(part[main:])
    width = D * (CAP - HEAD) // HEAD
    pieces = [p[:, c : c + width] for p in lates for c in range(0, tile, width)]
    stacked = jnp.concatenate(pieces, axis=0)
    out_row = lax.broadcasted_iota(jnp.int32, (main, 1), 0)
    within = out_row & (HEAD - 1)
    source = (within & 7) * lates_count + (out_row >> 4) * (CAP - HEAD) + (within >> 3)
    in_row = lax.broadcasted_iota(jnp.int32, (1, len(pieces) * lates_count), 1)
    fold = (in_row == source).astype(F32).astype(BF)
    back_ref[:, D:] = jnp.dot(fold, stacked, preferred_element_type=F32).astype(BF)
    back_stores.append(back_store(D, width))
    back_stores[-1].start()
    for store in stores + back_stores:
        store.wait()


def expert(position, arrays, gate_up, down, blocks_of):
    _, total = chunk_bases(blocks_of)
    main = NX * NZ * HEAD
    wide = D + D * (CAP - HEAD) // HEAD
    shapes = [(total, D), (total, D), (total, GU), (total, FF)]
    any_spec = pl.BlockSpec(memory_space=pl.ANY)
    outs = pl.pallas_call(
        functools.partial(expert_kernel, blocks_of),
        out_shape=[jax.ShapeDtypeStruct(s, BF) for s in shapes + [(main, wide)]],
        grid=(1,),
        in_specs=[SMEM] + [any_spec] * (len(arrays) + 2),
        out_specs=[any_spec] * (len(shapes) + 1),
        scratch_shapes=[pltpu.VMEM(a.shape, BF) for a in arrays]
        + [pltpu.VMEM((D, GU), BF), pltpu.VMEM((FF, D), BF)]
        + [pltpu.VMEM(s, BF) for s in shapes + [(main, wide)]]
        + [pltpu.SemaphoreType.DMA((n,)) for n in (len(arrays), 3 * (FF // TILE), 9)],
        compiler_params=params(),
        cost_estimate=cost(2 * total * D * GU * 2.5, 30 << 20),
        name="expert",
    )(position, *arrays, gate_up, down)
    return outs[:4], outs[4]


def combine_kernel(routes_ref, slots_ref, rows_ref, out_ref):
    code = (routes_ref[...].astype(F32) * CAP + slots_ref[...].astype(F32)).T
    main = NX * NZ * HEAD
    col = lax.broadcasted_iota(jnp.int32, (1, main), 1)
    device, within = col >> 4, col & (HEAD - 1)
    head_code = (device * CAP + within).astype(F32)
    late_code = (device * CAP + HEAD + (within >> 3)).astype(F32)
    head = jnp.zeros((TOK, main), F32)
    late = jnp.zeros((TOK, main), F32)
    for k in range(TOP):
        head = head + (code[:, k : k + 1] == head_code).astype(F32)
        late = late + (code[:, k : k + 1] == late_code).astype(F32)
    folds = HEAD // (CAP - HEAD)
    lates = jnp.concatenate([jnp.where((within & 7) == j, late, 0.0) for j in range(folds)], axis=0)
    tail = jnp.dot(lates.astype(BF), rows_ref[:, D:], preferred_element_type=F32)
    total = jnp.dot(head.astype(BF), rows_ref[:, 0:D], preferred_element_type=F32)
    width = D // folds
    for j in range(folds):
        at = slice(j * width, (j + 1) * width)
        out_ref[:, at] = (total[:, at] + tail[j * TOK : (j + 1) * TOK]).astype(BF)


def combine(routes, slots, rows):
    return pl.pallas_call(
        combine_kernel,
        out_shape=jax.ShapeDtypeStruct((TOK, D), BF),
        grid=(1,),
        in_specs=[whole(a) for a in (routes, slots, rows)],
        out_specs=pl.BlockSpec((TOK, D), lambda i: (0, 0)),
        compiler_params=params(),
        cost_estimate=cost(2 * TOK * 512 * D, 3 << 20),
        name="combine",
    )(routes, slots, rows)


def weight_kernel(count, halves, which_ref, tok, cot, grad, act, *rest):
    extra, outs = (rest[:1], rest[1:]) if len(rest) > (2 * count if halves else 1) else ((), rest)
    first = (((0,), (0,)), ((), ()))
    rows = BLK_D // 2
    for cols, left, right in ((slice(0, GU), tok, grad), (slice(GU, GU + FF), cot, act)):
        total = lax.dot_general(left[...], right[...], first, preferred_element_type=F32)
        if extra:
            total = total + extra[0][:, cols].astype(F32)
        total = total.astype(BF)
        if not halves:
            outs[0][:, cols] = total
            continue
        for i in range(count):

            @pl.when(pl.program_id(0) == i)
            def _():
                outs[2 * i][:, cols] = total[0:rows]
                outs[2 * i + 1][:, cols] = total[rows:]


def weight_blocks(which, group, received=None, block=0, halves=False):
    tok, cot, grad, act = group
    count = which.shape[0]

    def cut(a):
        return pl.BlockSpec((a.shape[0], BLK_D), lambda i, w: (0, w[i]))

    def full(a):
        return pl.BlockSpec(a.shape, lambda i, w: (0, 0))

    specs = [cut(tok), cut(cot), full(grad), full(act)]
    extra = []
    if received is not None:
        specs.append(pl.BlockSpec((BLK_D, GU + FF), lambda i, w: (block + i, 0)))
        extra.append(received)
    if halves:
        shapes = [(BLK_D // 2, GU + FF)] * (2 * count)
        out_specs = [pl.BlockSpec(shapes[0], lambda i, w: (0, 0))] * (2 * count)
    else:
        shapes = [(count * BLK_D, GU + FF)]
        out_specs = [pl.BlockSpec((BLK_D, GU + FF), lambda i, w: (i, 0))]
    return pl.pallas_call(
        functools.partial(weight_kernel, count, halves),
        out_shape=[jax.ShapeDtypeStruct(s, BF) for s in shapes],
        grid_spec=pltpu.PrefetchScalarGridSpec(
            num_scalar_prefetch=1, grid=(count,), in_specs=specs, out_specs=out_specs
        ),
        compiler_params=params(),
        cost_estimate=cost(2 * 640 * BLK_D * (GU + FF) * count, 5 << 20),
        name="weight_blocks",
    )(which, tok, cot, grad, act, *extra)


def finish_kernel(own, plus_top, plus_bottom, minus_top, minus_bottom, gate_up, down):
    hop = BLK_D // 2
    for at, plus, minus in ((slice(0, hop), plus_top, minus_top), (slice(hop, BLK_D), plus_bottom, minus_bottom)):
        total = own[at, :].astype(F32) + plus[...].astype(F32) + minus[...].astype(F32)
        gate_up[at, :] = total[:, 0:GU].astype(BF)
        down[:, at] = total[:, GU:].T.astype(BF)


def finish(*parts):
    return pl.pallas_call(
        finish_kernel,
        out_shape=[jax.ShapeDtypeStruct((BLK_D, GU), BF), jax.ShapeDtypeStruct((FF, BLK_D), BF)],
        grid=(1,),
        in_specs=[whole(a) for a in parts],
        out_specs=[pl.BlockSpec((BLK_D, GU), lambda i: (0, 0)), pl.BlockSpec((FF, BLK_D), lambda i: (0, 0))],
        compiler_params=params(),
        cost_estimate=cost(1e6, 4 << 20),
        name="finish",
    )(*parts)


def shift(array, axis, size, by):
    return lax.ppermute(array, axis, [(i, (i + by) % size) for i in range(size)])


def per_device(tokens, cotangent, routes, slot_index, gate_probs, lengths, w_gate_up, w_down):
    x, z = lax.axis_index("x"), lax.axis_index("z")
    y, core = lax.axis_index("y"), lax.axis_index("core")
    position = jnp.stack([x, z]).astype(jnp.int32)
    gate_up, down = w_gate_up[0], w_down[0]
    routes, slots, gates = routes.T, slot_index.T, gate_probs.T

    own, sent = pack(position, tokens, cotangent, routes, slots, gates, lengths)
    up, dn = {0: own}, {0: own}
    half = NZ // 2
    results = []

    def exchange(rows):
        results.append([rows[0]] + [shift(rows[s], "x", NX, s) for s in range(1, NX)])

    up[1], dn[1] = shift(own, "z", NZ, 1), shift(own, "z", NZ, -1)
    exchange(sent)
    up[1], dn[1], results[0] = lax.optimization_barrier((up[1], dn[1], results[0]))
    for d in range(2, half):
        up[d] = shift(up[d - 1], "z", NZ, 1)
        dn[d] = shift(dn[d - 1], "z", NZ, -1)
    far_tok = shift(up[half - 1][0:TOK], "z", NZ, 1)
    far_cot = shift(dn[half - 1][TOK:], "z", NZ, -1)

    chunks = [((up[d], dn[d]), 2, False) for d in range(1, half)]
    chunks += [((far_tok, far_cot), 1, True)]
    blocks_of = (1,) + tuple(c[1] for c in chunks)
    for index, (inputs, blocks, split) in enumerate(chunks, start=1):
        if index >= 3:
            inputs, results[index - 2] = lax.optimization_barrier((inputs, results[index - 2]))
        exchange(select(position, inputs, blocks, split))
    arrays = [a for r in results for a in r]
    group, sent_back = expert(position, arrays, gate_up, down, blocks_of)
    width = sent_back.shape[1]
    got_back = lax.all_to_all(
        sent_back.reshape(NX * NZ, HEAD, width), ("x", "z"), split_axis=0, concat_axis=0, tiled=True
    )
    token_grad = combine(routes, slots, got_back.reshape(NX * NZ * HEAD, width))

    def blocks_at(steps, of_core):
        return jnp.stack([2 * ((y + s) % NY) + of_core for s in steps]).astype(jnp.int32)

    def add(a, b):
        return (a.astype(F32) + b.astype(F32)).astype(BF)

    early = shift(weight_blocks(blocks_at((2,), 1 - core), group)[0], "core", 2, 1)
    late = shift(weight_blocks(blocks_at((1, 3, 0), 1 - core), group)[0], "core", 2, 1)
    top, bottom = weight_blocks(blocks_at((2,), core), group, early, 0, halves=True)
    top, bottom = shift(top, "y", NY, 1), shift(bottom, "y", NY, -1)
    plus_top, plus_bottom, minus_top, minus_bottom = weight_blocks(
        blocks_at((1, 3), core), group, late, 0, halves=True
    )
    plus_bottom = shift(plus_bottom, "y", NY, 1)
    minus_top = shift(minus_top, "y", NY, -1)
    plus_top = shift(add(plus_top, top), "y", NY, 1)
    minus_bottom = shift(add(minus_bottom, bottom), "y", NY, -1)
    (mine,) = weight_blocks(blocks_at((0,), core), group, late, 2)
    grad_gate_up, grad_down = finish(mine, plus_top, plus_bottom, minus_top, minus_bottom)
    return token_grad, grad_gate_up[None], grad_down[None]


def solution(mesh):
    torus = Mesh(mesh.devices.reshape(NY, 2, NX, NZ), ("y", "core", "x", "z"))
    dp, ep = ("y", "core"), ("x", "z")
    return jax.shard_map(
        per_device,
        mesh=torus,
        in_specs=(P(dp + ep, None),) * 6 + (P(ep, None, None),) * 2,
        out_specs=(P(dp + ep, None), P(ep, dp, None), P(ep, None, dp)),
        check_vma=False,
    )
```

```python
import functools

import jax
import jax.numpy as jnp
from jax import lax
from jax.experimental import pallas as pl
from jax.experimental.pallas import tpu as pltpu
from jax.sharding import Mesh
from jax.sharding import PartitionSpec as P

TOP = 8
SEGS = 4
TOK = 64
CAP = 18
D = 2048
FF = 768
GU = 2 * FF
META = 128
NX = 4
NZ = 8
NY = 4
BLK_D = 256
BF = jnp.bfloat16
F32 = jnp.float32
SMEM = pl.BlockSpec(memory_space=pltpu.SMEM)

HEAD = 16


def params():
    return pltpu.CompilerParams(vmem_limit_bytes=56 * 1024 * 1024)


def whole(a):
    return pl.BlockSpec(a.shape, lambda i: (0,) * len(a.shape))


def pad8(n):
    return (n + 7) // 8 * 8


def layout(blocks):
    count = CAP * blocks
    rem = count % 8
    full = count - rem
    return full, rem, full + rem if 2 * rem <= 8 else full + 8


def slot_rows(blocks):
    return pad8(CAP * blocks)


def send_rows(blocks):
    full, rem, cot = layout(blocks)
    return 2 * full + (8 if cot < full + 8 else 16)


def cost(micros):
    return pl.CostEstimate(flops=int(micros * 1e9), bytes_accessed=int(micros * 3e6), transcendentals=0)


def pick(blocks, pos_ref, data, meta, out):
    width = 2 * TOK * blocks
    lane = lax.broadcasted_iota(jnp.int32, (1, width), 1)
    block = lane >> 7
    is_cot = (lane >> 6) & 1
    code = meta[0:TOP] * CAP + meta[TOP : 2 * TOP] + (1024 * is_cot + 2048 * block).astype(F32)
    value = meta[2 * TOP : 3 * TOP]
    rows, count = send_rows(blocks), CAP * blocks
    full, rem, cot = layout(blocks)
    row = lax.broadcasted_iota(jnp.int32, (rows, 1), 0)
    row_cot = (row >= cot).astype(jnp.int32)
    if cot < full + 8:
        item = jnp.where(row >= full + 8, row - full - 8, row - rem * row_cot)
        used = (row < full + 2 * rem) | (row >= full + 8)
    else:
        item = row - cot * row_cot
        used = item < count
    row_block = jnp.zeros_like(row)
    for i in range(1, blocks):
        row_block = row_block + (item >= i * CAP).astype(jnp.int32)
    slot = item - row_block * CAP
    picks = []
    for step in range(NX):
        row_code = (step * NZ + pos_ref[1]) * CAP + slot + 1024 * row_cot + 2048 * row_block
        row_code = jnp.where(used, row_code, -1).astype(F32)
        chosen = jnp.zeros((rows, width), F32)
        for k in range(TOP):
            chosen = chosen + jnp.where(code[k : k + 1] == row_code, value[k : k + 1], 0.0)
        picks.append(chosen)
    chosen = jnp.concatenate(picks, axis=0).astype(BF)
    out[...] = jnp.dot(chosen, data, preferred_element_type=F32).astype(BF)


def pack_kernel(len_ref, tok_ref, cot_ref, routes_ref, slots_ref, gate_ref, out_ref):
    position = lax.broadcasted_iota(jnp.int32, (1, TOK), 1)
    end = jnp.int32(0)
    picked = jnp.zeros((1, TOK), F32)
    for seg in range(SEGS):
        length = len_ref[0, seg]
        inside = (position >= end) & (position < end + length)
        picked = jnp.where(inside, length.astype(F32), picked)
        end = end + length
    weight = (TOK / SEGS) / picked
    scale = (weight * gate_ref[...]).astype(BF).astype(F32)
    routes = routes_ref[...].astype(F32)
    slots = slots_ref[...].astype(F32)
    ones = jnp.ones((TOP, TOK), F32)
    fill = jnp.zeros((META - 3 * TOP, TOK), F32)
    out_ref[0:TOK, 0:D] = tok_ref[...]
    out_ref[TOK : 2 * TOK, 0:D] = cot_ref[...]
    out_ref[0:TOK, D : D + META] = jnp.concatenate([routes, slots, ones, fill], axis=0).T.astype(BF)
    out_ref[TOK : 2 * TOK, D : D + META] = jnp.concatenate([routes, slots, scale, fill], axis=0).T.astype(BF)


def pack(tokens, cotangent, routes, slots, gates, lengths):
    return pl.pallas_call(
        pack_kernel,
        out_shape=jax.ShapeDtypeStruct((2 * TOK, D + META), BF),
        grid=(1,),
        in_specs=[SMEM] + [whole(a) for a in (tokens, cotangent, routes, slots, gates)],
        out_specs=pl.BlockSpec((2 * TOK, D + META), lambda i: (0, 0)),
        compiler_params=params(),
        cost_estimate=cost(1),
        name="pack",
    )(lengths, tokens, cotangent, routes, slots, gates)


def select_kernel(blocks, pos_ref, *refs):
    inputs, out = refs[:blocks], refs[blocks]
    data = jnp.concatenate([r[:, 0:D] for r in inputs], axis=0)
    meta = jnp.concatenate([r[:, D:].astype(F32).T for r in inputs], axis=1)
    pick(blocks, pos_ref, data, meta, out)


def select(position, inputs):
    blocks = len(inputs)
    rows = NX * send_rows(blocks)
    return pl.pallas_call(
        functools.partial(select_kernel, blocks),
        out_shape=jax.ShapeDtypeStruct((rows, D), BF),
        grid=(1,),
        in_specs=[SMEM] + [whole(a) for a in inputs],
        out_specs=pl.BlockSpec((rows, D), lambda i: (0, 0)),
        compiler_params=params(),
        cost_estimate=cost(40),
        name="select",
    )(position, *inputs)


def chunk_bases(blocks_of):
    bases, base = [], 0
    for blocks in blocks_of:
        bases.append(base)
        base += NX * slot_rows(blocks)
    return bases, base


TILE = 256


def gather_rows(blocks_of, arrays, copies, tok, cot):
    bases, _ = chunk_bases(blocks_of)
    for index, blocks in enumerate(blocks_of):
        copies[index].wait()
        full, rem, cot_at = layout(blocks)
        sent = send_rows(blocks)
        everything = arrays[index][...].astype(F32)
        sub = lax.broadcasted_iota(jnp.int32, (8, 1), 0)
        tok_parts, cot_parts = [], []
        for step in range(NX):
            rows = everything[step * sent : (step + 1) * sent]
            if cot_at < full + 8:
                mixed = rows[full : full + 8]
                tok_parts += [rows[0:full], jnp.where(sub < rem, mixed, 0.0)]
                cot_parts += [rows[full + 8 :], jnp.where(sub < rem, pltpu.roll(mixed, 8 - rem, 0), 0.0)]
            else:
                tok_parts.append(rows[0:cot_at])
                cot_parts.append(rows[cot_at:])
        at = pl.ds(bases[index], NX * slot_rows(blocks))
        tok[at, :] = jnp.concatenate(tok_parts, axis=0).astype(BF)
        cot[at, :] = jnp.concatenate(cot_parts, axis=0).astype(BF)


def return_order(members, pos_ref):
    blocks_of = [len(m) for m in members]
    bases, total = chunk_bases(blocks_of)
    main, devices = NX * NZ * HEAD, NX * NZ
    extra = CAP - HEAD
    row = lax.broadcasted_iota(jnp.int32, (main + devices * extra, 1), 0)
    late = row >= main
    rest = row - main
    device = jnp.where(late, rest >> 1, row >> 4)
    slot = jnp.where(late, HEAD + (rest & 1), row & (HEAD - 1))
    step = device >> 3
    away = ((device & (NZ - 1)) - pos_ref[1]) & (NZ - 1)
    place = jnp.full_like(row, -1)
    for base, distances in zip(bases, members):
        for i, distance in enumerate(distances):
            at = base + step * slot_rows(len(distances)) + i * CAP + slot
            place = jnp.where(away == distance % NZ, at, place)
    col = lax.broadcasted_iota(jnp.int32, (1, total), 1)
    return (col == place).astype(F32).astype(BF)


def expert_kernel(members, earlier, pos_ref, *refs):
    blocks_of = [len(m) for m in members]
    count = len(blocks_of)
    before = 1 if earlier else 0
    arrays, (gate_up_hbm, down_hbm) = refs[:count], refs[count : count + 2]
    rest = refs[count + 2 + before :]
    outs, held = rest[:5], rest[5 : 5 + count]
    gate_up, down, tok, cot, grad, act, back_ref, row_sems, in_sems, out_sems = rest[5 + count : 15 + count]
    copies = [pltpu.make_async_copy(a, h, row_sems.at[i]) for i, (a, h) in enumerate(zip(arrays, held))]
    for copy in copies:
        copy.start()
    loads = []
    for index, f in enumerate(range(0, FF, TILE)):
        loads.append([
            pltpu.make_async_copy(
                gate_up_hbm.at[:, pl.ds(f, TILE)], gate_up.at[:, pl.ds(f, TILE)], in_sems.at[3 * index]
            ),
            pltpu.make_async_copy(
                gate_up_hbm.at[:, pl.ds(FF + f, TILE)], gate_up.at[:, pl.ds(FF + f, TILE)], in_sems.at[3 * index + 1]
            ),
            pltpu.make_async_copy(
                down_hbm.at[pl.ds(f, TILE), :], down.at[pl.ds(f, TILE), :], in_sems.at[3 * index + 2]
            ),
        ])
    for group in loads:
        for copy in group:
            copy.start()
    if earlier:
        earlier_back, own_back, earlier_sem = rest[15 + count :]
        earlier_copy = pltpu.make_async_copy(refs[count + 2], earlier_back, earlier_sem.at[0])
        earlier_copy.start()
    stores = [pltpu.make_async_copy(v, o, out_sems.at[i]) for i, (v, o) in enumerate(zip((tok, cot, grad, act), outs))]
    gather_rows(blocks_of, held, copies, tok, cot)
    stores[0].start()
    stores[1].start()
    for index, f in enumerate(range(0, FF, TILE)):
        for copy in loads[index]:
            copy.wait()
        gate_pre = jnp.dot(tok[...], gate_up[:, f : f + TILE], preferred_element_type=F32)
        up_pre = jnp.dot(tok[...], gate_up[:, FF + f : FF + f + TILE], preferred_element_type=F32)
        back = lax.dot_general(
            cot[...], down[f : f + TILE, :], (((1,), (1,)), ((), ())), preferred_element_type=F32
        )
        sigmoid = jax.nn.sigmoid(gate_pre)
        silu = gate_pre * sigmoid
        act[:, f : f + TILE] = (silu * up_pre).astype(BF)
        gate_grad = back * up_pre * sigmoid * (1.0 + gate_pre * (1.0 - sigmoid))
        grad[:, f : f + TILE] = gate_grad.astype(BF)
        grad[:, FF + f : FF + f + TILE] = (back * silu).astype(BF)
    stores[2].start()
    stores[3].start()

    tile = 512

    def store_back(at, size):
        cols = pl.ds(at, size)
        stores.append(pltpu.make_async_copy(back_ref.at[:, cols], outs[4].at[:, cols], out_sems.at[4 + at // tile]))
        stores[-1].start()

    def row_grads(d):
        return lax.dot_general(
            grad[...], gate_up[d : d + tile, :], (((1,), (1,)), ((), ())), preferred_element_type=F32
        ).astype(BF)

    if not earlier:
        for d in range(0, D, tile):
            back_ref[:, d : d + tile] = row_grads(d)
            store_back(d, tile)
    else:
        main, lates_count = NX * NZ * HEAD, NX * NZ * (CAP - HEAD)
        order = return_order(members, pos_ref)
        earlier_order = return_order(earlier, pos_ref)
        earlier_copy.wait()
        lates = []
        for d in range(0, D, tile):
            own_back[:, d : d + tile] = row_grads(d)
            part = jnp.dot(order, own_back[:, d : d + tile], preferred_element_type=F32)
            part = part + jnp.dot(earlier_order, earlier_back[:, d : d + tile], preferred_element_type=F32)
            part = part.astype(BF)
            back_ref[:, d : d + tile] = part[0:main]
            store_back(d, tile)
            lates.append(part[main:])
        width = D * (CAP - HEAD) // HEAD
        pieces = [p[:, c : c + width] for p in lates for c in range(0, tile, width)]
        stacked = jnp.concatenate(pieces, axis=0)
        out_row = lax.broadcasted_iota(jnp.int32, (main, 1), 0)
        within = out_row & (HEAD - 1)
        source = (within & 7) * lates_count + (out_row >> 4) * (CAP - HEAD) + (within >> 3)
        in_row = lax.broadcasted_iota(jnp.int32, (1, len(pieces) * lates_count), 1)
        fold = (in_row == source).astype(F32).astype(BF)
        back_ref[:, D:] = jnp.dot(fold, stacked, preferred_element_type=F32).astype(BF)
        store_back(D, width)
    for store in stores:
        store.wait()


def expert(position, arrays, gate_up, down, members, earlier=(), earlier_back=None):
    _, total = chunk_bases([len(m) for m in members])
    back = (NX * NZ * HEAD, D + D * (CAP - HEAD) // HEAD) if earlier else (total, D)
    shapes = [(total, D), (total, D), (total, GU), (total, FF), back]
    any_spec = pl.BlockSpec(memory_space=pl.ANY)
    operands = [*arrays, gate_up, down] + ([earlier_back] if earlier else [])
    scratch = [pltpu.VMEM(a.shape, BF) for a in arrays]
    scratch += [pltpu.VMEM(s, BF) for s in [(D, GU), (FF, D)] + shapes]
    scratch += [pltpu.SemaphoreType.DMA((n,)) for n in (len(arrays), 3 * (FF // TILE), 9)]
    if earlier:
        scratch += [pltpu.VMEM(earlier_back.shape, BF), pltpu.VMEM((total, D), BF), pltpu.SemaphoreType.DMA((1,))]
    outs = pl.pallas_call(
        functools.partial(expert_kernel, members, earlier),
        out_shape=[jax.ShapeDtypeStruct(s, BF) for s in shapes],
        grid=(1,),
        in_specs=[SMEM] + [any_spec] * len(operands),
        out_specs=[any_spec] * len(shapes),
        scratch_shapes=scratch,
        compiler_params=params(),
        cost_estimate=cost(1 if earlier else 40),
        name="expert",
    )(position, *operands)
    return outs[:4], outs[4]


def combine_kernel(routes_ref, slots_ref, rows_ref, out_ref):
    code = (routes_ref[...].astype(F32) * CAP + slots_ref[...].astype(F32)).T
    main = NX * NZ * HEAD
    col = lax.broadcasted_iota(jnp.int32, (1, main), 1)
    device, within = col >> 4, col & (HEAD - 1)
    head_code = (device * CAP + within).astype(F32)
    late_code = (device * CAP + HEAD + (within >> 3)).astype(F32)
    head = jnp.zeros((TOK, main), F32)
    late = jnp.zeros((TOK, main), F32)
    for k in range(TOP):
        head = head + (code[:, k : k + 1] == head_code).astype(F32)
        late = late + (code[:, k : k + 1] == late_code).astype(F32)
    folds = HEAD // (CAP - HEAD)
    lates = jnp.concatenate([jnp.where((within & 7) == j, late, 0.0) for j in range(folds)], axis=0)
    tail = jnp.dot(lates.astype(BF), rows_ref[:, D:], preferred_element_type=F32)
    total = jnp.dot(head.astype(BF), rows_ref[:, 0:D], preferred_element_type=F32)
    width = D // folds
    for j in range(folds):
        at = slice(j * width, (j + 1) * width)
        out_ref[:, at] = (total[:, at] + tail[j * TOK : (j + 1) * TOK]).astype(BF)


def combine(routes, slots, rows):
    return pl.pallas_call(
        combine_kernel,
        out_shape=jax.ShapeDtypeStruct((TOK, D), BF),
        grid=(1,),
        in_specs=[whole(a) for a in (routes, slots, rows)],
        out_specs=pl.BlockSpec((TOK, D), lambda i: (0, 0)),
        compiler_params=params(),
        cost_estimate=cost(20),
        name="combine",
    )(routes, slots, rows)


def weight_kernel(groups, count, halves, which_ref, *refs):
    rest = refs[4 * groups :]
    extra, outs = (rest[:1], rest[1:]) if len(rest) > (2 * count if halves else 1) else ((), rest)
    first = (((0,), (0,)), ((), ()))
    rows = BLK_D // 2
    for cols, left, right in ((slice(0, GU), 0, 2), (slice(GU, GU + FF), 1, 3)):
        total = extra[0][:, cols].astype(F32) if extra else None
        for g in range(groups):
            part = lax.dot_general(
                refs[4 * g + left][...], refs[4 * g + right][...], first, preferred_element_type=F32
            )
            total = part if total is None else total + part
        total = total.astype(BF)
        if not halves:
            outs[0][:, cols] = total
            continue
        for i in range(count):

            @pl.when(pl.program_id(0) == i)
            def _():
                outs[2 * i][:, cols] = total[0:rows]
                outs[2 * i + 1][:, cols] = total[rows:]


def weight_blocks(which, groups, received=None, block=0, halves=False):
    count = which.shape[0]

    def cut(a):
        return pl.BlockSpec((a.shape[0], BLK_D), lambda i, w: (0, w[i]))

    def full(a):
        return pl.BlockSpec(a.shape, lambda i, w: (0, 0))

    specs = [spec for g in groups for spec in (cut(g[0]), cut(g[1]), full(g[2]), full(g[3]))]
    extra = []
    if received is not None:
        specs.append(pl.BlockSpec((BLK_D, GU + FF), lambda i, w: (block + i, 0)))
        extra.append(received)
    if halves:
        shapes = [(BLK_D // 2, GU + FF)] * (2 * count)
        out_specs = [pl.BlockSpec(shapes[0], lambda i, w: (0, 0))] * (2 * count)
    else:
        shapes = [(count * BLK_D, GU + FF)]
        out_specs = [pl.BlockSpec((BLK_D, GU + FF), lambda i, w: (i, 0))]
    return pl.pallas_call(
        functools.partial(weight_kernel, len(groups), count, halves),
        out_shape=[jax.ShapeDtypeStruct(s, BF) for s in shapes],
        grid_spec=pltpu.PrefetchScalarGridSpec(
            num_scalar_prefetch=1, grid=(count,), in_specs=specs, out_specs=out_specs
        ),
        compiler_params=params(),
        cost_estimate=cost(20 if count == 3 else 1),
        name="weight_blocks",
    )(which, *(a for g in groups for a in g), *extra)


def finish_kernel(own_top, own_bottom, plus_top, plus_bottom, minus_top, minus_bottom, gate_up, down):
    hop = BLK_D // 2
    tops, bottoms = (own_top, plus_top, minus_top), (own_bottom, plus_bottom, minus_bottom)
    for at, (own, plus, minus) in ((slice(0, hop), tops), (slice(hop, BLK_D), bottoms)):
        total = own[...].astype(F32) + plus[...].astype(F32) + minus[...].astype(F32)
        gate_up[at, :] = total[:, 0:GU].astype(BF)
        down[:, at] = total[:, GU:].T.astype(BF)


def finish(*parts):
    return pl.pallas_call(
        finish_kernel,
        out_shape=[jax.ShapeDtypeStruct((BLK_D, GU), BF), jax.ShapeDtypeStruct((FF, BLK_D), BF)],
        grid=(1,),
        in_specs=[whole(a) for a in parts],
        out_specs=[pl.BlockSpec((BLK_D, GU), lambda i: (0, 0)), pl.BlockSpec((FF, BLK_D), lambda i: (0, 0))],
        compiler_params=params(),
        cost_estimate=cost(1),
        name="finish",
    )(*parts)


def shift(array, axis, size, by):
    return lax.ppermute(array, axis, [(i, (i + by) % size) for i in range(size)])


def per_device(tokens, cotangent, routes, slot_index, gate_probs, lengths, w_gate_up, w_down):
    x, z = lax.axis_index("x"), lax.axis_index("z")
    y, core = lax.axis_index("y"), lax.axis_index("core")
    position = jnp.stack([x, z]).astype(jnp.int32)
    gate_up, down = w_gate_up[0], w_down[0]
    routes, slots, gates = routes.T, slot_index.T, gate_probs.T

    own = pack(tokens, cotangent, routes, slots, gates, lengths)

    def exchange(rows):
        return lax.all_to_all(rows, "x", split_axis=0, concat_axis=0, tiled=True)

    half = NZ // 2
    up1, dn1 = shift(own, "z", NZ, 1), shift(own, "z", NZ, -1)
    own, up1, dn1 = lax.optimization_barrier((own, up1, dn1))
    far = shift(own, "z", NZ, half)
    sent_near = select(position, (own, up1, dn1))
    near = exchange(sent_near)
    up2, dn2 = shift(up1, "z", NZ, 1), shift(dn1, "z", NZ, -1)
    up2, dn2, sent_near = lax.optimization_barrier((up2, dn2, sent_near))
    up3, dn3 = shift(up2, "z", NZ, 1), shift(dn2, "z", NZ, -1)
    middle = exchange(select(position, (up2, dn2)))
    last = exchange(select(position, (up3, dn3, far)))

    early_members = ((0, -1, 1), (-2, 2))
    late_members = ((-3, 3, half),)
    group_a, back_a = expert(position, [near, middle], gate_up, down, early_members)
    group_b, sent_back = expert(position, [last], gate_up, down, late_members, early_members, back_a)
    group = (group_a, group_b)
    width = sent_back.shape[1]
    got_back = lax.all_to_all(
        sent_back.reshape(NX * NZ, HEAD, width), ("x", "z"), split_axis=0, concat_axis=0, tiled=True
    )

    def blocks_at(steps, of_core):
        return jnp.stack([2 * ((y + s) % NY) + of_core for s in steps]).astype(jnp.int32)

    def add(a, b):
        return (a.astype(F32) + b.astype(F32)).astype(BF)

    received = shift(weight_blocks(blocks_at((2, 1, 3, 0), 1 - core), group)[0], "core", 2, 1)
    top, bottom = weight_blocks(blocks_at((2,), core), group, received, 0, halves=True)
    top, bottom, nearer = lax.optimization_barrier((top, bottom, blocks_at((1, 3, 0), core)))
    top, bottom = shift(top, "y", NY, 1), shift(bottom, "y", NY, -1)
    plus_top, plus_bottom, minus_top, minus_bottom, own_top, own_bottom = weight_blocks(
        nearer, group, received, 1, halves=True
    )
    plus_bottom = shift(plus_bottom, "y", NY, 1)
    minus_top = shift(minus_top, "y", NY, -1)
    top, bottom = lax.optimization_barrier((top, bottom))
    plus_top, minus_bottom = add(plus_top, top), add(minus_bottom, bottom)
    plus_top, minus_bottom = lax.optimization_barrier((plus_top, minus_bottom))
    got_back = lax.optimization_barrier((got_back, plus_top, minus_bottom))[0]
    plus_top = shift(plus_top, "y", NY, 1)
    minus_bottom = shift(minus_bottom, "y", NY, -1)
    token_grad = combine(routes, slots, got_back.reshape(NX * NZ * HEAD, width))
    grad_gate_up, grad_down = finish(own_top, own_bottom, plus_top, plus_bottom, minus_top, minus_bottom)
    return token_grad, grad_gate_up[None], grad_down[None]


def solution(mesh):
    torus = Mesh(mesh.devices.reshape(NY, 2, NX, NZ), ("y", "core", "x", "z"))
    dp, ep = ("y", "core"), ("x", "z")
    return jax.shard_map(
        per_device,
        mesh=torus,
        in_specs=(P(dp + ep, None),) * 6 + (P(ep, None, None),) * 2,
        out_specs=(P(dp + ep, None), P(ep, dp, None), P(ep, None, dp)),
        check_vma=False,
    )
```

```python
import functools

import jax
import jax.numpy as jnp
from jax import lax
from jax.experimental import pallas as pl
from jax.experimental.pallas import tpu as pltpu
from jax.sharding import Mesh
from jax.sharding import PartitionSpec as P

TOP = 8
SEGS = 4
TOK = 64
CAP = 18
D = 2048
FF = 768
GU = 2 * FF
META = 128
NX = 4
NZ = 8
NY = 4
BLK_D = 256
BF = jnp.bfloat16
F32 = jnp.float32
SMEM = pl.BlockSpec(memory_space=pltpu.SMEM)

HEAD = 16


def params():
    return pltpu.CompilerParams(vmem_limit_bytes=56 * 1024 * 1024)


def whole(a):
    return pl.BlockSpec(a.shape, lambda i: (0,) * len(a.shape))


def pad8(n):
    return (n + 7) // 8 * 8


def layout(blocks):
    count = CAP * blocks
    rem = count % 8
    full = count - rem
    return full, rem, full + rem if 2 * rem <= 8 else full + 8


def slot_rows(blocks):
    return pad8(CAP * blocks)


def send_rows(blocks):
    full, rem, cot = layout(blocks)
    return 2 * full + (8 if cot < full + 8 else 16)


def cost(micros):
    return pl.CostEstimate(flops=int(micros * 1e9), bytes_accessed=int(micros * 3e6), transcendentals=0)


def pick(blocks, pos_ref, data, meta, outs):
    width = 2 * TOK * blocks
    lane = lax.broadcasted_iota(jnp.int32, (1, width), 1)
    block = lane >> 7
    is_cot = (lane >> 6) & 1
    code = meta[0:TOP] * CAP + meta[TOP : 2 * TOP] + (1024 * is_cot + 2048 * block).astype(F32)
    value = meta[2 * TOP : 3 * TOP]
    rows, count = send_rows(blocks), CAP * blocks
    full, rem, cot = layout(blocks)
    row = lax.broadcasted_iota(jnp.int32, (rows, 1), 0)
    row_cot = (row >= cot).astype(jnp.int32)
    if cot < full + 8:
        item = jnp.where(row >= full + 8, row - full - 8, row - rem * row_cot)
        used = (row < full + 2 * rem) | (row >= full + 8)
    else:
        item = row - cot * row_cot
        used = item < count
    row_block = jnp.zeros_like(row)
    for i in range(1, blocks):
        row_block = row_block + (item >= i * CAP).astype(jnp.int32)
    slot = item - row_block * CAP
    picks = []
    for step in range(NX):
        to = (pos_ref[0] + step) & (NX - 1) if len(outs) == NX else step
        row_code = (to * NZ + pos_ref[1]) * CAP + slot + 1024 * row_cot + 2048 * row_block
        row_code = jnp.where(used, row_code, -1).astype(F32)
        chosen = jnp.zeros((rows, width), F32)
        for k in range(TOP):
            chosen = chosen + jnp.where(code[k : k + 1] == row_code, value[k : k + 1], 0.0)
        picks.append(chosen)
    if len(outs) == NX:
        for chosen, out in zip(picks, outs):
            out[...] = jnp.dot(chosen.astype(BF), data, preferred_element_type=F32).astype(BF)
    else:
        chosen = jnp.concatenate(picks, axis=0).astype(BF)
        outs[0][...] = jnp.dot(chosen, data, preferred_element_type=F32).astype(BF)


def pack_kernel(len_ref, tok_ref, cot_ref, routes_ref, slots_ref, gate_ref, out_ref):
    position = lax.broadcasted_iota(jnp.int32, (1, TOK), 1)
    end = jnp.int32(0)
    picked = jnp.zeros((1, TOK), F32)
    for seg in range(SEGS):
        length = len_ref[0, seg]
        inside = (position >= end) & (position < end + length)
        picked = jnp.where(inside, length.astype(F32), picked)
        end = end + length
    weight = (TOK / SEGS) / picked
    scale = (weight * gate_ref[...]).astype(BF).astype(F32)
    routes = routes_ref[...].astype(F32)
    slots = slots_ref[...].astype(F32)
    ones = jnp.ones((TOP, TOK), F32)
    fill = jnp.zeros((META - 3 * TOP, TOK), F32)
    out_ref[0:TOK, 0:D] = tok_ref[...]
    out_ref[TOK : 2 * TOK, 0:D] = cot_ref[...]
    out_ref[0:TOK, D : D + META] = jnp.concatenate([routes, slots, ones, fill], axis=0).T.astype(BF)
    out_ref[TOK : 2 * TOK, D : D + META] = jnp.concatenate([routes, slots, scale, fill], axis=0).T.astype(BF)


def pack(tokens, cotangent, routes, slots, gates, lengths):
    return pl.pallas_call(
        pack_kernel,
        out_shape=jax.ShapeDtypeStruct((2 * TOK, D + META), BF),
        grid=(1,),
        in_specs=[SMEM] + [whole(a) for a in (tokens, cotangent, routes, slots, gates)],
        out_specs=pl.BlockSpec((2 * TOK, D + META), lambda i: (0, 0)),
        compiler_params=params(),
        cost_estimate=cost(1),
        name="pack",
    )(lengths, tokens, cotangent, routes, slots, gates)


def select_kernel(blocks, count, pos_ref, *refs):
    inputs, outs = refs[:count], refs[count:]
    data = jnp.concatenate([r[:, 0:D] for r in inputs], axis=0)
    if count > blocks:
        metas = [jnp.concatenate([r[:, D:] for r in inputs], axis=0)]
    else:
        metas = [r[:, D:] for r in inputs]
    meta = jnp.concatenate([m.astype(F32).T for m in metas], axis=1)
    pick(blocks, pos_ref, data, meta, outs)


def select(position, inputs, blocks, apart):
    rows = send_rows(blocks) * (1 if apart else NX)
    outs = pl.pallas_call(
        functools.partial(select_kernel, blocks, len(inputs)),
        out_shape=[jax.ShapeDtypeStruct((rows, D), BF)] * (NX if apart else 1),
        grid=(1,),
        in_specs=[SMEM] + [whole(a) for a in inputs],
        out_specs=[pl.BlockSpec((rows, D), lambda i: (0, 0))] * (NX if apart else 1),
        compiler_params=params(),
        cost_estimate=cost(40),
        name="select",
    )(position, *inputs)
    return outs if apart else outs[0]


def chunk_bases(blocks_of):
    bases, base = [], 0
    for blocks in blocks_of:
        bases.append(base)
        base += NX * slot_rows(blocks)
    return bases, base


TILE = 256


def gather_rows(blocks_of, arrays, copies, tok, cot):
    bases, _ = chunk_bases(blocks_of)
    for index, blocks in enumerate(blocks_of):
        for copy in copies[index]:
            copy.wait()
        full, rem, cot_at = layout(blocks)
        sent = send_rows(blocks)
        sub = lax.broadcasted_iota(jnp.int32, (8, 1), 0)
        tok_parts, cot_parts = [], []
        for step in range(NX):
            if len(arrays[index]) == NX:
                rows = arrays[index][step][...].astype(F32)
            else:
                if step == 0:
                    everything = arrays[index][0][...].astype(F32)
                rows = everything[step * sent : (step + 1) * sent]
            if cot_at < full + 8:
                mixed = rows[full : full + 8]
                tok_parts += [rows[0:full], jnp.where(sub < rem, mixed, 0.0)]
                cot_parts += [rows[full + 8 :], jnp.where(sub < rem, pltpu.roll(mixed, 8 - rem, 0), 0.0)]
            else:
                tok_parts.append(rows[0:cot_at])
                cot_parts.append(rows[cot_at:])
        at = pl.ds(bases[index], NX * slot_rows(blocks))
        tok[at, :] = jnp.concatenate(tok_parts, axis=0).astype(BF)
        cot[at, :] = jnp.concatenate(cot_parts, axis=0).astype(BF)


def return_order(members, apart, pos_ref):
    blocks_of = [len(m) for m in members]
    bases, total = chunk_bases(blocks_of)
    main, devices = NX * NZ * HEAD, NX * NZ
    extra = CAP - HEAD
    row = lax.broadcasted_iota(jnp.int32, (main + devices * extra, 1), 0)
    late = row >= main
    rest = row - main
    device = jnp.where(late, rest >> 1, row >> 4)
    slot = jnp.where(late, HEAD + (rest & 1), row & (HEAD - 1))
    place_x = device >> 3
    away_x = (pos_ref[0] - place_x) & (NX - 1)
    away = ((device & (NZ - 1)) - pos_ref[1]) & (NZ - 1)
    place = jnp.full_like(row, -1)
    for base, distances, is_apart in zip(bases, members, apart):
        step = away_x if is_apart else place_x
        for i, distance in enumerate(distances):
            at = base + step * slot_rows(len(distances)) + i * CAP + slot
            place = jnp.where(away == distance % NZ, at, place)
    col = lax.broadcasted_iota(jnp.int32, (1, total), 1)
    return (col == place).astype(F32).astype(BF)


def expert_kernel(members, apart, earlier, earlier_apart, pos_ref, *refs):
    blocks_of = [len(m) for m in members]
    sizes = [NX if a else 1 for a in apart]
    count = sum(sizes)
    arrays, (gate_up_in, down_in) = refs[:count], refs[count : count + 2]
    rest = refs[count + 2 + (1 if earlier else 0) :]
    outs, rest = rest[:5], rest[5:]
    (gate_up, down), rest = rest[:2], rest[2:]
    held, rest = rest[:count], rest[count:]
    tok, cot, grad, act, back_ref, row_sems, in_sems, out_sems = rest[:8]
    copies = [pltpu.make_async_copy(a, h, row_sems.at[i]) for i, (a, h) in enumerate(zip(arrays, held))]
    for copy in copies:
        copy.start()
    starts = [sum(sizes[:i]) for i in range(len(sizes))]
    held = [held[i : i + n] for i, n in zip(starts, sizes)]
    copies = [copies[i : i + n] for i, n in zip(starts, sizes)]
    loads = []
    for index, f in enumerate(range(0, FF, TILE)):
        loads.append([
            pltpu.make_async_copy(
                gate_up_in.at[:, pl.ds(f, TILE)], gate_up.at[:, pl.ds(f, TILE)], in_sems.at[3 * index]
            ),
            pltpu.make_async_copy(
                gate_up_in.at[:, pl.ds(FF + f, TILE)], gate_up.at[:, pl.ds(FF + f, TILE)], in_sems.at[3 * index + 1]
            ),
            pltpu.make_async_copy(
                down_in.at[pl.ds(f, TILE), :], down.at[pl.ds(f, TILE), :], in_sems.at[3 * index + 2]
            ),
        ])
    for group in loads:
        for copy in group:
            copy.start()
    if earlier:
        earlier_back, own_back, earlier_sem = rest[8:]
        earlier_copy = pltpu.make_async_copy(refs[count + 2], earlier_back, earlier_sem.at[0])
        earlier_copy.start()
    stores = [pltpu.make_async_copy(v, o, out_sems.at[i]) for i, (v, o) in enumerate(zip((tok, cot, grad, act), outs))]
    gather_rows(blocks_of, held, copies, tok, cot)
    stores[0].start()
    stores[1].start()
    for index, f in enumerate(range(0, FF, TILE)):
        for copy in loads[index]:
            copy.wait()
        gate_pre = jnp.dot(tok[...], gate_up[:, f : f + TILE], preferred_element_type=F32)
        up_pre = jnp.dot(tok[...], gate_up[:, FF + f : FF + f + TILE], preferred_element_type=F32)
        back = lax.dot_general(
            cot[...], down[f : f + TILE, :], (((1,), (1,)), ((), ())), preferred_element_type=F32
        )
        sigmoid = jax.nn.sigmoid(gate_pre)
        silu = gate_pre * sigmoid
        act[:, f : f + TILE] = (silu * up_pre).astype(BF)
        gate_grad = back * up_pre * sigmoid * (1.0 + gate_pre * (1.0 - sigmoid))
        grad[:, f : f + TILE] = gate_grad.astype(BF)
        grad[:, FF + f : FF + f + TILE] = (back * silu).astype(BF)
    stores[2].start()
    stores[3].start()

    tile = 512

    def store_back(at, size):
        cols = pl.ds(at, size)
        stores.append(pltpu.make_async_copy(back_ref.at[:, cols], outs[4].at[:, cols], out_sems.at[4 + at // tile]))
        stores[-1].start()

    def row_grads(d):
        return lax.dot_general(
            grad[...], gate_up[d : d + tile, :], (((1,), (1,)), ((), ())), preferred_element_type=F32
        ).astype(BF)

    if not earlier:
        for d in range(0, D, tile):
            back_ref[:, d : d + tile] = row_grads(d)
            store_back(d, tile)
    else:
        main, lates_count = NX * NZ * HEAD, NX * NZ * (CAP - HEAD)
        order = return_order(members, apart, pos_ref)
        earlier_order = return_order(earlier, earlier_apart, pos_ref)
        earlier_copy.wait()
        lates = []
        for d in range(0, D, tile):
            own_back[:, d : d + tile] = row_grads(d)
            part = jnp.dot(order, own_back[:, d : d + tile], preferred_element_type=F32)
            part = part + jnp.dot(earlier_order, earlier_back[:, d : d + tile], preferred_element_type=F32)
            part = part.astype(BF)
            back_ref[:, d : d + tile] = part[0:main]
            store_back(d, tile)
            lates.append(part[main:])
        width = D * (CAP - HEAD) // HEAD
        pieces = [p[:, c : c + width] for p in lates for c in range(0, tile, width)]
        stacked = jnp.concatenate(pieces, axis=0)
        out_row = lax.broadcasted_iota(jnp.int32, (main, 1), 0)
        within = out_row & (HEAD - 1)
        source = (within & 7) * lates_count + (out_row >> 4) * (CAP - HEAD) + (within >> 3)
        in_row = lax.broadcasted_iota(jnp.int32, (1, len(pieces) * lates_count), 1)
        fold = (in_row == source).astype(F32).astype(BF)
        back_ref[:, D:] = jnp.dot(fold, stacked, preferred_element_type=F32).astype(BF)
        store_back(D, width)
    for store in stores:
        store.wait()


def expert(position, arrays, gate_up, down, members, apart, earlier=(), earlier_apart=(), earlier_back=None):
    _, total = chunk_bases([len(m) for m in members])
    back = (NX * NZ * HEAD, D + D * (CAP - HEAD) // HEAD) if earlier else (total, D)
    shapes = [(total, D), (total, D), (total, GU), (total, FF), back]
    any_spec = pl.BlockSpec(memory_space=pl.ANY)
    operands = [*arrays, gate_up, down] + ([earlier_back] if earlier else [])
    scratch = [pltpu.VMEM(s, BF) for s in [(D, GU), (FF, D)] + [a.shape for a in arrays] + shapes]
    scratch += [pltpu.SemaphoreType.DMA((n,)) for n in (len(arrays), 3 * (FF // TILE), 9)]
    if earlier:
        scratch += [pltpu.VMEM(earlier_back.shape, BF), pltpu.VMEM((total, D), BF), pltpu.SemaphoreType.DMA((1,))]
    outs = pl.pallas_call(
        functools.partial(expert_kernel, members, apart, earlier, earlier_apart),
        out_shape=[jax.ShapeDtypeStruct(s, BF) for s in shapes],
        grid=(1,),
        in_specs=[SMEM] + [any_spec] * len(operands),
        out_specs=[any_spec] * len(shapes),
        scratch_shapes=scratch,
        compiler_params=params(),
        cost_estimate=cost(1 if earlier else 5),
        name="expert",
    )(position, *operands)
    return outs[:4], outs[4]


def combine_kernel(routes_ref, slots_ref, rows_ref, out_ref):
    code = (routes_ref[...].astype(F32) * CAP + slots_ref[...].astype(F32)).T
    main = NX * NZ * HEAD
    col = lax.broadcasted_iota(jnp.int32, (1, main), 1)
    device, within = col >> 4, col & (HEAD - 1)
    head_code = (device * CAP + within).astype(F32)
    late_code = (device * CAP + HEAD + (within >> 3)).astype(F32)
    head = jnp.zeros((TOK, main), F32)
    late = jnp.zeros((TOK, main), F32)
    for k in range(TOP):
        head = head + (code[:, k : k + 1] == head_code).astype(F32)
        late = late + (code[:, k : k + 1] == late_code).astype(F32)
    folds = HEAD // (CAP - HEAD)
    lates = jnp.concatenate([jnp.where((within & 7) == j, late, 0.0) for j in range(folds)], axis=0)
    tail = jnp.dot(lates.astype(BF), rows_ref[:, D:], preferred_element_type=F32)
    total = jnp.dot(head.astype(BF), rows_ref[:, 0:D], preferred_element_type=F32)
    width = D // folds
    for j in range(folds):
        at = slice(j * width, (j + 1) * width)
        out_ref[:, at] = (total[:, at] + tail[j * TOK : (j + 1) * TOK]).astype(BF)


def combine(routes, slots, rows):
    return pl.pallas_call(
        combine_kernel,
        out_shape=jax.ShapeDtypeStruct((TOK, D), BF),
        grid=(1,),
        in_specs=[whole(a) for a in (routes, slots, rows)],
        out_specs=pl.BlockSpec((TOK, D), lambda i: (0, 0)),
        compiler_params=params(),
        cost_estimate=cost(20),
        name="combine",
    )(routes, slots, rows)


def weight_kernel(groups, count, halves, which_ref, *refs):
    rest = refs[4 * groups :]
    extra, outs = (rest[:1], rest[1:]) if len(rest) > (2 * count if halves else 1) else ((), rest)
    first = (((0,), (0,)), ((), ()))
    rows = BLK_D // 2
    for cols, left, right in ((slice(0, GU), 0, 2), (slice(GU, GU + FF), 1, 3)):
        total = extra[0][:, cols].astype(F32) if extra else None
        for g in range(groups):
            part = lax.dot_general(
                refs[4 * g + left][...], refs[4 * g + right][...], first, preferred_element_type=F32
            )
            total = part if total is None else total + part
        total = total.astype(BF)
        if not halves:
            outs[0][:, cols] = total
            continue
        for i in range(count):

            @pl.when(pl.program_id(0) == i)
            def _():
                outs[2 * i][:, cols] = total[0:rows]
                outs[2 * i + 1][:, cols] = total[rows:]


def weight_blocks(which, groups, received=None, block=0, halves=False):
    count = which.shape[0]

    def cut(a):
        return pl.BlockSpec((a.shape[0], BLK_D), lambda i, w: (0, w[i]))

    def full(a):
        return pl.BlockSpec(a.shape, lambda i, w: (0, 0))

    specs = [spec for g in groups for spec in (cut(g[0]), cut(g[1]), full(g[2]), full(g[3]))]
    extra = []
    if received is not None:
        specs.append(pl.BlockSpec((BLK_D, GU + FF), lambda i, w: (block + i, 0)))
        extra.append(received)
    if halves:
        shapes = [(BLK_D // 2, GU + FF)] * (2 * count)
        out_specs = [pl.BlockSpec(shapes[0], lambda i, w: (0, 0))] * (2 * count)
    else:
        shapes = [(count * BLK_D, GU + FF)]
        out_specs = [pl.BlockSpec((BLK_D, GU + FF), lambda i, w: (i, 0))]
    return pl.pallas_call(
        functools.partial(weight_kernel, len(groups), count, halves),
        out_shape=[jax.ShapeDtypeStruct(s, BF) for s in shapes],
        grid_spec=pltpu.PrefetchScalarGridSpec(
            num_scalar_prefetch=1, grid=(count,), in_specs=specs, out_specs=out_specs
        ),
        compiler_params=params(),
        cost_estimate=cost(3 if count == 3 else 1),
        name="weight_blocks",
    )(which, *(a for g in groups for a in g), *extra)


def finish_kernel(own_top, own_bottom, plus_top, plus_bottom, minus_top, minus_bottom, gate_up, down):
    hop = BLK_D // 2
    tops, bottoms = (own_top, plus_top, minus_top), (own_bottom, plus_bottom, minus_bottom)
    for at, (own, plus, minus) in ((slice(0, hop), tops), (slice(hop, BLK_D), bottoms)):
        total = own[...].astype(F32) + plus[...].astype(F32) + minus[...].astype(F32)
        gate_up[at, :] = total[:, 0:GU].astype(BF)
        down[:, at] = total[:, GU:].T.astype(BF)


def finish(*parts):
    return pl.pallas_call(
        finish_kernel,
        out_shape=[jax.ShapeDtypeStruct((BLK_D, GU), BF), jax.ShapeDtypeStruct((FF, BLK_D), BF)],
        grid=(1,),
        in_specs=[whole(a) for a in parts],
        out_specs=[pl.BlockSpec((BLK_D, GU), lambda i: (0, 0)), pl.BlockSpec((FF, BLK_D), lambda i: (0, 0))],
        compiler_params=params(),
        cost_estimate=cost(1),
        name="finish",
    )(*parts)


def shift(array, axis, size, by):
    return lax.ppermute(array, axis, [(i, (i + by) % size) for i in range(size)])


def per_device(tokens, cotangent, routes, slot_index, gate_probs, lengths, w_gate_up, w_down):
    x, z = lax.axis_index("x"), lax.axis_index("z")
    y, core = lax.axis_index("y"), lax.axis_index("core")
    position = jnp.stack([x, z]).astype(jnp.int32)
    gate_up, down = w_gate_up[0], w_down[0]
    routes, slots, gates = routes.T, slot_index.T, gate_probs.T

    own = pack(tokens, cotangent, routes, slots, gates, lengths)

    def exchange(rows):
        return [lax.all_to_all(rows, "x", split_axis=0, concat_axis=0, tiled=True)]

    def exchange_apart(rows):
        return [rows[0]] + [shift(rows[s], "x", NX, s) for s in range(1, NX)]

    half = NZ // 2
    up1, dn1 = shift(own, "z", NZ, 1), shift(own, "z", NZ, -1)
    sent_near = select(position, (own, up1, dn1), 3, True)
    near = exchange_apart(sent_near)
    up2, dn2 = shift(up1, "z", NZ, 1), shift(dn1, "z", NZ, -1)
    up2, dn2, sent_near = lax.optimization_barrier((up2, dn2, sent_near))
    up3, dn3 = shift(up2, "z", NZ, 1), shift(dn2, "z", NZ, -1)
    middle = exchange(select(position, (up2, dn2), 2, False))
    far_tok, far_cot = shift(up3[0:TOK], "z", NZ, 1), shift(dn3[TOK:], "z", NZ, -1)
    third = exchange(select(position, (up3, dn3), 2, False))
    far_tok, far_cot, near, middle = lax.optimization_barrier((far_tok, far_cot, near, middle))
    last = exchange_apart(select(position, (far_tok, far_cot), 1, True))

    members_a, apart_a = ((0, -1, 1), (-2, 2)), (True, False)
    members_b, apart_b = ((-3, 3), (half,)), (False, True)
    group_a, back_a = expert(position, near + middle, gate_up, down, members_a, apart_a)
    group_b, sent_back = expert(
        position, third + last, gate_up, down, members_b, apart_b, members_a, apart_a, back_a
    )
    group = (group_a, group_b)
    width = sent_back.shape[1]
    got_back = lax.all_to_all(
        sent_back.reshape(NX * NZ, HEAD, width), ("x", "z"), split_axis=0, concat_axis=0, tiled=True
    )

    def blocks_at(steps, of_core):
        return jnp.stack([2 * ((y + s) % NY) + of_core for s in steps]).astype(jnp.int32)

    def add(a, b):
        return (a.astype(F32) + b.astype(F32)).astype(BF)

    received = shift(weight_blocks(blocks_at((2, 1, 3, 0), 1 - core), group)[0], "core", 2, 1)
    top, bottom = weight_blocks(blocks_at((2,), core), group, received, 0, halves=True)
    top, bottom, nearer = lax.optimization_barrier((top, bottom, blocks_at((1, 3, 0), core)))
    top, bottom = shift(top, "y", NY, 1), shift(bottom, "y", NY, -1)
    plus_top, plus_bottom, minus_top, minus_bottom, own_top, own_bottom = weight_blocks(
        nearer, group, received, 1, halves=True
    )
    plus_bottom = shift(plus_bottom, "y", NY, 1)
    minus_top = shift(minus_top, "y", NY, -1)
    top, bottom = lax.optimization_barrier((top, bottom))
    plus_top, minus_bottom = add(plus_top, top), add(minus_bottom, bottom)
    plus_top, minus_bottom = lax.optimization_barrier((plus_top, minus_bottom))
    got_back = lax.optimization_barrier((got_back, plus_top, minus_bottom))[0]
    plus_top = shift(plus_top, "y", NY, 1)
    minus_bottom = shift(minus_bottom, "y", NY, -1)
    token_grad = combine(routes, slots, got_back.reshape(NX * NZ * HEAD, width))
    grad_gate_up, grad_down = finish(own_top, own_bottom, plus_top, plus_bottom, minus_top, minus_bottom)
    return token_grad, grad_gate_up[None], grad_down[None]


def solution(mesh):
    torus = Mesh(mesh.devices.reshape(NY, 2, NX, NZ), ("y", "core", "x", "z"))
    dp, ep = ("y", "core"), ("x", "z")
    return jax.shard_map(
        per_device,
        mesh=torus,
        in_specs=(P(dp + ep, None),) * 6 + (P(ep, None, None),) * 2,
        out_specs=(P(dp + ep, None), P(ep, dp, None), P(ep, None, dp)),
        check_vma=False,
    )
```

```python
import functools

import jax
import jax.numpy as jnp
from jax import lax
from jax.experimental import pallas as pl
from jax.experimental.pallas import tpu as pltpu
from jax.sharding import Mesh
from jax.sharding import PartitionSpec as P

TOP = 8
SEGS = 4
TOK = 64
CAP = 18
D = 2048
FF = 768
GU = 2 * FF
META = 128
NX = 4
NZ = 8
NY = 4
BLK_D = 256
BF = jnp.bfloat16
F32 = jnp.float32
SMEM = pl.BlockSpec(memory_space=pltpu.SMEM)

HEAD = 16


def params():
    return pltpu.CompilerParams(vmem_limit_bytes=56 * 1024 * 1024)


def whole(a):
    return pl.BlockSpec(a.shape, lambda i: (0,) * len(a.shape))


def pad8(n):
    return (n + 7) // 8 * 8


def layout(blocks):
    count = CAP * blocks
    rem = count % 8
    full = count - rem
    return full, rem, full + rem if 2 * rem <= 8 else full + 8


def slot_rows(blocks):
    return pad8(CAP * blocks)


def send_rows(blocks):
    full, rem, cot = layout(blocks)
    return 2 * full + (8 if cot < full + 8 else 16)


def cost(micros):
    return pl.CostEstimate(flops=int(micros * 1e9), bytes_accessed=int(micros * 3e6), transcendentals=0)


def pick(blocks, pos_ref, data, meta, outs):
    width = 2 * TOK * blocks
    lane = lax.broadcasted_iota(jnp.int32, (1, width), 1)
    block = lane >> 7
    is_cot = (lane >> 6) & 1
    code = meta[0:TOP] * CAP + meta[TOP : 2 * TOP] + (1024 * is_cot + 2048 * block).astype(F32)
    value = meta[2 * TOP : 3 * TOP]
    rows, count = send_rows(blocks), CAP * blocks
    full, rem, cot = layout(blocks)
    row = lax.broadcasted_iota(jnp.int32, (rows, 1), 0)
    row_cot = (row >= cot).astype(jnp.int32)
    if cot < full + 8:
        item = jnp.where(row >= full + 8, row - full - 8, row - rem * row_cot)
        used = (row < full + 2 * rem) | (row >= full + 8)
    else:
        item = row - cot * row_cot
        used = item < count
    first = item < full
    row_block = jnp.where(first, item >> 4, (item - full) >> 1)
    slot = jnp.where(first, item & (HEAD - 1), HEAD + ((item - full) & 1))
    picks = []
    for step in range(NX):
        to = (pos_ref[0] + step) & (NX - 1) if len(outs) == NX else step
        row_code = (to * NZ + pos_ref[1]) * CAP + slot + 1024 * row_cot + 2048 * row_block
        row_code = jnp.where(used, row_code, -1).astype(F32)
        chosen = jnp.zeros((rows, width), F32)
        for k in range(TOP):
            chosen = chosen + jnp.where(code[k : k + 1] == row_code, value[k : k + 1], 0.0)
        picks.append(chosen)
    if len(outs) == NX:
        for chosen, out in zip(picks, outs):
            out[...] = jnp.dot(chosen.astype(BF), data, preferred_element_type=F32).astype(BF)
    else:
        chosen = jnp.concatenate(picks, axis=0).astype(BF)
        outs[0][...] = jnp.dot(chosen, data, preferred_element_type=F32).astype(BF)


def pack_kernel(len_ref, tok_ref, cot_ref, routes_ref, slots_ref, gate_ref, out_ref):
    position = lax.broadcasted_iota(jnp.int32, (1, TOK), 1)
    end = jnp.int32(0)
    picked = jnp.zeros((1, TOK), F32)
    for seg in range(SEGS):
        length = len_ref[0, seg]
        inside = (position >= end) & (position < end + length)
        picked = jnp.where(inside, length.astype(F32), picked)
        end = end + length
    weight = (TOK / SEGS) / picked
    scale = (weight * gate_ref[...]).astype(BF).astype(F32)
    routes = routes_ref[...].astype(F32)
    slots = slots_ref[...].astype(F32)
    ones = jnp.ones((TOP, TOK), F32)
    fill = jnp.zeros((META - 3 * TOP, TOK), F32)
    out_ref[0:TOK, 0:D] = tok_ref[...]
    out_ref[TOK : 2 * TOK, 0:D] = cot_ref[...]
    out_ref[0:TOK, D : D + META] = jnp.concatenate([routes, slots, ones, fill], axis=0).T.astype(BF)
    out_ref[TOK : 2 * TOK, D : D + META] = jnp.concatenate([routes, slots, scale, fill], axis=0).T.astype(BF)


def pack(tokens, cotangent, routes, slots, gates, lengths):
    return pl.pallas_call(
        pack_kernel,
        out_shape=jax.ShapeDtypeStruct((2 * TOK, D + META), BF),
        grid=(1,),
        in_specs=[SMEM] + [whole(a) for a in (tokens, cotangent, routes, slots, gates)],
        out_specs=pl.BlockSpec((2 * TOK, D + META), lambda i: (0, 0)),
        compiler_params=params(),
        cost_estimate=cost(1),
        name="pack",
    )(lengths, tokens, cotangent, routes, slots, gates)


def select_kernel(blocks, count, pos_ref, *refs):
    inputs, outs = refs[:count], refs[count:]
    data = jnp.concatenate([r[:, 0:D] for r in inputs], axis=0)
    if count > blocks:
        metas = [jnp.concatenate([r[:, D:] for r in inputs], axis=0)]
    else:
        metas = [r[:, D:] for r in inputs]
    meta = jnp.concatenate([m.astype(F32).T for m in metas], axis=1)
    pick(blocks, pos_ref, data, meta, outs)


def select(position, inputs, blocks, apart):
    rows = send_rows(blocks) * (1 if apart else NX)
    outs = pl.pallas_call(
        functools.partial(select_kernel, blocks, len(inputs)),
        out_shape=[jax.ShapeDtypeStruct((rows, D), BF)] * (NX if apart else 1),
        grid=(1,),
        in_specs=[SMEM] + [whole(a) for a in inputs],
        out_specs=[pl.BlockSpec((rows, D), lambda i: (0, 0))] * (NX if apart else 1),
        compiler_params=params(),
        cost_estimate=cost(40),
        name="select",
    )(position, *inputs)
    return outs if apart else outs[0]


def chunk_bases(blocks_of):
    bases, base = [], 0
    for blocks in blocks_of:
        bases.append(base)
        base += NX * slot_rows(blocks)
    return bases, base


TILE = 256


def gather_rows(blocks_of, arrays, copies, tok, cot):
    bases, _ = chunk_bases(blocks_of)
    for index, blocks in enumerate(blocks_of):
        for copy in copies[index]:
            copy.wait()
        full, rem, cot_at = layout(blocks)
        sent = send_rows(blocks)
        sub = lax.broadcasted_iota(jnp.int32, (8, 1), 0)
        heads, lates = ([], []), ([], [])
        for step in range(NX):
            if len(arrays[index]) == NX:
                rows = arrays[index][step][...].astype(F32)
            else:
                if step == 0:
                    everything = arrays[index][0][...].astype(F32)
                rows = everything[step * sent : (step + 1) * sent]
            heads[0].append(rows[0:full])
            heads[1].append(rows[sent - full :] if cot_at < full + 8 else rows[cot_at : cot_at + full])
            if cot_at < full + 8:
                mixed = rows[full : full + 8]
                lates[0].append(jnp.where(sub < rem, mixed, 0.0))
                lates[1].append(jnp.where(sub < rem, pltpu.roll(mixed, 8 - rem, 0), 0.0))
            else:
                lates[0].append(rows[full:cot_at])
                lates[1].append(rows[cot_at + full :])
        at = pl.ds(bases[index], NX * slot_rows(blocks))
        tok[at, :] = jnp.concatenate(heads[0] + lates[0], axis=0).astype(BF)
        cot[at, :] = jnp.concatenate(heads[1] + lates[1], axis=0).astype(BF)


def return_places(members, apart, pos_ref):
    bases, _ = chunk_bases([len(m) for m in members])
    places = []
    for base, distances, is_apart in zip(bases, members, apart):
        for step in range(NX):
            to_x = (pos_ref[0] - step) & (NX - 1) if is_apart else step
            for i, distance in enumerate(distances):
                to_z = (pos_ref[1] + distance) & (NZ - 1)
                source = base + (step * len(distances) + i) * HEAD
                places.append((source, pl.multiple_of((to_x * NZ + to_z) * HEAD, HEAD)))
    return places


def late_fold(members, apart, pos_ref):
    main = NX * NZ * HEAD
    row = lax.broadcasted_iota(jnp.int32, (main, 1), 0)
    device, within = row >> 4, row & (HEAD - 1)
    place_x = device >> 3
    away_x = (pos_ref[0] - place_x) & (NX - 1)
    away = ((device & (NZ - 1)) - pos_ref[1]) & (NZ - 1)
    late = jnp.zeros_like(row)
    for c, (distances, is_apart) in enumerate(zip(members, apart)):
        for i, distance in enumerate(distances):
            at = (c * NX + (away_x if is_apart else place_x)) * 8 + 2 * i + (within >> 3)
            late = jnp.where(away == distance % NZ, at, late)
    count = len(members) * NX * 8
    col = lax.broadcasted_iota(jnp.int32, (1, 8 * count), 1)
    return (col == (within & 7) * count + late).astype(F32).astype(BF)


def expert_kernel(members, apart, earlier, earlier_apart, pos_ref, *refs):
    blocks_of = [len(m) for m in members]
    sizes = [NX if a else 1 for a in apart]
    count = sum(sizes)
    arrays, (gate_up_in, down_in) = refs[:count], refs[count : count + 2]
    rest = refs[count + 2 + (1 if earlier else 0) :]
    outs, rest = rest[:5], rest[5:]
    (gate_up, down), rest = rest[:2], rest[2:]
    held, rest = rest[:count], rest[count:]
    tok, cot, grad, act, own_back, row_sems, in_sems, out_sems = rest[:8]
    copies = [pltpu.make_async_copy(a, h, row_sems.at[i]) for i, (a, h) in enumerate(zip(arrays, held))]
    for copy in copies:
        copy.start()
    starts = [sum(sizes[:i]) for i in range(len(sizes))]
    held = [held[i : i + n] for i, n in zip(starts, sizes)]
    copies = [copies[i : i + n] for i, n in zip(starts, sizes)]
    loads = []
    for index, f in enumerate(range(0, FF, TILE)):
        loads.append([
            pltpu.make_async_copy(
                gate_up_in.at[:, pl.ds(f, TILE)], gate_up.at[:, pl.ds(f, TILE)], in_sems.at[3 * index]
            ),
            pltpu.make_async_copy(
                gate_up_in.at[:, pl.ds(FF + f, TILE)], gate_up.at[:, pl.ds(FF + f, TILE)], in_sems.at[3 * index + 1]
            ),
            pltpu.make_async_copy(
                down_in.at[pl.ds(f, TILE), :], down.at[pl.ds(f, TILE), :], in_sems.at[3 * index + 2]
            ),
        ])
    for group in loads:
        for copy in group:
            copy.start()
    stores = [pltpu.make_async_copy(v, o, out_sems.at[i]) for i, (v, o) in enumerate(zip((tok, cot, grad, act), outs))]
    if earlier:
        back_in = refs[count + 2]
        folded, late_rows, place_sems, late_sems = rest[8:]
        places = return_places(earlier, earlier_apart, pos_ref)
        for i, (source, to) in enumerate(places):
            place = outs[4].at[pl.ds(to, HEAD), pl.ds(0, D)]
            stores.append(pltpu.make_async_copy(back_in.at[pl.ds(source, HEAD), :], place, place_sems.at[i]))
            stores[-1].start()
        late_copies = []
        for i, (base, distances) in enumerate(zip(chunk_bases([len(m) for m in earlier])[0], earlier)):
            rows = back_in.at[pl.ds(base + NX * len(distances) * HEAD, NX * 8), :]
            late_copies.append(pltpu.make_async_copy(rows, late_rows.at[pl.ds(i * NX * 8, NX * 8), :], late_sems.at[i]))
            late_copies[-1].start()
    gather_rows(blocks_of, held, copies, tok, cot)
    stores[0].start()
    stores[1].start()
    for index, f in enumerate(range(0, FF, TILE)):
        for copy in loads[index]:
            copy.wait()
        gate_pre = jnp.dot(tok[...], gate_up[:, f : f + TILE], preferred_element_type=F32)
        up_pre = jnp.dot(tok[...], gate_up[:, FF + f : FF + f + TILE], preferred_element_type=F32)
        back = lax.dot_general(
            cot[...], down[f : f + TILE, :], (((1,), (1,)), ((), ())), preferred_element_type=F32
        )
        sigmoid = jax.nn.sigmoid(gate_pre)
        silu = gate_pre * sigmoid
        act[:, f : f + TILE] = (silu * up_pre).astype(BF)
        gate_grad = back * up_pre * sigmoid * (1.0 + gate_pre * (1.0 - sigmoid))
        grad[:, f : f + TILE] = gate_grad.astype(BF)
        grad[:, FF + f : FF + f + TILE] = (back * silu).astype(BF)
    stores[2].start()
    stores[3].start()

    tile = 512
    for d in range(0, D, tile):
        own_back[:, d : d + tile] = lax.dot_general(
            grad[...], gate_up[d : d + tile, :], (((1,), (1,)), ((), ())), preferred_element_type=F32
        ).astype(BF)
    if not earlier:
        stores.append(pltpu.make_async_copy(own_back, outs[4], out_sems.at[4]))
        stores[-1].start()
    else:
        own_places = return_places(members, apart, pos_ref)
        first = len(places)
        for i, (source, to) in enumerate(own_places):
            place = outs[4].at[pl.ds(to, HEAD), pl.ds(0, D)]
            stores.append(pltpu.make_async_copy(own_back.at[pl.ds(source, HEAD), :], place, place_sems.at[first + i]))
            stores[-1].start()
        for copy in late_copies:
            copy.wait()
        lates = [late_rows[...]]
        for base, distances in zip(chunk_bases(blocks_of)[0], members):
            at = base + NX * len(distances) * HEAD
            lates.append(own_back[at : at + NX * 8, :])
        lates = jnp.concatenate(lates, axis=0)
        width = D * (CAP - HEAD) // HEAD
        stacked = jnp.concatenate([lates[:, c : c + width] for c in range(0, D, width)], axis=0)
        fold = late_fold(earlier + members, earlier_apart + apart, pos_ref)
        folded[...] = jnp.dot(fold, stacked, preferred_element_type=F32).astype(BF)
        stores.append(pltpu.make_async_copy(folded, outs[4].at[:, pl.ds(D, width)], out_sems.at[4]))
        stores[-1].start()
    for store in stores:
        store.wait()


def expert(position, arrays, gate_up, down, members, apart, earlier=(), earlier_apart=(), earlier_back=None):
    _, total = chunk_bases([len(m) for m in members])
    back = (NX * NZ * HEAD, D + D * (CAP - HEAD) // HEAD) if earlier else (total, D)
    shapes = [(total, D), (total, D), (total, GU), (total, FF), back]
    any_spec = pl.BlockSpec(memory_space=pl.ANY)
    operands = [*arrays, gate_up, down] + ([earlier_back] if earlier else [])
    buffers = [(D, GU), (FF, D)] + [a.shape for a in arrays] + shapes[:4] + [(total, D)]
    scratch = [pltpu.VMEM(s, BF) for s in buffers]
    scratch += [pltpu.SemaphoreType.DMA((n,)) for n in (len(arrays), 3 * (FF // TILE), 5)]
    if earlier:
        scratch += [pltpu.VMEM((back[0], back[1] - D), BF), pltpu.VMEM((len(earlier) * NX * 8, D), BF)]
        scratch += [pltpu.SemaphoreType.DMA((n,)) for n in (NX * NZ, len(earlier))]
    outs = pl.pallas_call(
        functools.partial(expert_kernel, members, apart, earlier, earlier_apart),
        out_shape=[jax.ShapeDtypeStruct(s, BF) for s in shapes],
        grid=(1,),
        in_specs=[SMEM] + [any_spec] * len(operands),
        out_specs=[any_spec] * len(shapes),
        scratch_shapes=scratch,
        compiler_params=params(),
        cost_estimate=cost(1 if earlier else 5),
        name="expert",
    )(position, *operands)
    return outs[:4], outs[4]


def combine_kernel(routes_ref, slots_ref, rows_ref, out_ref):
    code = (routes_ref[...].astype(F32) * CAP + slots_ref[...].astype(F32)).T
    main = NX * NZ * HEAD
    col = lax.broadcasted_iota(jnp.int32, (1, main), 1)
    device, within = col >> 4, col & (HEAD - 1)
    head_code = (device * CAP + within).astype(F32)
    late_code = (device * CAP + HEAD + (within >> 3)).astype(F32)
    head = jnp.zeros((TOK, main), F32)
    late = jnp.zeros((TOK, main), F32)
    for k in range(TOP):
        head = head + (code[:, k : k + 1] == head_code).astype(F32)
        late = late + (code[:, k : k + 1] == late_code).astype(F32)
    folds = HEAD // (CAP - HEAD)
    lates = jnp.concatenate([jnp.where((within & 7) == j, late, 0.0) for j in range(folds)], axis=0)
    tail = jnp.dot(lates.astype(BF), rows_ref[:, D:], preferred_element_type=F32)
    total = jnp.dot(head.astype(BF), rows_ref[:, 0:D], preferred_element_type=F32)
    width = D // folds
    for j in range(folds):
        at = slice(j * width, (j + 1) * width)
        out_ref[:, at] = (total[:, at] + tail[j * TOK : (j + 1) * TOK]).astype(BF)


def combine(routes, slots, rows):
    return pl.pallas_call(
        combine_kernel,
        out_shape=jax.ShapeDtypeStruct((TOK, D), BF),
        grid=(1,),
        in_specs=[whole(a) for a in (routes, slots, rows)],
        out_specs=pl.BlockSpec((TOK, D), lambda i: (0, 0)),
        compiler_params=params(),
        cost_estimate=cost(20),
        name="combine",
    )(routes, slots, rows)


def weight_kernel(groups, count, halves, which_ref, *refs):
    rest = refs[4 * groups :]
    extra, outs = (rest[:1], rest[1:]) if len(rest) > (2 * count if halves else 1) else ((), rest)
    first = (((0,), (0,)), ((), ()))
    rows = BLK_D // 2
    for cols, left, right in ((slice(0, GU), 0, 2), (slice(GU, GU + FF), 1, 3)):
        total = extra[0][:, cols].astype(F32) if extra else None
        for g in range(groups):
            part = lax.dot_general(
                refs[4 * g + left][...], refs[4 * g + right][...], first, preferred_element_type=F32
            )
            total = part if total is None else total + part
        total = total.astype(BF)
        if not halves:
            outs[0][:, cols] = total
            continue
        for i in range(count):

            @pl.when(pl.program_id(0) == i)
            def _():
                outs[2 * i][:, cols] = total[0:rows]
                outs[2 * i + 1][:, cols] = total[rows:]


def weight_blocks(which, groups, received=None, block=0, halves=False):
    count = which.shape[0]

    def cut(a):
        return pl.BlockSpec((a.shape[0], BLK_D), lambda i, w: (0, w[i]))

    def full(a):
        return pl.BlockSpec(a.shape, lambda i, w: (0, 0))

    specs = [spec for g in groups for spec in (cut(g[0]), cut(g[1]), full(g[2]), full(g[3]))]
    extra = []
    if received is not None:
        specs.append(pl.BlockSpec((BLK_D, GU + FF), lambda i, w: (block + i, 0)))
        extra.append(received)
    if halves:
        shapes = [(BLK_D // 2, GU + FF)] * (2 * count)
        out_specs = [pl.BlockSpec(shapes[0], lambda i, w: (0, 0))] * (2 * count)
    else:
        shapes = [(count * BLK_D, GU + FF)]
        out_specs = [pl.BlockSpec((BLK_D, GU + FF), lambda i, w: (i, 0))]
    return pl.pallas_call(
        functools.partial(weight_kernel, len(groups), count, halves),
        out_shape=[jax.ShapeDtypeStruct(s, BF) for s in shapes],
        grid_spec=pltpu.PrefetchScalarGridSpec(
            num_scalar_prefetch=1, grid=(count,), in_specs=specs, out_specs=out_specs
        ),
        compiler_params=params(),
        cost_estimate=cost(3 if count == 3 else 1),
        name="weight_blocks",
    )(which, *(a for g in groups for a in g), *extra)


def finish_kernel(own_top, own_bottom, plus_top, plus_bottom, minus_top, minus_bottom, gate_up, down):
    hop = BLK_D // 2
    tops, bottoms = (own_top, plus_top, minus_top), (own_bottom, plus_bottom, minus_bottom)
    for at, (own, plus, minus) in ((slice(0, hop), tops), (slice(hop, BLK_D), bottoms)):
        total = own[...].astype(F32) + plus[...].astype(F32) + minus[...].astype(F32)
        gate_up[at, :] = total[:, 0:GU].astype(BF)
        down[:, at] = total[:, GU:].T.astype(BF)


def finish(*parts):
    return pl.pallas_call(
        finish_kernel,
        out_shape=[jax.ShapeDtypeStruct((BLK_D, GU), BF), jax.ShapeDtypeStruct((FF, BLK_D), BF)],
        grid=(1,),
        in_specs=[whole(a) for a in parts],
        out_specs=[pl.BlockSpec((BLK_D, GU), lambda i: (0, 0)), pl.BlockSpec((FF, BLK_D), lambda i: (0, 0))],
        compiler_params=params(),
        cost_estimate=cost(1),
        name="finish",
    )(*parts)


def shift(array, axis, size, by):
    return lax.ppermute(array, axis, [(i, (i + by) % size) for i in range(size)])


def per_device(tokens, cotangent, routes, slot_index, gate_probs, lengths, w_gate_up, w_down):
    x, z = lax.axis_index("x"), lax.axis_index("z")
    y, core = lax.axis_index("y"), lax.axis_index("core")
    position = jnp.stack([x, z]).astype(jnp.int32)
    gate_up, down = w_gate_up[0], w_down[0]
    routes, slots, gates = routes.T, slot_index.T, gate_probs.T

    own = pack(tokens, cotangent, routes, slots, gates, lengths)

    def exchange(rows):
        return [lax.all_to_all(rows, "x", split_axis=0, concat_axis=0, tiled=True)]

    def exchange_apart(rows):
        return [rows[0]] + [shift(rows[s], "x", NX, s) for s in range(1, NX)]

    half = NZ // 2
    up1, dn1 = shift(own, "z", NZ, 1), shift(own, "z", NZ, -1)
    sent_near = select(position, (own, up1, dn1), 3, True)
    near = exchange_apart(sent_near)
    up2, dn2 = shift(up1, "z", NZ, 1), shift(dn1, "z", NZ, -1)
    up2, dn2, sent_near = lax.optimization_barrier((up2, dn2, sent_near))
    up3, dn3 = shift(up2, "z", NZ, 1), shift(dn2, "z", NZ, -1)
    middle = exchange(select(position, (up2, dn2), 2, False))
    far_tok, far_cot = shift(up3[0:TOK], "z", NZ, 1), shift(dn3[TOK:], "z", NZ, -1)
    third = exchange_apart(select(position, (up3, dn3), 2, True))
    far_tok, far_cot, near, middle = lax.optimization_barrier((far_tok, far_cot, near, middle))
    last = exchange_apart(select(position, (far_tok, far_cot), 1, True))

    members_a, apart_a = ((0, -1, 1), (-2, 2)), (True, False)
    members_b, apart_b = ((-3, 3), (half,)), (True, True)
    group_a, back_a = expert(position, near + middle, gate_up, down, members_a, apart_a)
    group_b, sent_back = expert(
        position, third + last, gate_up, down, members_b, apart_b, members_a, apart_a, back_a
    )
    group = (group_a, group_b)
    width = sent_back.shape[1]
    got_back = lax.all_to_all(
        sent_back.reshape(NX * NZ, HEAD, width), ("x", "z"), split_axis=0, concat_axis=0, tiled=True
    )

    def blocks_at(steps, of_core):
        return jnp.stack([2 * ((y + s) % NY) + of_core for s in steps]).astype(jnp.int32)

    def add(a, b):
        return (a.astype(F32) + b.astype(F32)).astype(BF)

    received = shift(weight_blocks(blocks_at((2, 1, 3, 0), 1 - core), group)[0], "core", 2, 1)
    top, bottom = weight_blocks(blocks_at((2,), core), group, received, 0, halves=True)
    top, bottom, nearer = lax.optimization_barrier((top, bottom, blocks_at((1, 3, 0), core)))
    top, bottom = shift(top, "y", NY, 1), shift(bottom, "y", NY, -1)
    plus_top, plus_bottom, minus_top, minus_bottom, own_top, own_bottom = weight_blocks(
        nearer, group, received, 1, halves=True
    )
    plus_bottom = shift(plus_bottom, "y", NY, 1)
    minus_top = shift(minus_top, "y", NY, -1)
    top, bottom = lax.optimization_barrier((top, bottom))
    plus_top, minus_bottom = add(plus_top, top), add(minus_bottom, bottom)
    plus_top, minus_bottom = lax.optimization_barrier((plus_top, minus_bottom))
    got_back = lax.optimization_barrier((got_back, plus_top, minus_bottom))[0]
    plus_top = shift(plus_top, "y", NY, 1)
    minus_bottom = shift(minus_bottom, "y", NY, -1)
    token_grad = combine(routes, slots, got_back.reshape(NX * NZ * HEAD, width))
    grad_gate_up, grad_down = finish(own_top, own_bottom, plus_top, plus_bottom, minus_top, minus_bottom)
    return token_grad, grad_gate_up[None], grad_down[None]


def solution(mesh):
    torus = Mesh(mesh.devices.reshape(NY, 2, NX, NZ), ("y", "core", "x", "z"))
    dp, ep = ("y", "core"), ("x", "z")
    return jax.shard_map(
        per_device,
        mesh=torus,
        in_specs=(P(dp + ep, None),) * 6 + (P(ep, None, None),) * 2,
        out_specs=(P(dp + ep, None), P(ep, dp, None), P(ep, None, dp)),
        check_vma=False,
    )
```

```python
import functools

import jax
import jax.numpy as jnp
from jax import lax
from jax.experimental import pallas as pl
from jax.experimental.pallas import tpu as pltpu
from jax.sharding import Mesh
from jax.sharding import PartitionSpec as P

TOP = 8
SEGS = 4
TOK = 64
CAP = 18
D = 2048
FF = 768
GU = 2 * FF
META = 128
NX = 4
NZ = 8
NY = 4
BLK_D = 256
BF = jnp.bfloat16
F32 = jnp.float32
SMEM = pl.BlockSpec(memory_space=pltpu.SMEM)

HEAD = 16


def params():
    return pltpu.CompilerParams(vmem_limit_bytes=56 * 1024 * 1024)


def whole(a):
    return pl.BlockSpec(a.shape, lambda i: (0,) * len(a.shape))


def pad8(n):
    return (n + 7) // 8 * 8


def layout(blocks):
    count = CAP * blocks
    rem = count % 8
    full = count - rem
    return full, rem, full + rem if 2 * rem <= 8 else full + 8


def slot_rows(blocks):
    return pad8(CAP * blocks)


def send_rows(blocks):
    full, rem, cot = layout(blocks)
    return 2 * full + (8 if cot < full + 8 else 16)


def cost(micros):
    return pl.CostEstimate(flops=int(micros * 1e9), bytes_accessed=int(micros * 3e6), transcendentals=0)


def pick(blocks, pos_ref, data, meta, outs):
    width = 2 * TOK * blocks
    lane = lax.broadcasted_iota(jnp.int32, (1, width), 1)
    block = lane >> 7
    is_cot = (lane >> 6) & 1
    code = meta[0:TOP] * CAP + meta[TOP : 2 * TOP] + (1024 * is_cot + 2048 * block).astype(F32)
    value = meta[2 * TOP : 3 * TOP]
    rows, count = send_rows(blocks), CAP * blocks
    full, rem, cot = layout(blocks)
    row = lax.broadcasted_iota(jnp.int32, (rows, 1), 0)
    row_cot = (row >= cot).astype(jnp.int32)
    if cot < full + 8:
        item = jnp.where(row >= full + 8, row - full - 8, row - rem * row_cot)
        used = (row < full + 2 * rem) | (row >= full + 8)
    else:
        item = row - cot * row_cot
        used = item < count
    first = item < full
    row_block = jnp.where(first, item >> 4, (item - full) >> 1)
    slot = jnp.where(first, item & (HEAD - 1), HEAD + ((item - full) & 1))
    picks = []
    for step in range(NX):
        to = (pos_ref[0] + step) & (NX - 1) if len(outs) == NX else step
        row_code = (to * NZ + pos_ref[1]) * CAP + slot + 1024 * row_cot + 2048 * row_block
        row_code = jnp.where(used, row_code, -1).astype(F32)
        chosen = jnp.zeros((rows, width), F32)
        for k in range(TOP):
            chosen = chosen + jnp.where(code[k : k + 1] == row_code, value[k : k + 1], 0.0)
        picks.append(chosen)
    if len(outs) == NX:
        for chosen, out in zip(picks, outs):
            out[...] = jnp.dot(chosen.astype(BF), data, preferred_element_type=F32).astype(BF)
    else:
        chosen = jnp.concatenate(picks, axis=0).astype(BF)
        outs[0][...] = jnp.dot(chosen, data, preferred_element_type=F32).astype(BF)


def pack_kernel(len_ref, tok_ref, cot_ref, routes_ref, slots_ref, gate_ref, out_ref):
    position = lax.broadcasted_iota(jnp.int32, (1, TOK), 1)
    end = jnp.int32(0)
    picked = jnp.zeros((1, TOK), F32)
    for seg in range(SEGS):
        length = len_ref[0, seg]
        inside = (position >= end) & (position < end + length)
        picked = jnp.where(inside, length.astype(F32), picked)
        end = end + length
    weight = (TOK / SEGS) / picked
    scale = (weight * gate_ref[...]).astype(BF).astype(F32)
    routes = routes_ref[...].astype(F32)
    slots = slots_ref[...].astype(F32)
    ones = jnp.ones((TOP, TOK), F32)
    fill = jnp.zeros((META - 3 * TOP, TOK), F32)
    out_ref[0:TOK, 0:D] = tok_ref[...]
    out_ref[TOK : 2 * TOK, 0:D] = cot_ref[...]
    out_ref[0:TOK, D : D + META] = jnp.concatenate([routes, slots, ones, fill], axis=0).T.astype(BF)
    out_ref[TOK : 2 * TOK, D : D + META] = jnp.concatenate([routes, slots, scale, fill], axis=0).T.astype(BF)


def pack(tokens, cotangent, routes, slots, gates, lengths):
    return pl.pallas_call(
        pack_kernel,
        out_shape=jax.ShapeDtypeStruct((2 * TOK, D + META), BF),
        grid=(1,),
        in_specs=[SMEM] + [whole(a) for a in (tokens, cotangent, routes, slots, gates)],
        out_specs=pl.BlockSpec((2 * TOK, D + META), lambda i: (0, 0)),
        compiler_params=params(),
        cost_estimate=cost(1),
        name="pack",
    )(lengths, tokens, cotangent, routes, slots, gates)


def select_kernel(blocks, count, pos_ref, *refs):
    inputs, outs = refs[:count], refs[count:]
    data = jnp.concatenate([r[:, 0:D] for r in inputs], axis=0)
    if count > blocks:
        metas = [jnp.concatenate([r[:, D:] for r in inputs], axis=0)]
    else:
        metas = [r[:, D:] for r in inputs]
    meta = jnp.concatenate([m.astype(F32).T for m in metas], axis=1)
    pick(blocks, pos_ref, data, meta, outs)


def select(position, inputs, blocks, apart):
    rows = send_rows(blocks) * (1 if apart else NX)
    outs = pl.pallas_call(
        functools.partial(select_kernel, blocks, len(inputs)),
        out_shape=[jax.ShapeDtypeStruct((rows, D), BF)] * (NX if apart else 1),
        grid=(1,),
        in_specs=[SMEM] + [whole(a) for a in inputs],
        out_specs=[pl.BlockSpec((rows, D), lambda i: (0, 0))] * (NX if apart else 1),
        compiler_params=params(),
        cost_estimate=cost(40),
        name="select",
    )(position, *inputs)
    return outs if apart else outs[0]


def chunk_bases(blocks_of):
    bases, base = [], 0
    for blocks in blocks_of:
        bases.append(base)
        base += NX * slot_rows(blocks)
    return bases, base


TILE = 384


def gather_rows(blocks_of, arrays, copies, tok, cot):
    bases, _ = chunk_bases(blocks_of)
    for index, blocks in enumerate(blocks_of):
        for copy in copies[index]:
            copy.wait()
        full, rem, cot_at = layout(blocks)
        sent = send_rows(blocks)
        sub = lax.broadcasted_iota(jnp.int32, (8, 1), 0)
        heads, lates = ([], []), ([], [])
        for step in range(NX):
            if len(arrays[index]) == NX:
                rows = arrays[index][step][...].astype(F32)
            else:
                if step == 0:
                    everything = arrays[index][0][...].astype(F32)
                rows = everything[step * sent : (step + 1) * sent]
            heads[0].append(rows[0:full])
            heads[1].append(rows[sent - full :] if cot_at < full + 8 else rows[cot_at : cot_at + full])
            if cot_at < full + 8:
                mixed = rows[full : full + 8]
                lates[0].append(jnp.where(sub < rem, mixed, 0.0))
                lates[1].append(jnp.where(sub < rem, pltpu.roll(mixed, 8 - rem, 0), 0.0))
            else:
                lates[0].append(rows[full:cot_at])
                lates[1].append(rows[cot_at + full :])
        at = pl.ds(bases[index], NX * slot_rows(blocks))
        tok[at, :] = jnp.concatenate(heads[0] + lates[0], axis=0).astype(BF)
        cot[at, :] = jnp.concatenate(heads[1] + lates[1], axis=0).astype(BF)


def return_places(members, apart, pos_ref):
    bases, _ = chunk_bases([len(m) for m in members])
    places = []
    for base, distances, is_apart in zip(bases, members, apart):
        for step in range(NX):
            to_x = (pos_ref[0] - step) & (NX - 1) if is_apart else step
            for i, distance in enumerate(distances):
                to_z = (pos_ref[1] + distance) & (NZ - 1)
                source = base + (step * len(distances) + i) * HEAD
                places.append((source, pl.multiple_of((to_x * NZ + to_z) * HEAD, HEAD)))
    return places


def late_fold(members, apart, pos_ref):
    main = NX * NZ * HEAD
    row = lax.broadcasted_iota(jnp.int32, (main, 1), 0)
    device, within = row >> 4, row & (HEAD - 1)
    place_x = device >> 3
    away_x = (pos_ref[0] - place_x) & (NX - 1)
    away = ((device & (NZ - 1)) - pos_ref[1]) & (NZ - 1)
    late = jnp.zeros_like(row)
    for c, (distances, is_apart) in enumerate(zip(members, apart)):
        for i, distance in enumerate(distances):
            at = (c * NX + (away_x if is_apart else place_x)) * 8 + 2 * i + (within >> 3)
            late = jnp.where(away == distance % NZ, at, late)
    count = len(members) * NX * 8
    col = lax.broadcasted_iota(jnp.int32, (1, 8 * count), 1)
    return (col == (within & 7) * count + late).astype(F32).astype(BF)


def expert_kernel(members, apart, earlier, earlier_apart, pos_ref, *refs):
    blocks_of = [len(m) for m in members]
    sizes = [NX if a else 1 for a in apart]
    count = sum(sizes)
    arrays, (gate_up_in, down_in) = refs[:count], refs[count : count + 2]
    rest = refs[count + 2 + (1 if earlier else 0) :]
    outs, rest = rest[:5], rest[5:]
    (gate_up, down), rest = rest[:2], rest[2:]
    held, rest = rest[:count], rest[count:]
    tok, cot, grad, act, own_back, row_sems, in_sems, out_sems = rest[:8]
    copies = [pltpu.make_async_copy(a, h, row_sems.at[i]) for i, (a, h) in enumerate(zip(arrays, held))]
    for copy in copies:
        copy.start()
    starts = [sum(sizes[:i]) for i in range(len(sizes))]
    held = [held[i : i + n] for i, n in zip(starts, sizes)]
    copies = [copies[i : i + n] for i, n in zip(starts, sizes)]
    loads = []
    for index, f in enumerate(range(0, FF, TILE)):
        loads.append([
            pltpu.make_async_copy(
                gate_up_in.at[:, pl.ds(f, TILE)], gate_up.at[:, pl.ds(f, TILE)], in_sems.at[3 * index]
            ),
            pltpu.make_async_copy(
                gate_up_in.at[:, pl.ds(FF + f, TILE)], gate_up.at[:, pl.ds(FF + f, TILE)], in_sems.at[3 * index + 1]
            ),
            pltpu.make_async_copy(
                down_in.at[pl.ds(f, TILE), :], down.at[pl.ds(f, TILE), :], in_sems.at[3 * index + 2]
            ),
        ])
    for group in loads:
        for copy in group:
            copy.start()
    stores = [pltpu.make_async_copy(v, o, out_sems.at[i]) for i, (v, o) in enumerate(zip((tok, cot, grad, act), outs))]
    if earlier:
        back_ref, earlier_back, earlier_sem = rest[8:]
        earlier_copy = pltpu.make_async_copy(refs[count + 2], earlier_back, earlier_sem.at[0])
        earlier_copy.start()
    gather_rows(blocks_of, held, copies, tok, cot)
    stores[0].start()
    stores[1].start()
    for index, f in enumerate(range(0, FF, TILE)):
        for copy in loads[index]:
            copy.wait()
        gate_pre = jnp.dot(tok[...], gate_up[:, f : f + TILE], preferred_element_type=F32)
        up_pre = jnp.dot(tok[...], gate_up[:, FF + f : FF + f + TILE], preferred_element_type=F32)
        back = lax.dot_general(
            cot[...], down[f : f + TILE, :], (((1,), (1,)), ((), ())), preferred_element_type=F32
        )
        sigmoid = jax.nn.sigmoid(gate_pre)
        silu = gate_pre * sigmoid
        act[:, f : f + TILE] = (silu * up_pre).astype(BF)
        gate_grad = back * up_pre * sigmoid * (1.0 + gate_pre * (1.0 - sigmoid))
        grad[:, f : f + TILE] = gate_grad.astype(BF)
        grad[:, FF + f : FF + f + TILE] = (back * silu).astype(BF)
    stores[2].start()
    stores[3].start()

    tile = 512
    for d in range(0, D, tile):
        own_back[:, d : d + tile] = lax.dot_general(
            grad[...], gate_up[d : d + tile, :], (((1,), (1,)), ((), ())), preferred_element_type=F32
        ).astype(BF)
    if not earlier:
        stores.append(pltpu.make_async_copy(own_back, outs[4], out_sems.at[4]))
        stores[-1].start()
    else:
        earlier_copy.wait()
        lates = []
        for rows, own_members, own_apart in ((earlier_back, earlier, earlier_apart), (own_back, members, apart)):
            for source, to in return_places(own_members, own_apart, pos_ref):
                back_ref[pl.ds(to, HEAD), 0:D] = rows[source : source + HEAD, :]
            for base, distances in zip(chunk_bases([len(m) for m in own_members])[0], own_members):
                at = base + NX * len(distances) * HEAD
                lates.append(rows[at : at + NX * 8, :])
        stores.append(pltpu.make_async_copy(back_ref.at[:, pl.ds(0, D)], outs[4].at[:, pl.ds(0, D)], out_sems.at[4]))
        stores[-1].start()
        lates = jnp.concatenate(lates, axis=0)
        width = D * (CAP - HEAD) // HEAD
        stacked = jnp.concatenate([lates[:, c : c + width] for c in range(0, D, width)], axis=0)
        fold = late_fold(earlier + members, earlier_apart + apart, pos_ref)
        back_ref[:, D:] = jnp.dot(fold, stacked, preferred_element_type=F32).astype(BF)
        stores.append(
            pltpu.make_async_copy(back_ref.at[:, pl.ds(D, width)], outs[4].at[:, pl.ds(D, width)], out_sems.at[5])
        )
        stores[-1].start()
    for store in stores:
        store.wait()


def expert(position, arrays, gate_up, down, members, apart, earlier=(), earlier_apart=(), earlier_back=None):
    _, total = chunk_bases([len(m) for m in members])
    back = (NX * NZ * HEAD, D + D * (CAP - HEAD) // HEAD) if earlier else (total, D)
    shapes = [(total, D), (total, D), (total, GU), (total, FF), back]
    any_spec = pl.BlockSpec(memory_space=pl.ANY)
    operands = [*arrays, gate_up, down] + ([earlier_back] if earlier else [])
    buffers = [(D, GU), (FF, D)] + [a.shape for a in arrays] + shapes[:4] + [(total, D)]
    scratch = [pltpu.VMEM(s, BF) for s in buffers]
    scratch += [pltpu.SemaphoreType.DMA((n,)) for n in (len(arrays), 3 * (FF // TILE), 6)]
    if earlier:
        scratch += [pltpu.VMEM(back, BF), pltpu.VMEM(earlier_back.shape, BF), pltpu.SemaphoreType.DMA((1,))]
    outs = pl.pallas_call(
        functools.partial(expert_kernel, members, apart, earlier, earlier_apart),
        out_shape=[jax.ShapeDtypeStruct(s, BF) for s in shapes],
        grid=(1,),
        in_specs=[SMEM] + [any_spec] * len(operands),
        out_specs=[any_spec] * len(shapes),
        scratch_shapes=scratch,
        compiler_params=params(),
        cost_estimate=cost(1 if earlier else 5),
        name="expert",
    )(position, *operands)
    return outs[:4], outs[4]


def combine_kernel(routes_ref, slots_ref, rows_ref, out_ref):
    code = (routes_ref[...].astype(F32) * CAP + slots_ref[...].astype(F32)).T
    main = NX * NZ * HEAD
    col = lax.broadcasted_iota(jnp.int32, (1, main), 1)
    device, within = col >> 4, col & (HEAD - 1)
    head_code = (device * CAP + within).astype(F32)
    late_code = (device * CAP + HEAD + (within >> 3)).astype(F32)
    head = jnp.zeros((TOK, main), F32)
    late = jnp.zeros((TOK, main), F32)
    for k in range(TOP):
        head = head + (code[:, k : k + 1] == head_code).astype(F32)
        late = late + (code[:, k : k + 1] == late_code).astype(F32)
    folds = HEAD // (CAP - HEAD)
    lates = jnp.concatenate([jnp.where((within & 7) == j, late, 0.0) for j in range(folds)], axis=0)
    tail = jnp.dot(lates.astype(BF), rows_ref[:, D:], preferred_element_type=F32)
    total = jnp.dot(head.astype(BF), rows_ref[:, 0:D], preferred_element_type=F32)
    width = D // folds
    for j in range(folds):
        at = slice(j * width, (j + 1) * width)
        out_ref[:, at] = (total[:, at] + tail[j * TOK : (j + 1) * TOK]).astype(BF)


def combine(routes, slots, rows):
    return pl.pallas_call(
        combine_kernel,
        out_shape=jax.ShapeDtypeStruct((TOK, D), BF),
        grid=(1,),
        in_specs=[whole(a) for a in (routes, slots, rows)],
        out_specs=pl.BlockSpec((TOK, D), lambda i: (0, 0)),
        compiler_params=params(),
        cost_estimate=cost(20),
        name="combine",
    )(routes, slots, rows)


def weight_kernel(groups, count, halves, which_ref, *refs):
    rest = refs[4 * groups :]
    extra, outs = (rest[:1], rest[1:]) if len(rest) > (2 * count if halves else 1) else ((), rest)
    first = (((0,), (0,)), ((), ()))
    rows = BLK_D // 2
    for cols, left, right in ((slice(0, GU), 0, 2), (slice(GU, GU + FF), 1, 3)):
        total = extra[0][:, cols].astype(F32) if extra else None
        for g in range(groups):
            part = lax.dot_general(
                refs[4 * g + left][...], refs[4 * g + right][...], first, preferred_element_type=F32
            )
            total = part if total is None else total + part
        total = total.astype(BF)
        if not halves:
            outs[0][:, cols] = total
            continue
        for i in range(count):

            @pl.when(pl.program_id(0) == i)
            def _():
                outs[2 * i][:, cols] = total[0:rows]
                outs[2 * i + 1][:, cols] = total[rows:]


def weight_blocks(which, groups, received=None, block=0, halves=False):
    count = which.shape[0]

    def cut(a):
        return pl.BlockSpec((a.shape[0], BLK_D), lambda i, w: (0, w[i]))

    def full(a):
        return pl.BlockSpec(a.shape, lambda i, w: (0, 0))

    specs = [spec for g in groups for spec in (cut(g[0]), cut(g[1]), full(g[2]), full(g[3]))]
    extra = []
    if received is not None:
        specs.append(pl.BlockSpec((BLK_D, GU + FF), lambda i, w: (block + i, 0)))
        extra.append(received)
    if halves:
        shapes = [(BLK_D // 2, GU + FF)] * (2 * count)
        out_specs = [pl.BlockSpec(shapes[0], lambda i, w: (0, 0))] * (2 * count)
    else:
        shapes = [(count * BLK_D, GU + FF)]
        out_specs = [pl.BlockSpec((BLK_D, GU + FF), lambda i, w: (i, 0))]
    return pl.pallas_call(
        functools.partial(weight_kernel, len(groups), count, halves),
        out_shape=[jax.ShapeDtypeStruct(s, BF) for s in shapes],
        grid_spec=pltpu.PrefetchScalarGridSpec(
            num_scalar_prefetch=1, grid=(count,), in_specs=specs, out_specs=out_specs
        ),
        compiler_params=params(),
        cost_estimate=cost(3 if count == 3 else 1),
        name="weight_blocks",
    )(which, *(a for g in groups for a in g), *extra)


def finish_kernel(own_top, own_bottom, plus_top, plus_bottom, minus_top, minus_bottom, gate_up, down):
    hop = BLK_D // 2
    tops, bottoms = (own_top, plus_top, minus_top), (own_bottom, plus_bottom, minus_bottom)
    for at, (own, plus, minus) in ((slice(0, hop), tops), (slice(hop, BLK_D), bottoms)):
        total = own[...].astype(F32) + plus[...].astype(F32) + minus[...].astype(F32)
        gate_up[at, :] = total[:, 0:GU].astype(BF)
        down[:, at] = total[:, GU:].T.astype(BF)


def finish(*parts):
    return pl.pallas_call(
        finish_kernel,
        out_shape=[jax.ShapeDtypeStruct((BLK_D, GU), BF), jax.ShapeDtypeStruct((FF, BLK_D), BF)],
        grid=(1,),
        in_specs=[whole(a) for a in parts],
        out_specs=[pl.BlockSpec((BLK_D, GU), lambda i: (0, 0)), pl.BlockSpec((FF, BLK_D), lambda i: (0, 0))],
        compiler_params=params(),
        cost_estimate=cost(1),
        name="finish",
    )(*parts)


def shift(array, axis, size, by):
    return lax.ppermute(array, axis, [(i, (i + by) % size) for i in range(size)])


def per_device(tokens, cotangent, routes, slot_index, gate_probs, lengths, w_gate_up, w_down):
    x, z = lax.axis_index("x"), lax.axis_index("z")
    y, core = lax.axis_index("y"), lax.axis_index("core")
    position = jnp.stack([x, z]).astype(jnp.int32)
    gate_up, down = w_gate_up[0], w_down[0]
    routes, slots, gates = routes.T, slot_index.T, gate_probs.T

    own = pack(tokens, cotangent, routes, slots, gates, lengths)

    def exchange(rows):
        return [lax.all_to_all(rows, "x", split_axis=0, concat_axis=0, tiled=True)]

    def exchange_apart(rows):
        return [rows[0]] + [shift(rows[s], "x", NX, s) for s in range(1, NX)]

    half = NZ // 2
    up1, dn1 = shift(own, "z", NZ, 1), shift(own, "z", NZ, -1)
    sent_near = select(position, (own, up1, dn1), 3, True)
    near = exchange_apart(sent_near)
    up2, dn2 = shift(up1, "z", NZ, 1), shift(dn1, "z", NZ, -1)
    up2, dn2, sent_near = lax.optimization_barrier((up2, dn2, sent_near))
    up3, dn3 = shift(up2, "z", NZ, 1), shift(dn2, "z", NZ, -1)
    middle = exchange(select(position, (up2, dn2), 2, False))
    far_tok, far_cot = shift(up3[0:TOK], "z", NZ, 1), shift(dn3[TOK:], "z", NZ, -1)
    third = exchange_apart(select(position, (up3, dn3), 2, True))
    far_tok, far_cot, near, middle = lax.optimization_barrier((far_tok, far_cot, near, middle))
    last = exchange_apart(select(position, (far_tok, far_cot), 1, True))

    members_a, apart_a = ((0, -1, 1), (-2, 2)), (True, False)
    members_b, apart_b = ((-3, 3), (half,)), (True, True)
    group_a, back_a = expert(position, near + middle, gate_up, down, members_a, apart_a)
    group_b, sent_back = expert(
        position, third + last, gate_up, down, members_b, apart_b, members_a, apart_a, back_a
    )
    group = (group_a, group_b)
    width = sent_back.shape[1]
    got_back = lax.all_to_all(
        sent_back.reshape(NX * NZ, HEAD, width), ("x", "z"), split_axis=0, concat_axis=0, tiled=True
    )

    def blocks_at(steps, of_core):
        return jnp.stack([2 * ((y + s) % NY) + of_core for s in steps]).astype(jnp.int32)

    def add(a, b):
        return (a.astype(F32) + b.astype(F32)).astype(BF)

    received = shift(weight_blocks(blocks_at((2, 1, 3, 0), 1 - core), group)[0], "core", 2, 1)
    top, bottom = weight_blocks(blocks_at((2,), core), group, received, 0, halves=True)
    top, bottom, nearer = lax.optimization_barrier((top, bottom, blocks_at((1, 3, 0), core)))
    top, bottom = shift(top, "y", NY, 1), shift(bottom, "y", NY, -1)
    plus_top, plus_bottom, minus_top, minus_bottom, own_top, own_bottom = weight_blocks(
        nearer, group, received, 1, halves=True
    )
    plus_bottom = shift(plus_bottom, "y", NY, 1)
    minus_top = shift(minus_top, "y", NY, -1)
    top, bottom = lax.optimization_barrier((top, bottom))
    plus_top, minus_bottom = add(plus_top, top), add(minus_bottom, bottom)
    plus_top, minus_bottom = lax.optimization_barrier((plus_top, minus_bottom))
    got_back = lax.optimization_barrier((got_back, plus_top, minus_bottom))[0]
    plus_top = shift(plus_top, "y", NY, 1)
    minus_bottom = shift(minus_bottom, "y", NY, -1)
    token_grad = combine(routes, slots, got_back.reshape(NX * NZ * HEAD, width))
    grad_gate_up, grad_down = finish(own_top, own_bottom, plus_top, plus_bottom, minus_top, minus_bottom)
    return token_grad, grad_gate_up[None], grad_down[None]


def solution(mesh):
    torus = Mesh(mesh.devices.reshape(NY, 2, NX, NZ), ("y", "core", "x", "z"))
    dp, ep = ("y", "core"), ("x", "z")
    return jax.shard_map(
        per_device,
        mesh=torus,
        in_specs=(P(dp + ep, None),) * 6 + (P(ep, None, None),) * 2,
        out_specs=(P(dp + ep, None), P(ep, dp, None), P(ep, None, dp)),
        check_vma=False,
    )
```

```python
import functools

import jax
import jax.numpy as jnp
from jax import lax
from jax.experimental import pallas as pl
from jax.experimental.pallas import tpu as pltpu
from jax.sharding import Mesh
from jax.sharding import PartitionSpec as P

TOP = 8
SEGS = 4
TOK = 64
CAP = 18
D = 2048
FF = 768
GU = 2 * FF
META = 128
NX = 4
NZ = 8
NY = 4
BLK_D = 256
BF = jnp.bfloat16
F32 = jnp.float32
SMEM = pl.BlockSpec(memory_space=pltpu.SMEM)

HEAD = 16


VMEM = pl.BlockSpec(memory_space=pltpu.VMEM)


def params(mib=56):
    return pltpu.CompilerParams(vmem_limit_bytes=mib * 1024 * 1024)


def whole(a):
    return pl.BlockSpec(a.shape, lambda i: (0,) * len(a.shape))


def pad8(n):
    return (n + 7) // 8 * 8


def layout(blocks):
    count = CAP * blocks
    rem = count % 8
    full = count - rem
    return full, rem, full + rem if 2 * rem <= 8 else full + 8


def slot_rows(blocks):
    return pad8(CAP * blocks)


def send_rows(blocks):
    full, rem, cot = layout(blocks)
    return 2 * full + (8 if cot < full + 8 else 16)


def cost(micros):
    return pl.CostEstimate(flops=int(micros * 1e9), bytes_accessed=int(micros * 3e6), transcendentals=0)


def pick(blocks, pos_ref, data, meta, outs):
    width = 2 * TOK * blocks
    lane = lax.broadcasted_iota(jnp.int32, (1, width), 1)
    block = lane >> 7
    is_cot = (lane >> 6) & 1
    code = meta[0:TOP] * CAP + meta[TOP : 2 * TOP] + (1024 * is_cot + 2048 * block).astype(F32)
    value = meta[2 * TOP : 3 * TOP]
    rows, count = send_rows(blocks), CAP * blocks
    full, rem, cot = layout(blocks)
    row = lax.broadcasted_iota(jnp.int32, (rows, 1), 0)
    row_cot = (row >= cot).astype(jnp.int32)
    if cot < full + 8:
        item = jnp.where(row >= full + 8, row - full - 8, row - rem * row_cot)
        used = (row < full + 2 * rem) | (row >= full + 8)
    else:
        item = row - cot * row_cot
        used = item < count
    first = item < full
    row_block = jnp.where(first, item >> 4, (item - full) >> 1)
    slot = jnp.where(first, item & (HEAD - 1), HEAD + ((item - full) & 1))
    picks = []
    for step in range(NX):
        to = (pos_ref[0] + step) & (NX - 1) if len(outs) == NX else step
        row_code = (to * NZ + pos_ref[1]) * CAP + slot + 1024 * row_cot + 2048 * row_block
        row_code = jnp.where(used, row_code, -1).astype(F32)
        chosen = jnp.zeros((rows, width), F32)
        for k in range(TOP):
            chosen = chosen + jnp.where(code[k : k + 1] == row_code, value[k : k + 1], 0.0)
        picks.append(chosen)
    if len(outs) == NX:
        for chosen, out in zip(picks, outs):
            out[...] = jnp.dot(chosen.astype(BF), data, preferred_element_type=F32).astype(BF)
    else:
        chosen = jnp.concatenate(picks, axis=0).astype(BF)
        outs[0][...] = jnp.dot(chosen, data, preferred_element_type=F32).astype(BF)


def pack_kernel(len_ref, tok_ref, cot_ref, routes_ref, slots_ref, gate_ref, out_ref):
    position = lax.broadcasted_iota(jnp.int32, (1, TOK), 1)
    end = jnp.int32(0)
    picked = jnp.zeros((1, TOK), F32)
    for seg in range(SEGS):
        length = len_ref[0, seg]
        inside = (position >= end) & (position < end + length)
        picked = jnp.where(inside, length.astype(F32), picked)
        end = end + length
    weight = (TOK / SEGS) / picked
    scale = (weight * gate_ref[...]).astype(BF).astype(F32)
    routes = routes_ref[...].astype(F32)
    slots = slots_ref[...].astype(F32)
    ones = jnp.ones((TOP, TOK), F32)
    fill = jnp.zeros((META - 3 * TOP, TOK), F32)
    out_ref[0:TOK, 0:D] = tok_ref[...]
    out_ref[TOK : 2 * TOK, 0:D] = cot_ref[...]
    out_ref[0:TOK, D : D + META] = jnp.concatenate([routes, slots, ones, fill], axis=0).T.astype(BF)
    out_ref[TOK : 2 * TOK, D : D + META] = jnp.concatenate([routes, slots, scale, fill], axis=0).T.astype(BF)


def pack(tokens, cotangent, routes, slots, gates, lengths):
    return pl.pallas_call(
        pack_kernel,
        out_shape=jax.ShapeDtypeStruct((2 * TOK, D + META), BF),
        grid=(1,),
        in_specs=[SMEM] + [whole(a) for a in (tokens, cotangent, routes, slots, gates)],
        out_specs=pl.BlockSpec((2 * TOK, D + META), lambda i: (0, 0)),
        compiler_params=params(),
        cost_estimate=cost(1),
        name="pack",
    )(lengths, tokens, cotangent, routes, slots, gates)


def select_kernel(blocks, count, pos_ref, *refs):
    inputs, outs = refs[:count], refs[count:]
    data = jnp.concatenate([r[:, 0:D] for r in inputs], axis=0)
    if count > blocks:
        metas = [jnp.concatenate([r[:, D:] for r in inputs], axis=0)]
    else:
        metas = [r[:, D:] for r in inputs]
    meta = jnp.concatenate([m.astype(F32).T for m in metas], axis=1)
    pick(blocks, pos_ref, data, meta, outs)


def select(position, inputs, blocks, apart):
    rows = send_rows(blocks) * (1 if apart else NX)
    outs = pl.pallas_call(
        functools.partial(select_kernel, blocks, len(inputs)),
        out_shape=[jax.ShapeDtypeStruct((rows, D), BF)] * (NX if apart else 1),
        grid=(1,),
        in_specs=[SMEM] + [VMEM] * len(inputs),
        out_specs=[pl.BlockSpec((rows, D), lambda i: (0, 0))] * (NX if apart else 1),
        compiler_params=params(16),
        cost_estimate=cost(40),
        name="select",
    )(position, *inputs)
    return outs if apart else outs[0]


def chunk_bases(blocks_of):
    bases, base = [], 0
    for blocks in blocks_of:
        bases.append(base)
        base += NX * slot_rows(blocks)
    return bases, base


TILE = 384


def gather_rows(blocks_of, arrays, copies, tok, cot):
    bases, _ = chunk_bases(blocks_of)
    for index, blocks in enumerate(blocks_of):
        for copy in copies[index]:
            copy.wait()
        full, rem, cot_at = layout(blocks)
        sent = send_rows(blocks)
        sub = lax.broadcasted_iota(jnp.int32, (8, 1), 0)
        heads, lates = ([], []), ([], [])
        for step in range(NX):
            if len(arrays[index]) == NX:
                rows = arrays[index][step][...].astype(F32)
            else:
                if step == 0:
                    everything = arrays[index][0][...].astype(F32)
                rows = everything[step * sent : (step + 1) * sent]
            heads[0].append(rows[0:full])
            heads[1].append(rows[sent - full :] if cot_at < full + 8 else rows[cot_at : cot_at + full])
            if cot_at < full + 8:
                mixed = rows[full : full + 8]
                lates[0].append(jnp.where(sub < rem, mixed, 0.0))
                lates[1].append(jnp.where(sub < rem, pltpu.roll(mixed, 8 - rem, 0), 0.0))
            else:
                lates[0].append(rows[full:cot_at])
                lates[1].append(rows[cot_at + full :])
        at = pl.ds(bases[index], NX * slot_rows(blocks))
        tok[at, :] = jnp.concatenate(heads[0] + lates[0], axis=0).astype(BF)
        cot[at, :] = jnp.concatenate(heads[1] + lates[1], axis=0).astype(BF)


def return_places(members, apart, pos_ref):
    bases, _ = chunk_bases([len(m) for m in members])
    places = []
    for base, distances, is_apart in zip(bases, members, apart):
        for step in range(NX):
            to_x = (pos_ref[0] - step) & (NX - 1) if is_apart else step
            for i, distance in enumerate(distances):
                to_z = (pos_ref[1] + distance) & (NZ - 1)
                source = base + (step * len(distances) + i) * HEAD
                places.append((source, pl.multiple_of((to_x * NZ + to_z) * HEAD, HEAD)))
    return places


def late_fold(members, apart, pos_ref):
    main = NX * NZ * HEAD
    row = lax.broadcasted_iota(jnp.int32, (main, 1), 0)
    device, within = row >> 4, row & (HEAD - 1)
    place_x = device >> 3
    away_x = (pos_ref[0] - place_x) & (NX - 1)
    away = ((device & (NZ - 1)) - pos_ref[1]) & (NZ - 1)
    late = jnp.zeros_like(row)
    for c, (distances, is_apart) in enumerate(zip(members, apart)):
        for i, distance in enumerate(distances):
            at = (c * NX + (away_x if is_apart else place_x)) * 8 + 2 * i + (within >> 3)
            late = jnp.where(away == distance % NZ, at, late)
    count = len(members) * NX * 8
    col = lax.broadcasted_iota(jnp.int32, (1, 8 * count), 1)
    return (col == (within & 7) * count + late).astype(F32).astype(BF)


def expert_kernel(members, apart, earlier, earlier_apart, pos_ref, *refs):
    blocks_of = [len(m) for m in members]
    sizes = [NX if a else 1 for a in apart]
    count = sum(sizes)
    arrays, (gate_up_in, down_in) = refs[:count], refs[count : count + 2]
    rest = refs[count + 2 + (1 if earlier else 0) :]
    outs, rest = rest[:5], rest[5:]
    (gate_up, down), rest = rest[:2], rest[2:]
    held, rest = rest[:count], rest[count:]
    tok, cot, grad, act, own_back, row_sems, in_sems, out_sems = rest[:8]
    copies = [pltpu.make_async_copy(a, h, row_sems.at[i]) for i, (a, h) in enumerate(zip(arrays, held))]
    for copy in copies:
        copy.start()
    starts = [sum(sizes[:i]) for i in range(len(sizes))]
    held = [held[i : i + n] for i, n in zip(starts, sizes)]
    copies = [copies[i : i + n] for i, n in zip(starts, sizes)]
    loads = []
    for index, f in enumerate(range(0, FF, TILE)):
        loads.append([
            pltpu.make_async_copy(
                gate_up_in.at[:, pl.ds(f, TILE)], gate_up.at[:, pl.ds(f, TILE)], in_sems.at[3 * index]
            ),
            pltpu.make_async_copy(
                gate_up_in.at[:, pl.ds(FF + f, TILE)], gate_up.at[:, pl.ds(FF + f, TILE)], in_sems.at[3 * index + 1]
            ),
            pltpu.make_async_copy(
                down_in.at[pl.ds(f, TILE), :], down.at[pl.ds(f, TILE), :], in_sems.at[3 * index + 2]
            ),
        ])
    for group in loads:
        for copy in group:
            copy.start()
    stores = [pltpu.make_async_copy(v, o, out_sems.at[i]) for i, (v, o) in enumerate(zip((tok, cot, grad, act), outs))]
    if earlier:
        back_ref, earlier_back, earlier_sem = rest[8:]
        earlier_copy = pltpu.make_async_copy(refs[count + 2], earlier_back, earlier_sem.at[0])
        earlier_copy.start()
    gather_rows(blocks_of, held, copies, tok, cot)
    stores[0].start()
    stores[1].start()
    for index, f in enumerate(range(0, FF, TILE)):
        for copy in loads[index]:
            copy.wait()
        gate_pre = jnp.dot(tok[...], gate_up[:, f : f + TILE], preferred_element_type=F32)
        up_pre = jnp.dot(tok[...], gate_up[:, FF + f : FF + f + TILE], preferred_element_type=F32)
        back = lax.dot_general(
            cot[...], down[f : f + TILE, :], (((1,), (1,)), ((), ())), preferred_element_type=F32
        )
        sigmoid = jax.nn.sigmoid(gate_pre)
        silu = gate_pre * sigmoid
        act[:, f : f + TILE] = (silu * up_pre).astype(BF)
        gate_grad = back * up_pre * sigmoid * (1.0 + gate_pre * (1.0 - sigmoid))
        grad[:, f : f + TILE] = gate_grad.astype(BF)
        grad[:, FF + f : FF + f + TILE] = (back * silu).astype(BF)
    stores[2].start()
    stores[3].start()

    tile = 512
    for d in range(0, D, tile):
        own_back[:, d : d + tile] = lax.dot_general(
            grad[...], gate_up[d : d + tile, :], (((1,), (1,)), ((), ())), preferred_element_type=F32
        ).astype(BF)
    if not earlier:
        stores.append(pltpu.make_async_copy(own_back, outs[4], out_sems.at[4]))
        stores[-1].start()
    else:
        earlier_copy.wait()
        lates = []
        for rows, own_members, own_apart in ((earlier_back, earlier, earlier_apart), (own_back, members, apart)):
            for source, to in return_places(own_members, own_apart, pos_ref):
                back_ref[pl.ds(to, HEAD), 0:D] = rows[source : source + HEAD, :]
            for base, distances in zip(chunk_bases([len(m) for m in own_members])[0], own_members):
                at = base + NX * len(distances) * HEAD
                lates.append(rows[at : at + NX * 8, :])
        stores.append(pltpu.make_async_copy(back_ref.at[:, pl.ds(0, D)], outs[4].at[:, pl.ds(0, D)], out_sems.at[4]))
        stores[-1].start()
        lates = jnp.concatenate(lates, axis=0)
        width = D * (CAP - HEAD) // HEAD
        stacked = jnp.concatenate([lates[:, c : c + width] for c in range(0, D, width)], axis=0)
        fold = late_fold(earlier + members, earlier_apart + apart, pos_ref)
        back_ref[:, D:] = jnp.dot(fold, stacked, preferred_element_type=F32).astype(BF)
        stores.append(
            pltpu.make_async_copy(back_ref.at[:, pl.ds(D, width)], outs[4].at[:, pl.ds(D, width)], out_sems.at[5])
        )
        stores[-1].start()
    for store in stores:
        store.wait()


def expert(position, arrays, gate_up, down, members, apart, earlier=(), earlier_apart=(), earlier_back=None):
    _, total = chunk_bases([len(m) for m in members])
    back = (NX * NZ * HEAD, D + D * (CAP - HEAD) // HEAD) if earlier else (total, D)
    shapes = [(total, D), (total, D), (total, GU), (total, FF), back]
    any_spec = pl.BlockSpec(memory_space=pl.ANY)
    operands = [*arrays, gate_up, down] + ([earlier_back] if earlier else [])
    buffers = [(D, GU), (FF, D)] + [a.shape for a in arrays] + shapes[:4] + [(total, D)]
    scratch = [pltpu.VMEM(s, BF) for s in buffers]
    scratch += [pltpu.SemaphoreType.DMA((n,)) for n in (len(arrays), 3 * (FF // TILE), 6)]
    if earlier:
        scratch += [pltpu.VMEM(back, BF), pltpu.VMEM(earlier_back.shape, BF), pltpu.SemaphoreType.DMA((1,))]
    outs = pl.pallas_call(
        functools.partial(expert_kernel, members, apart, earlier, earlier_apart),
        out_shape=[jax.ShapeDtypeStruct(s, BF) for s in shapes],
        grid=(1,),
        in_specs=[SMEM] + [any_spec] * len(operands),
        out_specs=[any_spec] * len(shapes),
        scratch_shapes=scratch,
        compiler_params=params(),
        cost_estimate=cost(1 if earlier else 5),
        name="expert",
    )(position, *operands)
    return outs[:4], outs[4]


def combine_kernel(routes_ref, slots_ref, rows_ref, out_ref):
    code = (routes_ref[...].astype(F32) * CAP + slots_ref[...].astype(F32)).T
    main = NX * NZ * HEAD
    col = lax.broadcasted_iota(jnp.int32, (1, main), 1)
    device, within = col >> 4, col & (HEAD - 1)
    head_code = (device * CAP + within).astype(F32)
    late_code = (device * CAP + HEAD + (within >> 3)).astype(F32)
    head = jnp.zeros((TOK, main), F32)
    late = jnp.zeros((TOK, main), F32)
    for k in range(TOP):
        head = head + (code[:, k : k + 1] == head_code).astype(F32)
        late = late + (code[:, k : k + 1] == late_code).astype(F32)
    folds = HEAD // (CAP - HEAD)
    lates = jnp.concatenate([jnp.where((within & 7) == j, late, 0.0) for j in range(folds)], axis=0)
    tail = jnp.dot(lates.astype(BF), rows_ref[:, D:], preferred_element_type=F32)
    total = jnp.dot(head.astype(BF), rows_ref[:, 0:D], preferred_element_type=F32)
    width = D // folds
    for j in range(folds):
        at = slice(j * width, (j + 1) * width)
        out_ref[:, at] = (total[:, at] + tail[j * TOK : (j + 1) * TOK]).astype(BF)


def combine(routes, slots, rows):
    return pl.pallas_call(
        combine_kernel,
        out_shape=jax.ShapeDtypeStruct((TOK, D), BF),
        grid=(1,),
        in_specs=[whole(routes), whole(slots), VMEM],
        out_specs=pl.BlockSpec((TOK, D), lambda i: (0, 0)),
        compiler_params=params(16),
        cost_estimate=cost(20),
        name="combine",
    )(routes, slots, rows)


def weight_kernel(groups, count, halves, which_ref, *refs):
    rest = refs[4 * groups :]
    extra, outs = (rest[:1], rest[1:]) if len(rest) > (2 * count if halves else 1) else ((), rest)
    first = (((0,), (0,)), ((), ()))
    rows = BLK_D // 2
    for cols, left, right in ((slice(0, GU), 0, 2), (slice(GU, GU + FF), 1, 3)):
        total = extra[0][:, cols].astype(F32) if extra else None
        for g in range(groups):
            part = lax.dot_general(
                refs[4 * g + left][...], refs[4 * g + right][...], first, preferred_element_type=F32
            )
            total = part if total is None else total + part
        total = total.astype(BF)
        if not halves:
            outs[0][:, cols] = total
            continue
        for i in range(count):

            @pl.when(pl.program_id(0) == i)
            def _():
                outs[2 * i][:, cols] = total[0:rows]
                outs[2 * i + 1][:, cols] = total[rows:]


def weight_blocks(which, groups, received=None, block=0, halves=False):
    count = which.shape[0]

    def cut(a):
        return pl.BlockSpec((a.shape[0], BLK_D), lambda i, w: (0, w[i]))

    def full(a):
        return pl.BlockSpec(a.shape, lambda i, w: (0, 0))

    specs = [spec for g in groups for spec in (cut(g[0]), cut(g[1]), full(g[2]), full(g[3]))]
    extra = []
    if received is not None:
        specs.append(pl.BlockSpec((BLK_D, GU + FF), lambda i, w: (block + i, 0)))
        extra.append(received)
    if halves:
        shapes = [(BLK_D // 2, GU + FF)] * (2 * count)
        out_specs = [pl.BlockSpec(shapes[0], lambda i, w: (0, 0))] * (2 * count)
    else:
        shapes = [(count * BLK_D, GU + FF)]
        out_specs = [pl.BlockSpec((BLK_D, GU + FF), lambda i, w: (i, 0))]
    return pl.pallas_call(
        functools.partial(weight_kernel, len(groups), count, halves),
        out_shape=[jax.ShapeDtypeStruct(s, BF) for s in shapes],
        grid_spec=pltpu.PrefetchScalarGridSpec(
            num_scalar_prefetch=1, grid=(count,), in_specs=specs, out_specs=out_specs
        ),
        compiler_params=params(),
        cost_estimate=cost(3 if count == 3 else 1),
        name="weight_blocks",
    )(which, *(a for g in groups for a in g), *extra)


def finish_kernel(own_top, own_bottom, plus_top, plus_bottom, minus_top, minus_bottom, gate_up, down):
    hop = BLK_D // 2
    tops, bottoms = (own_top, plus_top, minus_top), (own_bottom, plus_bottom, minus_bottom)
    for at, (own, plus, minus) in ((slice(0, hop), tops), (slice(hop, BLK_D), bottoms)):
        total = own[...].astype(F32) + plus[...].astype(F32) + minus[...].astype(F32)
        gate_up[at, :] = total[:, 0:GU].astype(BF)
        down[:, at] = total[:, GU:].T.astype(BF)


def finish(*parts):
    return pl.pallas_call(
        finish_kernel,
        out_shape=[jax.ShapeDtypeStruct((BLK_D, GU), BF), jax.ShapeDtypeStruct((FF, BLK_D), BF)],
        grid=(1,),
        in_specs=[whole(a) for a in parts[:2]] + [VMEM] * 4,
        out_specs=[pl.BlockSpec((BLK_D, GU), lambda i: (0, 0)), pl.BlockSpec((FF, BLK_D), lambda i: (0, 0))],
        compiler_params=params(16),
        cost_estimate=cost(1),
        name="finish",
    )(*parts)


def shift(array, axis, size, by):
    return lax.ppermute(array, axis, [(i, (i + by) % size) for i in range(size)])


def per_device(tokens, cotangent, routes, slot_index, gate_probs, lengths, w_gate_up, w_down):
    x, z = lax.axis_index("x"), lax.axis_index("z")
    y, core = lax.axis_index("y"), lax.axis_index("core")
    position = jnp.stack([x, z]).astype(jnp.int32)
    gate_up, down = w_gate_up[0], w_down[0]
    routes, slots, gates = routes.T, slot_index.T, gate_probs.T

    own = pack(tokens, cotangent, routes, slots, gates, lengths)

    def exchange(rows):
        return [lax.all_to_all(rows, "x", split_axis=0, concat_axis=0, tiled=True)]

    def exchange_apart(rows):
        return [rows[0]] + [shift(rows[s], "x", NX, s) for s in range(1, NX)]

    half = NZ // 2
    up1, dn1 = shift(own, "z", NZ, 1), shift(own, "z", NZ, -1)
    sent_near = select(position, (own, up1, dn1), 3, True)
    near = exchange_apart(sent_near)
    up2, dn2 = shift(up1, "z", NZ, 1), shift(dn1, "z", NZ, -1)
    up2, dn2, sent_near = lax.optimization_barrier((up2, dn2, sent_near))
    up3, dn3 = shift(up2, "z", NZ, 1), shift(dn2, "z", NZ, -1)
    middle = exchange(select(position, (up2, dn2), 2, False))
    far_tok, far_cot = shift(up3[0:TOK], "z", NZ, 1), shift(dn3[TOK:], "z", NZ, -1)
    third = exchange_apart(select(position, (up3, dn3), 2, True))
    far_tok, far_cot, near, middle = lax.optimization_barrier((far_tok, far_cot, near, middle))
    last = exchange_apart(select(position, (far_tok, far_cot), 1, True))

    members_a, apart_a = ((0, -1, 1), (-2, 2)), (True, False)
    members_b, apart_b = ((-3, 3), (half,)), (True, True)
    group_a, back_a = expert(position, near + middle, gate_up, down, members_a, apart_a)
    group_b, sent_back = expert(
        position, third + last, gate_up, down, members_b, apart_b, members_a, apart_a, back_a
    )
    group = (group_a, group_b)
    width = sent_back.shape[1]
    got_back = lax.all_to_all(
        sent_back.reshape(NX * NZ, HEAD, width), ("x", "z"), split_axis=0, concat_axis=0, tiled=True
    )

    def blocks_at(steps, of_core):
        return jnp.stack([2 * ((y + s) % NY) + of_core for s in steps]).astype(jnp.int32)

    def add(a, b):
        return (a.astype(F32) + b.astype(F32)).astype(BF)

    received = shift(weight_blocks(blocks_at((2, 1, 3, 0), 1 - core), group)[0], "core", 2, 1)
    top, bottom = weight_blocks(blocks_at((2,), core), group, received, 0, halves=True)
    top, bottom, nearer = lax.optimization_barrier((top, bottom, blocks_at((1, 3, 0), core)))
    top, bottom = shift(top, "y", NY, 1), shift(bottom, "y", NY, -1)
    plus_top, plus_bottom, minus_top, minus_bottom, own_top, own_bottom = weight_blocks(
        nearer, group, received, 1, halves=True
    )
    plus_bottom = shift(plus_bottom, "y", NY, 1)
    minus_top = shift(minus_top, "y", NY, -1)
    top, bottom = lax.optimization_barrier((top, bottom))
    plus_top, minus_bottom = add(plus_top, top), add(minus_bottom, bottom)
    plus_top, minus_bottom = lax.optimization_barrier((plus_top, minus_bottom))
    got_back = lax.optimization_barrier((got_back, plus_top, minus_bottom))[0]
    plus_top = shift(plus_top, "y", NY, 1)
    minus_bottom = shift(minus_bottom, "y", NY, -1)
    token_grad = combine(routes, slots, got_back.reshape(NX * NZ * HEAD, width))
    grad_gate_up, grad_down = finish(own_top, own_bottom, plus_top, plus_bottom, minus_top, minus_bottom)
    return token_grad, grad_gate_up[None], grad_down[None]


def solution(mesh):
    torus = Mesh(mesh.devices.reshape(NY, 2, NX, NZ), ("y", "core", "x", "z"))
    dp, ep = ("y", "core"), ("x", "z")
    return jax.shard_map(
        per_device,
        mesh=torus,
        in_specs=(P(dp + ep, None),) * 6 + (P(ep, None, None),) * 2,
        out_specs=(P(dp + ep, None), P(ep, dp, None), P(ep, None, dp)),
        check_vma=False,
    )
```
